32 devices in a mesh: section: 2 (over y), fsdp: 16 (over z, x, core).
Axes of the slice: x: 2, y: 2, z: 4, core: 2. Of those that a mesh axis runs over, the one named last changes fastest.
Arguments:
- tokens: bfloat16 [2, 1536, 1024], P(None, 'fsdp'), may hold values from -6 to 6
- cotangent: bfloat16 [2, 1536, 1024], P(None, 'fsdp'), may hold values from -6 to 6
- routes: int32 [2, 2, 1536, 8], P('section', None, 'fsdp'), may hold values from 0 to 31, all different within a row; in each aligned block of 96 rows (0 to 95, 96 to 191, ..., all dimensions but the last counted through in order) at most 28 rows name the same one
- picture_start: int32 [2, 16], P(None, 'fsdp'), may hold values from 0 to 32
- w_qkv: bfloat16 [2, 1024, 2048], P('section', 'fsdp'), may hold values from -0.1875 to 0.1875
- w_out: bfloat16 [2, 1024, 1024], P('section', 'fsdp'), may hold values from -1 to 1
- w_router: bfloat16 [2, 1024, 32], P('section', 'fsdp'), may hold values from -0.09375 to 0.09375
- gain_attn: bfloat16 [2, 1024], P('section', 'fsdp'), may hold values from 0.099609375 to 1.8984375
- gain_moe: bfloat16 [2, 1024], P('section', 'fsdp'), may hold values from 0.099609375 to 1.8984375
- w_gate_up: bfloat16 [2, 16384, 2048], P('section', 'fsdp'), may hold values from -0.1875 to 0.1875
- w_down: bfloat16 [2, 16384, 1024], P('section', 'fsdp'), may hold values from -0.75 to 0.75
Outputs:
- section_out: bfloat16 [2, 2, 1536, 1024], P('section', None, 'fsdp')
- section_grad: bfloat16 [2, 2, 1536, 1024], P('section', None, 'fsdp')
- grad_qkv: float32 [2, 1024, 2048], P('section', 'fsdp')
- grad_out: float32 [2, 1024, 1024], P('section', 'fsdp')
- grad_router: float32 [2, 1024, 32], P('section', 'fsdp')
- grad_gain_attn: float32 [2, 1024], P('section', 'fsdp')
- grad_gain_moe: float32 [2, 1024], P('section', 'fsdp')
- grad_gate_up: float32 [2, 16384, 2048], P('section', 'fsdp')
- grad_down: float32 [2, 16384, 1024], P('section', 'fsdp')
The draws below stay inside these ranges and needn't reach their ends.
Inputs may be any that keep to these rules, and one draw needn't show every extreme that they name: `routes`: each token names 8 different experts. In each layer and micro-batch no expert is named by more than 28 tokens of one sequence, and in some sequence one expert is named by exactly 28.
All inputs are finite; a program needn't handle non-finite values.
Results may differ from the reference program's by a relative error of at most 0.034.
Values may be sent and summed in bfloat16 or wider, within the bound.
No kernel may reach another device: no remote copies, remote signals or barrier semaphores. Data moves between devices by JAX's collectives and lax.ppermute only.
A program may use at most 256 MiB of HBM per device.

```python
import math
import jax
import jax.numpy as jnp
import numpy as np
from jax import lax

D = 1024
QUERY_HEADS = 16
KEY_VALUE_HEADS = 8
HEAD_SIZE = 64
EXPERTS = 32
HID = 512
TOP = 8
SEQUENCE_LENGTH = 96
PIC = 64
MB = 2
CAP = 28
QKV = 2048
SEQS = 16
TOKENS = 1536
N_SECTION = 2


def place_ends(values, own_key, smallest, largest):
    longest = values.shape.index(max(values.shape))
    spots = []
    for shift in (0, 1):
        where = [jax.random.randint(jax.random.fold_in(own_key, axis), (), 0, length) for axis, length in enumerate(values.shape)]
        where[longest] = (where[longest] + shift) % values.shape[longest]
        spots.append(tuple(where))
    return values.at[spots[0]].set(smallest).at[spots[1]].set(largest)


def shard_levels(key, extent, split, smallest, largest):
    def one(position, parts):
        steps = jax.random.uniform(jax.random.fold_in(jax.random.fold_in(key, 6), position), (parts,), jnp.float32, smallest / len(split), largest / len(split))
        return jnp.repeat(jnp.exp(steps), extent[position] // parts).reshape((-1,) + (1,) * (len(extent) - position - 1))

    gain = one(*split[0])
    for cut in split[1:]:
        gain = gain * one(*cut)
    return gain


def shared_out(stream_key, own, number, rows, number_of, top, reach, slope):
    ranking = jax.random.permutation(stream_key, number_of)
    crowded, common = shares(number_of, rows * top, reach, slope, True), shares(number_of, rows * top, reach, slope, False)
    places = jnp.arange(number_of)

    def named(lengths, rotation):
        used = int((lengths > 0).sum())
        fixed = max(1, used // 4)
        moved = fixed + (places - fixed + rotation * (used - fixed)) % max(1, number_of - fixed)
        return jnp.zeros((number_of,), jnp.int32).at[ranking[jnp.where(places < fixed, places, moved)]].set(jnp.asarray(lengths, jnp.int32))

    lengths = jnp.where(number % 4 == 0, named(crowded, number // 4), named(common, number - number // 4 - 1))
    mixed = jax.random.permutation(jax.random.fold_in(own, 3), number_of)
    source_of, taker = mixed[0:number_of // 2 * 2:2], mixed[1:number_of // 2 * 2:2]
    slack = jnp.minimum(lengths[source_of] - 1, reach - lengths[taker]) // 2
    slack = jnp.where((source_of == ranking[0]) | (taker == ranking[0]) | (lengths[taker] == 0), 0, jnp.maximum(slack, 0))
    moved = jax.random.randint(jax.random.fold_in(own, 4), (number_of // 2,), 0, 1 << 20) % (slack + 1)
    lengths = lengths.at[source_of].add(-moved).at[taker].add(moved)
    members = jnp.searchsorted(jnp.cumsum(lengths), jnp.arange(rows * top), side="right").astype(jnp.int32)
    listing = members.reshape(top, rows).T
    listing = listing[jax.random.permutation(jax.random.fold_in(own, 1), rows)]
    rotation = jax.random.randint(jax.random.fold_in(own, 2), (rows, 1), 0, top)
    return jnp.take_along_axis(listing, (jnp.arange(top)[None, :] + rotation) % top, axis=1)


def shares(amount, total, reach, skew, full):
    loads = [(1 << 20) // math.isqrt(standing ** skew) + 1 for standing in range(1, amount + 1)]
    largest = reach if full else min(reach, max(-(-total // amount), total * loads[0] // sum(loads)))
    least = 1 if total - largest >= amount - 1 else 0
    given, surplus = [largest] + [least] * (amount - 1), total - largest - least * (amount - 1)
    while surplus > 0:
        candidates = [i for i in range(1, amount) if given[i] < largest] or [i for i in range(1, amount) if given[i] < reach]
        whole, budget = sum([loads[i] for i in candidates]), surplus
        for i in candidates:
            more = min(reach - given[i], max(1, budget * loads[i] // whole), surplus)
            given[i] = given[i] + more
            surplus = surplus - more
    return np.array(given)


def noise(key, dims, spread, limit, cuts=(), kind=jnp.bfloat16):
    loudness = shard_levels(key, dims, cuts, -0.22, 0.18) if cuts else 1.0
    array = jax.random.normal(key, dims, jnp.float32) * spread * loudness
    return jnp.minimum(jnp.maximum(array, -limit), limit).astype(kind)


def setup_inputs(seed: int = 0) -> dict:
    seeds = jax.random.split(jax.random.key(seed), 12)
    tokens = noise(seeds[0], (MB, TOKENS, D), 1.0, 6.0, ((1, 16),))
    cotangent = noise(seeds[1], (MB, TOKENS, D), 1.0, 6.0, ((1, 16),))
    routes_keys = jax.random.split(jax.random.fold_in(seeds[2], 1), N_SECTION * MB * TOKENS // SEQUENCE_LENGTH)
    routes_turns = jax.random.permutation(jax.random.fold_in(seeds[2], 3), N_SECTION * MB * TOKENS // SEQUENCE_LENGTH)
    routes = jax.vmap(lambda own, number: shared_out(jax.random.fold_in(seeds[2], 2), own, number, SEQUENCE_LENGTH, EXPERTS, TOP, CAP, 1))(routes_keys, routes_turns).reshape((N_SECTION, MB, TOKENS, TOP))
    picture_start = place_ends(jax.random.randint(seeds[3], (MB, SEQS), 0, SEQUENCE_LENGTH - PIC + 1), jax.random.fold_in(seeds[3], 1), 0, SEQUENCE_LENGTH - PIC).astype(jnp.int32)
    w_qkv = noise(seeds[4], (N_SECTION, D, QKV), D ** -0.5, 0.1875, ((0, 2), (1, 16)))
    w_out = noise(seeds[5], (N_SECTION, QUERY_HEADS * HEAD_SIZE, D), (QUERY_HEADS * HEAD_SIZE // 32) ** -0.5, 1.0, ((0, 2), (1, 16)))
    w_router = noise(seeds[6], (N_SECTION, D, EXPERTS), (4 * D) ** -0.5, 0.09375, ((0, 2), (1, 16)))
    gain_attn = jnp.clip(1.0 + 0.18 * jax.random.normal(seeds[7], (N_SECTION, D), jnp.float32), 0.099609375, 1.8984375).astype(jnp.bfloat16)
    gain_moe = jnp.clip(1.0 + 0.18 * jax.random.normal(seeds[8], (N_SECTION, D), jnp.float32), 0.099609375, 1.8984375).astype(jnp.bfloat16)
    w_gate_up = noise(seeds[9], (N_SECTION, EXPERTS * HID, 2 * D), D ** -0.5, 0.1875, ((0, 2), (1, 16)))
    w_down = noise(seeds[10], (N_SECTION, EXPERTS * HID, D), (HID // 8) ** -0.5, 0.75, ((0, 2), (1, 16)))
    return {"tokens": tokens, "cotangent": cotangent, "routes": routes, "picture_start": picture_start, "w_qkv": w_qkv, "w_out": w_out, "w_router": w_router, "gain_attn": gain_attn, "gain_moe": gain_moe, "w_gate_up": w_gate_up, "w_down": w_down}


highest = lax.Precision.HIGHEST
epsilon = 1e-05

@jax.custom_vjp
def lower_bits(v):
    return lax.optimization_barrier(v.astype(jnp.bfloat16)).astype(jnp.float32)

@jax.custom_vjp
def low_back(v):
    return v

def low_keep(v):
    return (lower_bits(v), None)

def low_pass(kept, grad):
    return (grad,)

def back_keep(v):
    return (v, None)

def back_low(kept, grad):
    return (lower_bits(grad),)
lower_bits.defvjp(low_keep, low_pass)
low_back.defvjp(back_keep, back_low)

def norm_rows(values, gain_vec):
    return values * lax.rsqrt(lax.optimization_barrier(jnp.mean(values * values, axis=-1, keepdims=True)) + epsilon) * gain_vec

def apply_rotary(values):
    half_width = HEAD_SIZE // 2
    token_length = values.shape[0]
    frequency = 10000.0 ** (-2.0 * jnp.arange(half_width, dtype=jnp.float32) / HEAD_SIZE)
    angles = jnp.arange(token_length, dtype=jnp.float32)[:, None] * frequency[None, :]
    cosine = jnp.cos(angles)[:, None, :]
    sine_table = jnp.sin(angles)[:, None, :]
    first_half = values[..., :half_width]
    second_half = values[..., half_width:]
    return jnp.concatenate([first_half * cosine - second_half * sine_table, second_half * cosine + first_half * sine_table], axis=-1)

def visible(start_pos, token_length):
    row_pos = jnp.arange(token_length, dtype=jnp.int32)[:, None]
    col_pos = jnp.arange(token_length, dtype=jnp.int32)[None, :]
    row_inside = (row_pos >= start_pos) & (row_pos < start_pos + PIC)
    col_inside = (col_pos >= start_pos) & (col_pos < start_pos + PIC)
    return (col_pos <= row_pos) | row_inside & col_inside

def slot_table(route_rows):
    token_length = route_rows.shape[0]
    flat_routes = route_rows.reshape(-1).astype(jnp.int32)
    onehot = (flat_routes[:, None] == jnp.arange(EXPERTS, dtype=jnp.int32)[None, :]).astype(jnp.int32)
    before = (jnp.cumsum(onehot, axis=0) - onehot).astype(jnp.int32)
    place_index = lax.optimization_barrier(jnp.sum(before * onehot, axis=1)).astype(jnp.int32)
    slot_index = flat_routes * CAP + place_index
    slot_owner = jnp.full((EXPERTS * CAP,), token_length * TOP, jnp.int32).at[slot_index].set(jnp.arange(token_length * TOP, dtype=jnp.int32))
    return (slot_index.reshape(token_length, TOP), slot_owner)

def sequence_layer(layer_in, route_rows, start_pos, weights):
    w_qkv, w_out, w_router, gain_attn, gain_moe, w_gate_up, w_down = weights
    query_width = QUERY_HEADS * HEAD_SIZE
    key_width = KEY_VALUE_HEADS * HEAD_SIZE
    normed = lower_bits(norm_rows(layer_in, gain_attn))
    query_key_value = low_back(jnp.dot(normed, w_qkv, precision=highest))
    query_matrix_rows = lower_bits(apply_rotary(query_key_value[:, :query_width].reshape(SEQUENCE_LENGTH, QUERY_HEADS, HEAD_SIZE))).reshape(SEQUENCE_LENGTH, KEY_VALUE_HEADS, QUERY_HEADS // KEY_VALUE_HEADS, HEAD_SIZE)
    key_matrix_rows = lower_bits(apply_rotary(query_key_value[:, query_width:query_width + key_width].reshape(SEQUENCE_LENGTH, KEY_VALUE_HEADS, HEAD_SIZE)))
    value_matrix_rows = lower_bits(query_key_value[:, query_width + key_width:].reshape(SEQUENCE_LENGTH, KEY_VALUE_HEADS, HEAD_SIZE))
    scores = low_back(jnp.einsum('qngd,knd->ngqk', query_matrix_rows, key_matrix_rows, precision=highest) * HEAD_SIZE ** (-0.5))
    scores = jnp.where(visible(start_pos, SEQUENCE_LENGTH)[None, None], scores, -1e+30)
    exponent = jnp.exp(scores - lax.optimization_barrier(jnp.max(scores, axis=-1, keepdims=True)))
    probs_low = lower_bits(exponent / lax.optimization_barrier(jnp.sum(exponent, axis=-1, keepdims=True)))
    mixed_heads = low_back(lower_bits(jnp.einsum('ngqk,knd->qngd', probs_low, value_matrix_rows, precision=highest).reshape(SEQUENCE_LENGTH, query_width)))
    residual = layer_in + low_back(jnp.dot(mixed_heads, w_out, precision=highest))
    normed_moe = lower_bits(norm_rows(residual, gain_moe))
    logits = jnp.dot(normed_moe, w_router, precision=highest)
    gate_weights = jax.nn.softmax(jnp.take_along_axis(logits, route_rows, axis=1), axis=-1)
    slot_index, slot_owner = slot_table(route_rows)
    padded = jnp.concatenate([normed_moe, jnp.zeros((1, D), jnp.float32)], axis=0)
    sent_rows = padded[slot_owner // TOP].reshape(EXPERTS, CAP, D)
    gate_w = w_gate_up[:, :D].reshape(EXPERTS, HID, D)
    up_w = w_gate_up[:, D:].reshape(EXPERTS, HID, D)
    gate_val = low_back(jnp.einsum('ecd,ehd->ech', sent_rows, gate_w, precision=highest))
    up_val = low_back(jnp.einsum('ecd,ehd->ech', sent_rows, up_w, precision=highest))
    activation = lower_bits(jax.nn.silu(gate_val) * up_val)
    expert_out = low_back(lower_bits(jnp.einsum('ech,ehd->ecd', activation, w_down.reshape(EXPERTS, HID, D), precision=highest)))
    picked = expert_out.reshape(EXPERTS * CAP, D)[slot_index]
    return residual + lax.optimization_barrier(jnp.sum(gate_weights[:, :, None] * picked, axis=1))

def run_layer(layer_in, route_rows, starts, weights):

    def one_sequence(bundle):
        return sequence_layer(bundle[0], bundle[1], bundle[2], weights)
    result = lax.map(jax.checkpoint(one_sequence), (layer_in.reshape(SEQS, SEQUENCE_LENGTH, D), route_rows.reshape(SEQS, SEQUENCE_LENGTH, TOP), starts))
    return result.reshape(SEQS * SEQUENCE_LENGTH, D)

def reference(tokens, cotangent, routes, picture_start, w_qkv, w_out, w_router, gain_attn, gain_moe, w_gate_up, w_down):
    weights = tuple((array_item.astype(jnp.float32) for array_item in (w_qkv, w_out, w_router, gain_attn, gain_moe, w_gate_up, w_down)))
    inputs = tokens.astype(jnp.float32)
    probe_zero = jnp.zeros(inputs.shape, jnp.float32)

    def network(inputs, probe_zero, weights):
        lower = tuple((array_item[0] for array_item in weights))
        upper = tuple((array_item[1] for array_item in weights))
        first_out = []
        second_out = []
        for micro_index in range(MB):
            hidden = run_layer(inputs[micro_index], routes[0, micro_index], picture_start[micro_index], lower)
            passed = low_back(lower_bits(hidden)) + probe_zero[micro_index]
            first_out.append(hidden)
            second_out.append(run_layer(passed, routes[1, micro_index], picture_start[micro_index], upper))
        return (jnp.stack(first_out), jnp.stack(second_out))
    (first_out, second_out), pull_back = jax.vjp(network, inputs, probe_zero, weights)
    grad_inputs, grad_probe, grad_weights = pull_back((jnp.zeros_like(first_out), cotangent.astype(jnp.float32)))
    section_out = jnp.stack([first_out, second_out]).astype(jnp.bfloat16)
    section_grad = jnp.stack([grad_inputs, grad_probe]).astype(jnp.bfloat16)
    return (section_out, section_grad, grad_weights[0], grad_weights[1], grad_weights[2], grad_weights[3], grad_weights[4], grad_weights[5], grad_weights[6])
```

```python
import functools

import jax
import jax.numpy as jnp
import numpy as np
from jax import lax
from jax.experimental import pallas as pl
from jax.experimental.pallas import tpu as pltpu
from jax.sharding import PartitionSpec as P

D = 1024
QUERY_HEADS = 16
KEY_VALUE_HEADS = 8
HEAD_SIZE = 64
EXPERTS = 32
TOP = 8
PIC = 64
SLOTS = 32
LANES = 128
QKV = 2048
WIDE = D + LANES
WCOLS = QKV + D + LANES
epsilon = 1e-05
scale = HEAD_SIZE ** (-0.5)
f32 = jnp.float32
bf16 = jnp.bfloat16
VMEM_LIMIT = 56 * 1024 * 1024

PATH = (0, 2, 4, 6, 7, 5, 3, 1)
PLACE = tuple(PATH.index(c) for c in range(8))


def dot(a, b, ca, cb):
    return lax.dot_general(a, b, (((ca,), (cb,)), ((), ())), preferred_element_type=f32)


def nn(a, b):
    return dot(a, b, 1, 0)


def nt(a, b):
    return dot(a, b, 1, 1)


def tn(a, b):
    return dot(a, b, 0, 0)


def lanes_of(shape):
    return lax.broadcasted_iota(jnp.int32, shape, len(shape) - 1)


def rms(values):
    return lax.rsqrt(jnp.mean(values * values, axis=-1, keepdims=True) + epsilon)


def norm_back(values, inv, gain, grad):
    scaled = grad * gain
    inner = jnp.mean(scaled * values, axis=-1, keepdims=True)
    return inv * scaled - values * (inv * inv * inv * inner)


def turn(chunk, cosine, sine, back):
    first = (lanes_of(chunk.shape) & 63) < 32
    ahead = pltpu.roll(chunk, 96, 1)
    behind = pltpu.roll(chunk, 32, 1)
    if back:
        swapped = jnp.where(first, ahead, -behind)
    else:
        swapped = jnp.where(first, -ahead, behind)
    return chunk * cosine + swapped * sine


def halves(chunk):
    low = lanes_of(chunk.shape) < 64
    return jnp.concatenate([jnp.where(low, chunk, 0.0), jnp.where(low, 0.0, chunk)], axis=0)


def join(stacked):
    rows = stacked.shape[0] // 2
    low = lanes_of((rows, LANES)) < 64
    return jnp.where(low, stacked[:rows], stacked[rows:])


def doubled(chunk, odd):
    low = lanes_of(chunk.shape) < 64
    other = pltpu.roll(chunk, 64, 1)
    return jnp.where(low, other, chunk) if odd else jnp.where(low, chunk, other)


def load_weights(order, w_hbm, w_vmem, sems):
    copies = []
    for k in range(8):
        for b in range(2):
            copies.append(
                pltpu.make_async_copy(
                    w_hbm.at[k, b], w_vmem.at[order[0, k] * 2 + (order[1, 0] ^ b)], sems.at[k * 2 + b]
                )
            )
    for copy in copies:
        copy.start()
    return copies


def gains_of(w_vmem):
    pieces = ([], [])
    for c in range(8):
        even = w_vmem[2 * c, 0:16, QKV + D :].astype(f32)
        odd = w_vmem[2 * c + 1, 0:16, QKV + D :].astype(f32)
        even = pltpu.roll(even, 64, 1)
        both = jnp.where(lanes_of(even.shape) < 64, even, odd)
        for i in range(2):
            pieces[i].append(both[i : i + 1])
    return jnp.concatenate(pieces[0], axis=1), jnp.concatenate(pieces[1], axis=1)


def attn_forward_kernel(
    save, order, starts, x_ref, pos_ref, cos_ref, sin_ref, w_hbm, *rest
):
    if save:
        (out_ref, resid_ref, gate_ref, normed_ref, q_ref, k_ref, v_ref, probs_ref, mixed_ref) = rest[:9]
        w_vmem, sems = rest[9:]
    else:
        out_ref, resid_ref, w_vmem, sems, mixed_ref = rest
    copies = load_weights(order, w_hbm, w_vmem, sems)
    seqs, length = x_ref.shape[0], x_ref.shape[1]
    rows = seqs * length
    for copy in copies:
        copy.wait()
    gain_attn, gain_moe = gains_of(w_vmem)
    x = x_ref[...].reshape(rows, D).astype(f32)
    normed = (x * rms(x) * gain_attn).astype(bf16)
    w_qkv = w_vmem[:, :, :QKV].reshape(D, QKV)
    qkv = nn(normed, w_qkv)
    cosine, sine = cos_ref[...], sin_ref[...]
    row_pos = lax.broadcasted_iota(jnp.int32, (length, length), 0)
    col_pos = lax.broadcasted_iota(jnp.int32, (length, length), 1)
    for s in range(seqs):
        top = slice(s * length, (s + 1) * length)
        start = starts[s]
        both = (
            (row_pos >= start) & (row_pos < start + PIC) & (col_pos >= start) & (col_pos < start + PIC)
        )
        bias = jnp.where((col_pos <= row_pos) | both, 0.0, -1e30)
        bias = jnp.concatenate([bias, bias], axis=0)
        keys, values = [], []
        for c in range(4):
            key = turn(qkv[top, D + c * LANES : D + (c + 1) * LANES], cosine, sine, False)
            value = qkv[top, D + 512 + c * LANES : D + 512 + (c + 1) * LANES]
            keys.append(key)
            values.append(value)
            if save:
                k_ref[top, c * LANES : (c + 1) * LANES] = key.astype(bf16)
                v_ref[top, c * LANES : (c + 1) * LANES] = value.astype(bf16)
        for j in range(KEY_VALUE_HEADS):
            query = turn(qkv[top, j * LANES : (j + 1) * LANES], cosine, sine, False)
            if save:
                q_ref[top, j * LANES : (j + 1) * LANES] = query.astype(bf16)
            key = doubled(keys[j // 2], j % 2 == 1).astype(bf16)
            value = doubled(values[j // 2], j % 2 == 1).astype(bf16)
            scores = nt(halves(query).astype(bf16), key) * scale + bias
            exponent = jnp.exp(scores - jnp.max(scores, axis=-1, keepdims=True))
            probs = exponent / jnp.sum(exponent, axis=-1, keepdims=True)
            if save:
                probs_ref[s * KEY_VALUE_HEADS + j] = probs
            mixed = join(nn(probs.astype(bf16), value))
            mixed_ref[top, j * LANES : (j + 1) * LANES] = mixed.astype(bf16)
    w_out = w_vmem[:, :, QKV : QKV + D].reshape(D, D)
    resid = x + nn(mixed_ref[...], w_out)
    normed_moe = (resid * rms(resid) * gain_moe).astype(bf16)
    w_small = w_vmem[:, :, QKV + D :].reshape(D, LANES)
    logits = nn(normed_moe, w_small)
    pos = pos_ref[...]
    routed = pos < 64.0
    logits = jnp.where(routed, logits, -1e30)
    exponent = jnp.where(routed, jnp.exp(logits - jnp.max(logits, axis=-1, keepdims=True)), 0.0)
    gate = exponent / jnp.sum(exponent, axis=-1, keepdims=True)
    high = gate.astype(bf16).astype(f32)
    low = gate - high
    lane = lanes_of(gate.shape)
    columns = jnp.where(
        lane < 32,
        high,
        jnp.where(
            lane < 64,
            pltpu.roll(low, 32, 1),
            jnp.where(lane < 96, pltpu.roll(pos, 64, 1), 0.0),
        ),
    )
    out_ref[:, :, :D] = normed_moe.reshape(seqs, length, D)
    out_ref[:, :, D:] = columns.astype(bf16).reshape(seqs, length, LANES)
    resid_ref[...] = resid
    if save:
        gate_ref[...] = gate
        normed_ref[...] = normed


def vmem():
    return pl.BlockSpec(memory_space=pltpu.VMEM)


def smem():
    return pl.BlockSpec(memory_space=pltpu.SMEM)


def anywhere():
    return pl.BlockSpec(memory_space=pl.ANY)


def attn_forward(save, order, starts, x, pos, cosine, sine, w_all):
    seqs, length = x.shape[0], x.shape[1]
    rows = seqs * length
    shape = jax.ShapeDtypeStruct
    outs = [shape((seqs, length, WIDE), bf16), shape((rows, D), f32)]
    scratch = [pltpu.VMEM((16, 64, WCOLS), bf16), pltpu.SemaphoreType.DMA((16,))]
    if save:
        outs += [
            shape((rows, LANES), f32),
            shape((rows, D), bf16),
            shape((rows, D), bf16),
            shape((rows, 512), bf16),
            shape((rows, 512), bf16),
            shape((seqs * KEY_VALUE_HEADS, 2 * length, length), f32),
            shape((rows, D), bf16),
        ]
    else:
        scratch.append(pltpu.VMEM((rows, D), bf16))
    return pl.pallas_call(
        functools.partial(attn_forward_kernel, save),
        out_shape=outs,
        in_specs=[smem(), smem(), vmem(), vmem(), vmem(), vmem(), anywhere()],
        out_specs=[vmem()] * len(outs),
        scratch_shapes=scratch,
        compiler_params=pltpu.CompilerParams(vmem_limit_bytes=VMEM_LIMIT),
        cost_estimate=pl.CostEstimate(
            flops=2 * rows * D * 3400, bytes_accessed=12_000_000, transcendentals=rows * 2048
        ),
        name="attn_forward",
    )(order, starts, x, pos, cosine, sine, w_all)


def attn_backward_kernel(
    with_grads,
    order,
    sum_ref,
    g_ref,
    x_ref,
    wide_ref,
    resid_ref,
    gate_ref,
    normed_ref,
    q_ref,
    k_ref,
    v_ref,
    probs_ref,
    mixed_ref,
    cos_ref,
    sin_ref,
    w_hbm,
    *rest,
):
    if with_grads:
        grad_ref, big_ref, w_vmem, sems, back_ref, gains_ref = rest
    else:
        grad_ref, w_vmem, sems, back_ref = rest
    copies = load_weights(order, w_hbm, w_vmem, sems)
    seqs, length = x_ref.shape[0], x_ref.shape[1]
    rows = seqs * length
    for copy in copies:
        copy.wait()
    gain_attn, gain_moe = gains_of(w_vmem)
    gate = gate_ref[...]
    high_low = sum_ref[:, D:]
    grad_gate = high_low + pltpu.roll(high_low, 96, 1)
    inner = jnp.sum(gate * grad_gate, axis=-1, keepdims=True)
    grad_logits = jnp.where(lanes_of(gate.shape) < 32, gate * (grad_gate - inner), 0.0)
    grad_logits = grad_logits.astype(bf16)
    w_small = w_vmem[:, :, QKV + D :].reshape(D, LANES)
    grad_normed_moe = sum_ref[:, :D] + nt(grad_logits, w_small)
    resid = resid_ref[...]
    inv_moe = rms(resid)
    grad_resid = g_ref[...].reshape(rows, D).astype(f32) + norm_back(
        resid, inv_moe, gain_moe, grad_normed_moe
    )
    grad_branch = grad_resid.astype(bf16)
    w_out = w_vmem[:, :, QKV : QKV + D].reshape(D, D)
    grad_mixed = nt(grad_branch, w_out)
    cosine, sine = cos_ref[...], sin_ref[...]
    low = lanes_of((length, LANES)) < 64
    for s in range(seqs):
        top = slice(s * length, (s + 1) * length)
        key_parts, value_parts = [], []
        for j in range(KEY_VALUE_HEADS):
            here = slice(j * LANES, (j + 1) * LANES)
            pair = slice((j // 2) * LANES, (j // 2 + 1) * LANES)
            query = halves(q_ref[top, here].astype(f32)).astype(bf16)
            key = doubled(k_ref[top, pair].astype(f32), j % 2 == 1).astype(bf16)
            value = doubled(v_ref[top, pair].astype(f32), j % 2 == 1).astype(bf16)
            grad_heads = halves(grad_mixed[top, here]).astype(bf16)
            probs = probs_ref[s * KEY_VALUE_HEADS + j]
            grad_probs = nt(grad_heads, value)
            grad_value = tn(probs.astype(bf16), grad_heads)
            grad_scores = probs * (grad_probs - jnp.sum(probs * grad_probs, axis=-1, keepdims=True))
            grad_scores = grad_scores.astype(bf16)
            grad_query = join(nn(grad_scores, key)) * scale
            grad_key = tn(grad_scores, query) * scale
            back_ref[top, here] = turn(grad_query, cosine, sine, True).astype(bf16)
            key_parts.append(grad_key + pltpu.roll(grad_key, 64, 1))
            value_parts.append(grad_value + pltpu.roll(grad_value, 64, 1))
        for c in range(4):
            grad_key = jnp.where(low, key_parts[2 * c], key_parts[2 * c + 1])
            grad_value = jnp.where(low, value_parts[2 * c], value_parts[2 * c + 1])
            back_ref[top, D + c * LANES : D + (c + 1) * LANES] = turn(
                grad_key, cosine, sine, True
            ).astype(bf16)
            back_ref[top, D + 512 + c * LANES : D + 512 + (c + 1) * LANES] = grad_value.astype(bf16)
    w_qkv = w_vmem[:, :, :QKV].reshape(D, QKV)
    grad_rows = back_ref[...]
    grad_normed = nt(grad_rows, w_qkv)
    x = x_ref[...].reshape(rows, D).astype(f32)
    inv_attn = rms(x)
    grad_in = grad_resid + norm_back(x, inv_attn, gain_attn, grad_normed)
    grad_ref[...] = grad_in.astype(bf16).reshape(seqs, length, D)
    if with_grads:
        gains_ref[0:1] = jnp.sum(grad_normed * x * inv_attn, axis=0, keepdims=True)
        gains_ref[1:2] = jnp.sum(grad_normed_moe * resid * inv_moe, axis=0, keepdims=True)
        row = lax.broadcasted_iota(jnp.int32, (LANES, LANES), 0)
        lane = lanes_of((LANES, LANES))
        for k in range(8):
            columns = pl.ds(pl.multiple_of(order[0, k] * LANES, LANES), LANES)
            part_qkv = tn(normed_ref[:, columns], grad_rows)
            part_out = tn(mixed_ref[:, columns], grad_branch)
            moe_rows = jnp.concatenate(
                [wide_ref[s, :, columns] for s in range(seqs)], axis=0
            )
            part_small = tn(moe_rows, grad_logits)
            for i in range(2):
                piece = gains_ref[i : i + 1, columns]
                turned = pltpu.roll(piece, 64, 1)
                part_small = part_small + jnp.where((row == i) & (lane >= 64), turned, 0.0)
                part_small = part_small + jnp.where((row == 64 + i) & (lane >= 64), piece, 0.0)
            for b in range(2):
                half = slice(b * 64, (b + 1) * 64)
                slot = order[1, 0] ^ b
                big_ref[k, slot, :, :QKV] = part_qkv[half].astype(bf16)
                big_ref[k, slot, :, QKV : QKV + D] = part_out[half].astype(bf16)
                big_ref[k, slot, :, QKV + D :] = part_small[half].astype(bf16)


def attn_backward(with_grads, order, sums, g, x, saved, cosine, sine, w_all):
    seqs, length = x.shape[0], x.shape[1]
    rows = seqs * length
    shape = jax.ShapeDtypeStruct
    outs = [shape((seqs, length, D), bf16)]
    scratch = [
        pltpu.VMEM((16, 64, WCOLS), bf16),
        pltpu.SemaphoreType.DMA((16,)),
        pltpu.VMEM((rows, QKV), bf16),
    ]
    if with_grads:
        outs.append(shape((8, 2, 64, WCOLS), bf16))
        scratch.append(pltpu.VMEM((8, D), f32))
    return pl.pallas_call(
        functools.partial(attn_backward_kernel, with_grads),
        out_shape=outs,
        in_specs=[smem()] + [vmem()] * 14 + [anywhere()],
        out_specs=[vmem()] * len(outs),
        scratch_shapes=scratch,
        compiler_params=pltpu.CompilerParams(vmem_limit_bytes=VMEM_LIMIT),
        cost_estimate=pl.CostEstimate(
            flops=4 * rows * D * 3400, bytes_accessed=20_000_000, transcendentals=0
        ),
        name="attn_backward",
    )(order, sums, g, x, *saved, cosine, sine, w_all)


def expert_kernel(mode, parts, which, *refs):
    refs = list(refs)
    take = lambda count: [refs.pop(0) for _ in range(count)]
    x_refs = take(parts)
    g_refs = take(parts) if mode else []
    w_in, w_down = take(2)
    out_refs = take(parts)
    if mode == 2:
        x_rows, g_rows, act_rows, gate_rows, up_rows = take(5)
    elif mode == 1:
        x_rows, g_rows = take(2)
    else:
        (x_rows,) = take(1)
    hot_ref, scale_ref, result_ref = take(3)
    per = x_rows.shape[0]
    hid = w_down.shape[0] // per
    first = which[0]
    spots = [(i, s) for i in range(parts) for s in range(x_refs[i].shape[0])]
    length = x_refs[0].shape[1]
    row8 = lax.broadcasted_iota(jnp.int32, (8, LANES), 0)
    lane8 = lanes_of((8, LANES))
    pick = jnp.where((lane8 == 64 + first + row8) & (row8 < per), 1.0, 0.0).astype(bf16)
    slot = lax.broadcasted_iota(jnp.int32, (SLOTS, length), 0).astype(f32)
    lane = lanes_of((SLOTS, LANES))
    for n, (i, s) in enumerate(spots):
        columns = x_refs[i][s, :, D:]
        places = nt(pick, columns)
        hot = jnp.concatenate(
            [jnp.where(places[j : j + 1] == slot, 1.0, 0.0) for j in range(per)], axis=0
        ).astype(bf16)
        hot_ref[n] = hot
        taken = nn(hot, x_refs[i][s])
        here = slice(n * SLOTS, (n + 1) * SLOTS)
        for j in range(per):
            block = taken[j * SLOTS : (j + 1) * SLOTS]
            x_rows[j, here] = block[:, :D].astype(bf16)
            own = (lane == first + j) | (lane == 32 + first + j)
            gate = jnp.sum(jnp.where(own, block[:, D:], 0.0), axis=-1, keepdims=True)
            scale_ref[j, here] = jnp.broadcast_to(gate, (SLOTS, LANES))
        if mode:
            taken = nn(hot, g_refs[i][s])
            for j in range(per):
                g_rows[j, here] = taken[j * SLOTS : (j + 1) * SLOTS].astype(bf16)
    total = len(spots) * SLOTS
    lane = lanes_of((total, LANES))
    for j in range(per):
        own_rows = slice(j * hid, (j + 1) * hid)
        rows = x_rows[j]
        gate_val = nt(rows, w_in[own_rows, :D])
        up_val = nt(rows, w_in[own_rows, D:])
        sig = jax.nn.sigmoid(gate_val)
        silu = gate_val * sig
        act = silu * up_val
        gate = scale_ref[j][:, 0:1]

        def forward():
            result_ref[j, :, :D] = (nn(act.astype(bf16), w_down[own_rows]) * gate).astype(bf16)

        def backward():
            inner = nt(g_rows[j], w_down[own_rows])
            grad_gw = jnp.sum(act.astype(bf16).astype(f32) * inner, axis=-1, keepdims=True)
            inner = inner * gate
            grad_gate = (inner * up_val * sig * (1.0 + gate_val * (1.0 - sig))).astype(bf16)
            grad_up = (inner * silu).astype(bf16)
            if mode == 2:
                act_rows[j] = (act * gate).astype(bf16)
                gate_rows[j] = grad_gate
                up_rows[j] = grad_up
            grad_in = nn(grad_gate, w_in[own_rows, :D]) + nn(grad_up, w_in[own_rows, D:])
            high = grad_gw.astype(bf16).astype(f32)
            extra = jnp.where(
                lane == first + j, high, jnp.where(lane == 32 + first + j, grad_gw - high, 0.0)
            )
            result_ref[j, :, :D] = grad_in.astype(bf16)
            result_ref[j, :, D:] = extra.astype(bf16)

        if mode == 0:
            forward()
        else:
            backward()
            if mode == 2:

                @pl.when(which[1] != 0)
                def _():
                    forward()

    for n, (i, s) in enumerate(spots):
        here = slice(n * SLOTS, (n + 1) * SLOTS)
        block = jnp.concatenate([result_ref[j, here] for j in range(per)], axis=0)
        out_refs[i][s] = tn(hot_ref[n], block).astype(bf16)


def expert_call(mode, which, x_parts, g_parts, w_in, w_down, per):
    parts = len(x_parts)
    seqs = sum(x.shape[0] for x in x_parts)
    length = x_parts[0].shape[1]
    hid = w_down.shape[0] // per
    total = seqs * SLOTS
    out_width = WIDE if mode else D
    shape = jax.ShapeDtypeStruct
    outs = [shape((x.shape[0], length, out_width), bf16) for x in x_parts]
    rows = (per, total, D)
    scratch = [
        pltpu.VMEM((seqs, per * SLOTS, length), bf16),
        pltpu.VMEM((per, total, LANES), f32),
        pltpu.VMEM((per, total, out_width), bf16),
    ]
    if mode == 2:
        outs += [shape(rows, bf16), shape(rows, bf16)] + [shape((per, total, hid), bf16)] * 3
    else:
        scratch = [pltpu.VMEM(rows, bf16)] * (2 if mode else 1) + scratch
    units = (3, 5, 7)[mode]
    whole = lambda a: pl.BlockSpec(a.shape, lambda i, *_: (0,) * len(a.shape))
    prefetch = [which]
    g_specs = []
    g_args = []
    if mode:
        if isinstance(g_parts, tuple):
            g_all, picks = g_parts
            prefetch.append(jnp.stack([p[0] for p in picks]))
            for n, (x, pick) in enumerate(zip(x_parts, picks)):
                count = x.shape[0]
                g_specs.append(
                    pl.BlockSpec(
                        (None, count, length, D),
                        functools.partial(
                            lambda n, m, i, which, index: (index[n], m, 0, 0), n, pick[1]
                        ),
                    )
                )
                g_args.append(g_all)
        else:
            g_specs = [whole(g) for g in g_parts]
            g_args = list(g_parts)
    body = functools.partial(expert_kernel, mode, parts)
    if len(prefetch) == 2:
        inner_body = body
        body = lambda which, index, *refs: inner_body(which, *refs)
    return pl.pallas_call(
        body,
        out_shape=outs,
        grid_spec=pltpu.PrefetchScalarGridSpec(
            num_scalar_prefetch=len(prefetch),
            grid=(1,),
            in_specs=[whole(x) for x in x_parts] + g_specs + [whole(w_in), whole(w_down)],
            out_specs=[whole(o) for o in outs],
            scratch_shapes=scratch,
        ),
        compiler_params=pltpu.CompilerParams(vmem_limit_bytes=VMEM_LIMIT),
        cost_estimate=pl.CostEstimate(
            flops=2 * units * per * total * D * hid,
            bytes_accessed=6_000_000 + 4 * seqs * length * WIDE,
            transcendentals=per * total * hid,
        ),
        name="experts_%d" % mode,
    )(*prefetch, *x_parts, *g_args, w_in, w_down)


def weight_grad_kernel(groups, *refs):
    refs = list(refs)
    sets = [[refs.pop(0) for _ in range(5)] for _ in range(groups)]
    in_ref, down_ref = refs
    for half in range(2):
        total = None
        for x_rows, g_rows, act, gate, up in sets:
            term = tn((up if half else gate)[0], x_rows[0])
            total = term if total is None else total + term
        in_ref[:, half * D : (half + 1) * D] = total
    total = None
    for x_rows, g_rows, act, gate, up in sets:
        term = tn(act[0], g_rows[0])
        total = term if total is None else total + term
    down_ref[...] = total


def weight_grads(saved, hid, per):
    tile = min(hid, 256)
    tiles = hid // tile
    specs, args = [], []
    for group in saved:
        for n, a in enumerate(group):
            if n < 2:
                specs.append(pl.BlockSpec((1,) + a.shape[1:], lambda j, h: (j, 0, 0)))
            else:
                specs.append(pl.BlockSpec((1, a.shape[1], tile), lambda j, h: (j, 0, h)))
            args.append(a)
    shape = jax.ShapeDtypeStruct
    count = sum(group[0].shape[1] for group in saved)
    return pl.pallas_call(
        functools.partial(weight_grad_kernel, len(saved)),
        out_shape=[shape((per * hid, 2 * D), f32), shape((per * hid, D), f32)],
        grid=(per, tiles),
        in_specs=specs,
        out_specs=[
            pl.BlockSpec((tile, 2 * D), lambda j, h: (j * tiles + h, 0)),
            pl.BlockSpec((tile, D), lambda j, h: (j * tiles + h, 0)),
        ],
        compiler_params=pltpu.CompilerParams(vmem_limit_bytes=VMEM_LIMIT),
        cost_estimate=pl.CostEstimate(
            flops=6 * per * count * D * hid, bytes_accessed=27_000_000, transcendentals=0
        ),
        name="weight_grads",
    )(*args)


class Ring:
    def __init__(self):
        self.ahead, self.behind, self.core = [], [], [(i, i ^ 1) for i in range(16)]
        for p, chip in enumerate(PATH):
            for b in range(2):
                here = chip * 2 + b
                self.ahead.append((here, PATH[(p + 1) % 8] * 2 + b))
                self.behind.append((here, PATH[(p - 1) % 8] * 2 + b))
        index = lax.axis_index("fsdp")
        place = jnp.asarray(PLACE, jnp.int32)[index // 2]
        chips = jnp.asarray(PATH, jnp.int32)[(place + jnp.arange(8)) % 8]
        self.chips = chips
        self.order = jnp.stack([chips, jnp.broadcast_to(index % 2, (8,))]).astype(jnp.int32)

    def plus(self, a):
        return lax.ppermute(a, "fsdp", self.ahead)

    def minus(self, a):
        return lax.ppermute(a, "fsdp", self.behind)

    def swap(self, a):
        return lax.ppermute(a, "fsdp", self.core)

    def gather(self, own):
        half = own.shape[0] // 2
        groups = [[own]]
        before = after = own
        for _ in range(3):
            before, after = self.plus(before), self.minus(after)
            groups.append([before, after])
        groups.append([self.plus(before[:half]), self.minus(after[half:])])
        return [group + [self.swap(a) for a in group] for group in groups]

    def picks(self):
        core = self.order[1, 0]
        out = []
        for k in range(5):
            chips = [self.chips[0]] if k == 0 else [self.chips[8 - k], self.chips[k]]
            out.append([(chip * 2 + (core ^ b), m if k == 4 else 0) for b in range(2) for m, chip in enumerate(chips)])
        return out

    def scatter(self, groups):
        kept = []
        for group in groups:
            count = len(group) // 2
            came = [self.swap(a) for a in group[count:]]
            kept.append([a.astype(f32) + b.astype(f32) for a, b in zip(group[:count], came)])
        up = self.minus(kept[4][0].astype(bf16))
        down = self.plus(kept[4][1].astype(bf16))
        for k in (3, 2, 1):
            to_before, to_after = kept[k]
            if k == 3:
                half = up.shape[0]
                to_before = jnp.concatenate([to_before[:half] + up, to_before[half:]])
                to_after = jnp.concatenate([to_after[:half], to_after[half:] + down])
            else:
                to_before, to_after = to_before + up, to_after + down
            up, down = self.minus(to_before.astype(bf16)), self.plus(to_after.astype(bf16))
        return kept[0][0] + up.astype(f32) + down.astype(f32)


def on_device(
    tokens,
    cotangent,
    routes,
    picture_start,
    w_qkv,
    w_out,
    w_router,
    gain_attn,
    gain_moe,
    w_gate_up,
    w_down,
):
    section = lax.axis_index("section")
    first_section = section == 0
    index = lax.axis_index("fsdp")
    devices = lax.axis_size("fsdp")
    seqs, length = tokens.shape[0], tokens.shape[1]
    rows = seqs * length
    w_in, w_down = w_gate_up[0], w_down[0]
    per = max(1, EXPERTS // devices)
    hid = w_down.shape[0] // per
    first_expert = index * EXPERTS // devices
    which = jnp.stack([first_expert, section]).astype(jnp.int32)
    ringed = devices == 16

    angles = np.arange(length)[:, None] * 10000.0 ** (-2.0 * (np.arange(LANES) % 32) / HEAD_SIZE)
    cosine = jnp.asarray(np.cos(angles), f32)
    sine = jnp.asarray(np.sin(angles), f32)
    starts = picture_start[:, 0]

    named = jnp.any(routes[0][..., None] == jnp.arange(LANES, dtype=jnp.int32), axis=2)
    earlier = jnp.asarray(np.tril(np.ones((length, length)), -1), bf16)
    place = jnp.einsum("ts,mse->mte", earlier, named.astype(bf16), preferred_element_type=f32)
    pos = jnp.where(named, place, 255.0).reshape(rows, LANES)

    if ringed:
        ring = Ring()
        order = ring.order
        gains = jnp.concatenate([gain_attn, gain_moe])
        side = jnp.concatenate([gains, jnp.zeros((62, 64), bf16)])
        small = jnp.concatenate([w_router[0], jnp.zeros((64, 32), bf16), side], axis=1)
        groups = ring.gather(jnp.concatenate([w_qkv[0], w_out[0], small], axis=1))
        near = [jnp.concatenate(groups[4][:2]), jnp.concatenate(groups[4][2:])]
        blocks = [[groups[0][0], groups[0][1]]]
        blocks += [[groups[k][1], groups[k][3]] for k in (1, 2, 3)]
        blocks += [[jnp.concatenate(groups[4][0:2]), jnp.concatenate(groups[4][2:4])]]
        blocks += [[groups[k][0], groups[k][2]] for k in (3, 2, 1)]
        w_all = jnp.stack([b for pair in blocks for b in pair]).reshape(8, 2, 64, WCOLS)
    else:
        order = jnp.stack([jnp.arange(8), jnp.zeros((8,))]).astype(jnp.int32)
        gather = lambda a: lax.all_gather(a[0], "fsdp", axis=0, tiled=True)
        big = jnp.concatenate([gather(w_qkv), gather(w_out)], axis=1).reshape(16, 64, QKV + D)
        gains = jnp.stack([gather(gain_attn), gather(gain_moe)]).reshape(2, 16, 64)
        side = jnp.concatenate(
            [jnp.moveaxis(gains, 0, 1), jnp.zeros((16, 62, 64), bf16)], axis=1
        )
        router = gather(w_router).reshape(16, 64, EXPERTS)
        small = jnp.concatenate([router, jnp.zeros((16, 64, 32), bf16), side], axis=2)
        w_all = jnp.concatenate([big, small], axis=2).reshape(8, 2, 64, WCOLS)

    def gather_rows(own):
        if ringed:
            return ring.gather(own)
        every = lax.all_gather(own, "fsdp", axis=0, tiled=True)
        return every.reshape(-1, 8, length, own.shape[-1])

    def scatter_rows(groups):
        if ringed:
            return ring.scatter(groups)
        every = groups.reshape((devices * seqs,) + groups.shape[2:])
        return lax.psum_scatter(every, "fsdp", scatter_dimension=0, tiled=True).astype(f32)

    def experts(mode, x_groups, g_groups):
        if ringed:
            payload, kept = [], []
            for n, group in enumerate(x_groups):
                g = None
                if mode:
                    g = (g_groups[0], g_groups[1][n]) if isinstance(g_groups, tuple) else g_groups[n]
                out = expert_call(mode, which, group, g, w_in, w_down, per)
                payload.append(out[: len(group)])
                kept.append(out[len(group) :])
            return payload, (weight_grads(kept, hid, per) if mode == 2 else None)

        def step(total, both):
            out = expert_call(
                mode, which, [both[0]], [both[1]] if mode else None, w_in, w_down, per
            )
            if mode == 2:
                total = jax.tree.map(jnp.add, total, list(weight_grads([out[1:]], hid, per)))
            return total, out[0]

        zero = [jnp.zeros((per * hid, 2 * D), f32), jnp.zeros((per * hid, D), f32)]
        total, payload = lax.scan(
            step, zero if mode == 2 else None, (x_groups, g_groups if mode else x_groups)
        )
        return payload, total

    payload, resid = attn_forward(False, order, starts, tokens, pos, cosine, sine, w_all)
    mixture = scatter_rows(experts(0, gather_rows(payload), None)[0])
    first_out = (resid.reshape(seqs, length, D) + mixture).astype(bf16)
    passed = lax.ppermute(first_out, "section", [(0, 1)])
    if ringed:
        g_all = lax.all_gather(cotangent, "fsdp", axis=0)
        g_second = (g_all, ring.picks())
    else:
        g_second = gather_rows(cotangent)

    layer_in = jnp.where(first_section, tokens, passed)
    payload, resid, *saved = attn_forward(True, order, starts, layer_in, pos, cosine, sine, w_all)
    saved = [payload, resid] + saved
    rows_all = gather_rows(payload)
    sums_second = scatter_rows(experts(1, rows_all, g_second)[0]).reshape(rows, WIDE)
    (grad_second,) = attn_backward(
        False, order, sums_second, cotangent, layer_in, saved, cosine, sine, w_all
    )

    passed_grad = lax.ppermute(grad_second, "section", [(1, 0)])
    g_third = jnp.where(first_section, passed_grad, cotangent)
    payload_third, (grad_in, grad_down) = experts(2, rows_all, gather_rows(g_third))
    sums_third = scatter_rows(payload_third)
    second_out = (resid.reshape(seqs, length, D) + sums_third[..., :D]).astype(bf16)
    section_out = jnp.where(first_section, first_out, second_out)
    sums = jnp.where(first_section, sums_third.reshape(rows, WIDE), sums_second)
    section_grad, big = attn_backward(
        True, order, sums, g_third, layer_in, saved, cosine, sine, w_all
    )

    if ringed:
        part = lambda k, b: big[k, b]
        own_groups = [[part(0, 0), part(0, 1)]]
        for k in (1, 2, 3):
            own_groups.append([part(8 - k, 0), part(k, 0), part(8 - k, 1), part(k, 1)])
        own_groups.append(
            [part(4, 0)[:32], part(4, 0)[32:], part(4, 1)[:32], part(4, 1)[32:]]
        )
        summed = ring.scatter(own_groups)
        g_qkv, g_out = summed[:, :QKV], summed[:, QKV : QKV + D]
        small = summed[:, QKV + D :]
        g_router, g_gain_attn, g_gain_moe = small[:, :EXPERTS], small[0, 64:], small[1, 64:]
    else:
        total = big.reshape(D, WCOLS)
        sum_up = lambda a: lax.psum_scatter(a, "fsdp", scatter_dimension=0, tiled=True)
        small = total[:, QKV + D :].astype(f32)
        g_qkv, g_out = sum_up(total[:, :QKV].astype(f32)), sum_up(total[:, QKV : QKV + D].astype(f32))
        g_router = sum_up(small[:, :EXPERTS])
        gains = small.reshape(16, 64, LANES)
        g_gain_attn = sum_up(gains[:, 0, 64:].reshape(D))
        g_gain_moe = sum_up(gains[:, 1, 64:].reshape(D))
    return (
        section_out[None],
        section_grad[None],
        g_qkv[None],
        g_out[None],
        g_router[None],
        g_gain_attn[None],
        g_gain_moe[None],
        grad_in[None],
        grad_down[None],
    )


def solution(mesh):
    return jax.shard_map(
        on_device,
        mesh=mesh,
        in_specs=(
            P(None, "fsdp", None),
            P(None, "fsdp", None),
            P("section", None, "fsdp", None),
            P(None, "fsdp"),
            P("section", "fsdp", None),
            P("section", "fsdp", None),
            P("section", "fsdp", None),
            P("section", "fsdp"),
            P("section", "fsdp"),
            P("section", "fsdp", None),
            P("section", "fsdp", None),
        ),
        out_specs=(
            P("section", None, "fsdp", None),
            P("section", None, "fsdp", None),
            P("section", "fsdp", None),
            P("section", "fsdp", None),
            P("section", "fsdp", None),
            P("section", "fsdp"),
            P("section", "fsdp"),
            P("section", "fsdp", None),
            P("section", "fsdp", None),
        ),
        check_vma=False,
    )
```

```python
import functools

import jax
import jax.numpy as jnp
import numpy as np
from jax import lax
from jax.experimental import pallas as pl
from jax.experimental.pallas import tpu as pltpu
from jax.sharding import PartitionSpec as P

D = 1024
QUERY_HEADS = 16
KEY_VALUE_HEADS = 8
HEAD_SIZE = 64
EXPERTS = 32
TOP = 8
PIC = 64
SLOTS = 32
LANES = 128
QKV = 2048
WIDE = D + LANES
WCOLS = QKV + D + LANES
epsilon = 1e-05
scale = HEAD_SIZE ** (-0.5)
f32 = jnp.float32
bf16 = jnp.bfloat16
VMEM_LIMIT = 30 * 1024 * 1024

PATH = (0, 2, 4, 6, 7, 5, 3, 1)
PLACE = tuple(PATH.index(c) for c in range(8))


def dot(a, b, ca, cb):
    return lax.dot_general(a, b, (((ca,), (cb,)), ((), ())), preferred_element_type=f32)


def nn(a, b):
    return dot(a, b, 1, 0)


def nt(a, b):
    return dot(a, b, 1, 1)


def tn(a, b):
    return dot(a, b, 0, 0)


def lanes_of(shape):
    return lax.broadcasted_iota(jnp.int32, shape, len(shape) - 1)


def rms(values):
    return lax.rsqrt(jnp.mean(values * values, axis=-1, keepdims=True) + epsilon)


def norm_back(values, inv, gain, grad):
    scaled = grad * gain
    inner = jnp.mean(scaled * values, axis=-1, keepdims=True)
    return inv * scaled - values * (inv * inv * inv * inner)


def turn(chunk, cosine, sine, back):
    first = (lanes_of(chunk.shape) & 63) < 32
    ahead = pltpu.roll(chunk, 96, 1)
    behind = pltpu.roll(chunk, 32, 1)
    if back:
        swapped = jnp.where(first, ahead, -behind)
    else:
        swapped = jnp.where(first, -ahead, behind)
    return chunk * cosine + swapped * sine


def halves(chunk):
    low = lanes_of(chunk.shape) < 64
    return jnp.concatenate([jnp.where(low, chunk, 0.0), jnp.where(low, 0.0, chunk)], axis=0)


def join(stacked):
    rows = stacked.shape[0] // 2
    low = lanes_of((rows, LANES)) < 64
    return jnp.where(low, stacked[:rows], stacked[rows:])


def doubled(chunk, odd):
    low = lanes_of(chunk.shape) < 64
    other = pltpu.roll(chunk, 64, 1)
    return jnp.where(low, other, chunk) if odd else jnp.where(low, chunk, other)


PARTS = ((0, QKV), (QKV, QKV + D), (QKV + D, WCOLS))


def load_weights(order, w_hbm, w_vmem, sems, first):
    copies = {}
    for part in first:
        columns = pl.ds(PARTS[part][0], PARTS[part][1] - PARTS[part][0])
        copies[part] = [
            pltpu.make_async_copy(
                w_hbm.at[k, b, :, columns],
                w_vmem.at[order[0, k] * 2 + (order[1, 0] ^ b), :, columns],
                sems.at[part * 16 + k * 2 + b],
            )
            for k in range(8)
            for b in range(2)
        ]
        for copy in copies[part]:
            copy.start()

    def wait(part):
        for copy in copies[part]:
            copy.wait()

    return wait


def gains_of(w_vmem):
    pieces = ([], [])
    for c in range(8):
        even = w_vmem[2 * c, 0:16, QKV + D :].astype(f32)
        odd = w_vmem[2 * c + 1, 0:16, QKV + D :].astype(f32)
        even = pltpu.roll(even, 64, 1)
        both = jnp.where(lanes_of(even.shape) < 64, even, odd)
        for i in range(2):
            pieces[i].append(both[i : i + 1])
    return jnp.concatenate(pieces[0], axis=1), jnp.concatenate(pieces[1], axis=1)


def attn_forward_kernel(
    save, order, starts, x_ref, pos_ref, cos_ref, sin_ref, w_hbm, *rest
):
    if not save:
        cot_ref, rest = rest[0], rest[1:]
    if save:
        (out_ref, resid_ref, gate_ref, normed_ref, q_ref, k_ref, v_ref, probs_ref, mixed_ref) = rest[:9]
        w_vmem, sems = rest[9:]
    else:
        out_ref, resid_ref, w_vmem, sems, mixed_ref = rest
    wait = load_weights(order, w_hbm, w_vmem, sems, (2, 0, 1))
    seqs, length = x_ref.shape[0], x_ref.shape[1]
    rows = seqs * length
    wait(2)
    gain_attn, gain_moe = gains_of(w_vmem)
    x = x_ref[...].reshape(rows, D).astype(f32)
    normed = (x * rms(x) * gain_attn).astype(bf16)
    wait(0)
    w_qkv = w_vmem[:, :, :QKV].reshape(D, QKV)
    qkv = nn(normed, w_qkv)
    cosine, sine = cos_ref[...], sin_ref[...]
    row_pos = lax.broadcasted_iota(jnp.int32, (length, length), 0)
    col_pos = lax.broadcasted_iota(jnp.int32, (length, length), 1)
    for s in range(seqs):
        top = slice(s * length, (s + 1) * length)
        start = starts[s]
        both = (
            (row_pos >= start) & (row_pos < start + PIC) & (col_pos >= start) & (col_pos < start + PIC)
        )
        bias = jnp.where((col_pos <= row_pos) | both, 0.0, -1e30)
        bias = jnp.concatenate([bias, bias], axis=0)
        keys, values = [], []
        for c in range(4):
            key = turn(qkv[top, D + c * LANES : D + (c + 1) * LANES], cosine, sine, False)
            value = qkv[top, D + 512 + c * LANES : D + 512 + (c + 1) * LANES]
            keys.append(key)
            values.append(value)
            if save:
                k_ref[top, c * LANES : (c + 1) * LANES] = key.astype(bf16)
                v_ref[top, c * LANES : (c + 1) * LANES] = value.astype(bf16)
        for j in range(KEY_VALUE_HEADS):
            query = turn(qkv[top, j * LANES : (j + 1) * LANES], cosine, sine, False)
            if save:
                q_ref[top, j * LANES : (j + 1) * LANES] = query.astype(bf16)
            key = doubled(keys[j // 2], j % 2 == 1).astype(bf16)
            value = doubled(values[j // 2], j % 2 == 1).astype(bf16)
            scores = nt(halves(query).astype(bf16), key) * scale + bias
            exponent = jnp.exp(scores - jnp.max(scores, axis=-1, keepdims=True))
            probs = exponent / jnp.sum(exponent, axis=-1, keepdims=True)
            if save:
                probs_ref[s * KEY_VALUE_HEADS + j] = probs
            mixed = join(nn(probs.astype(bf16), value))
            mixed_ref[top, j * LANES : (j + 1) * LANES] = mixed.astype(bf16)
    wait(1)
    w_out = w_vmem[:, :, QKV : QKV + D].reshape(D, D)
    resid = x + nn(mixed_ref[...], w_out)
    normed_moe = (resid * rms(resid) * gain_moe).astype(bf16)
    w_small = w_vmem[:, :, QKV + D :].reshape(D, LANES)
    logits = nn(normed_moe, w_small)
    pos = pos_ref[...]
    routed = pos < 64.0
    logits = jnp.where(routed, logits, -1e30)
    exponent = jnp.where(routed, jnp.exp(logits - jnp.max(logits, axis=-1, keepdims=True)), 0.0)
    gate = exponent / jnp.sum(exponent, axis=-1, keepdims=True)
    high = gate.astype(bf16).astype(f32)
    low = gate - high
    lane = lanes_of(gate.shape)
    columns = jnp.where(
        lane < 32,
        high,
        jnp.where(
            lane < 64,
            pltpu.roll(low, 32, 1),
            jnp.where(lane < 96, pltpu.roll(pos, 64, 1), 0.0),
        ),
    )
    out_ref[:, :, :D] = normed_moe.reshape(seqs, length, D)
    out_ref[:, :, D:] = columns.astype(bf16).reshape(seqs, length, LANES)
    resid_ref[...] = resid
    if not save:

        @pl.when(order[2, 0] != 0)
        def _():
            out_ref[:, :, :D] = cot_ref[...]

    if save:
        gate_ref[...] = gate
        normed_ref[...] = normed


def vmem():
    return pl.BlockSpec(memory_space=pltpu.VMEM)


def smem():
    return pl.BlockSpec(memory_space=pltpu.SMEM)


def hbm():
    return pl.BlockSpec(memory_space=pltpu.HBM)


def in_hbm(a):
    return pltpu.with_memory_space_constraint(a, pltpu.HBM)


def attn_forward(save, order, starts, x, pos, cosine, sine, w_all, cot=None):
    seqs, length = x.shape[0], x.shape[1]
    rows = seqs * length
    shape = jax.ShapeDtypeStruct
    outs = [shape((seqs, length, WIDE), bf16), shape((rows, D), f32)]
    scratch = [pltpu.VMEM((16, 64, WCOLS), bf16), pltpu.SemaphoreType.DMA((48,))]
    if save:
        outs += [
            shape((rows, LANES), f32),
            shape((rows, D), bf16),
            shape((rows, D), bf16),
            shape((rows, 512), bf16),
            shape((rows, 512), bf16),
            shape((seqs * KEY_VALUE_HEADS, 2 * length, length), f32),
            shape((rows, D), bf16),
        ]
    else:
        scratch.append(pltpu.VMEM((rows, D), bf16))
    return pl.pallas_call(
        functools.partial(attn_forward_kernel, save),
        out_shape=outs,
        in_specs=[smem(), smem(), vmem(), vmem(), vmem(), vmem(), hbm()] + [vmem()] * (not save),
        out_specs=[vmem()] * len(outs),
        scratch_shapes=scratch,
        compiler_params=pltpu.CompilerParams(vmem_limit_bytes=VMEM_LIMIT),
        cost_estimate=pl.CostEstimate(
            flops=2 * rows * D * 3400, bytes_accessed=12_000_000, transcendentals=rows * 2048
        ),
        name="attn_forward",
    )(order, starts, x, pos, cosine, sine, in_hbm(w_all), *(() if save else (cot,)))


def attn_backward_kernel(
    with_grads,
    order,
    sum_ref,
    g_ref,
    x_ref,
    wide_ref,
    resid_ref,
    gate_ref,
    normed_ref,
    q_ref,
    k_ref,
    v_ref,
    probs_ref,
    mixed_ref,
    cos_ref,
    sin_ref,
    w_hbm,
    *rest,
):
    if with_grads:
        grad_ref, big_ref, w_vmem, sems, back_ref, gains_ref = rest
    else:
        grad_ref, w_vmem, sems, back_ref = rest
    wait = load_weights(order, w_hbm, w_vmem, sems, (2, 1, 0))
    seqs, length = x_ref.shape[0], x_ref.shape[1]
    rows = seqs * length
    wait(2)
    gain_attn, gain_moe = gains_of(w_vmem)
    gate = gate_ref[...]
    high_low = sum_ref[:, D:]
    grad_gate = high_low + pltpu.roll(high_low, 96, 1)
    inner = jnp.sum(gate * grad_gate, axis=-1, keepdims=True)
    grad_logits = jnp.where(lanes_of(gate.shape) < 32, gate * (grad_gate - inner), 0.0)
    grad_logits = grad_logits.astype(bf16)
    w_small = w_vmem[:, :, QKV + D :].reshape(D, LANES)
    grad_normed_moe = sum_ref[:, :D] + nt(grad_logits, w_small)
    resid = resid_ref[...]
    inv_moe = rms(resid)
    grad_resid = g_ref[...].reshape(rows, D).astype(f32) + norm_back(
        resid, inv_moe, gain_moe, grad_normed_moe
    )
    grad_branch = grad_resid.astype(bf16)
    wait(1)
    w_out = w_vmem[:, :, QKV : QKV + D].reshape(D, D)
    grad_mixed = nt(grad_branch, w_out)
    cosine, sine = cos_ref[...], sin_ref[...]
    low = lanes_of((length, LANES)) < 64
    for s in range(seqs):
        top = slice(s * length, (s + 1) * length)
        key_parts, value_parts = [], []
        for j in range(KEY_VALUE_HEADS):
            here = slice(j * LANES, (j + 1) * LANES)
            pair = slice((j // 2) * LANES, (j // 2 + 1) * LANES)
            query = halves(q_ref[top, here].astype(f32)).astype(bf16)
            key = doubled(k_ref[top, pair].astype(f32), j % 2 == 1).astype(bf16)
            value = doubled(v_ref[top, pair].astype(f32), j % 2 == 1).astype(bf16)
            grad_heads = halves(grad_mixed[top, here]).astype(bf16)
            probs = probs_ref[s * KEY_VALUE_HEADS + j]
            grad_probs = nt(grad_heads, value)
            grad_value = tn(probs.astype(bf16), grad_heads)
            grad_scores = probs * (grad_probs - jnp.sum(probs * grad_probs, axis=-1, keepdims=True))
            grad_scores = grad_scores.astype(bf16)
            grad_query = join(nn(grad_scores, key)) * scale
            grad_key = tn(grad_scores, query) * scale
            back_ref[top, here] = turn(grad_query, cosine, sine, True).astype(bf16)
            key_parts.append(grad_key + pltpu.roll(grad_key, 64, 1))
            value_parts.append(grad_value + pltpu.roll(grad_value, 64, 1))
        for c in range(4):
            grad_key = jnp.where(low, key_parts[2 * c], key_parts[2 * c + 1])
            grad_value = jnp.where(low, value_parts[2 * c], value_parts[2 * c + 1])
            back_ref[top, D + c * LANES : D + (c + 1) * LANES] = turn(
                grad_key, cosine, sine, True
            ).astype(bf16)
            back_ref[top, D + 512 + c * LANES : D + 512 + (c + 1) * LANES] = grad_value.astype(bf16)
    wait(0)
    w_qkv = w_vmem[:, :, :QKV].reshape(D, QKV)
    grad_rows = back_ref[...]
    grad_normed = nt(grad_rows, w_qkv)
    x = x_ref[...].reshape(rows, D).astype(f32)
    inv_attn = rms(x)
    grad_in = grad_resid + norm_back(x, inv_attn, gain_attn, grad_normed)
    grad_ref[...] = grad_in.astype(bf16).reshape(seqs, length, D)
    if with_grads:
        gains_ref[0:1] = jnp.sum(grad_normed * x * inv_attn, axis=0, keepdims=True)
        gains_ref[1:2] = jnp.sum(grad_normed_moe * resid * inv_moe, axis=0, keepdims=True)
        row = lax.broadcasted_iota(jnp.int32, (LANES, LANES), 0)
        lane = lanes_of((LANES, LANES))
        for k in range(8):
            columns = pl.ds(pl.multiple_of(order[0, k] * LANES, LANES), LANES)
            part_qkv = tn(normed_ref[:, columns], grad_rows)
            part_out = tn(mixed_ref[:, columns], grad_branch)
            moe_rows = jnp.concatenate(
                [wide_ref[s, :, columns] for s in range(seqs)], axis=0
            )
            part_small = tn(moe_rows, grad_logits)
            for i in range(2):
                piece = gains_ref[i : i + 1, columns]
                turned = pltpu.roll(piece, 64, 1)
                part_small = part_small + jnp.where((row == i) & (lane >= 64), turned, 0.0)
                part_small = part_small + jnp.where((row == 64 + i) & (lane >= 64), piece, 0.0)
            for b in range(2):
                half = slice(b * 64, (b + 1) * 64)
                slot = order[1, 0] ^ b
                big_ref[k, slot, :, :QKV] = part_qkv[half].astype(bf16)
                big_ref[k, slot, :, QKV : QKV + D] = part_out[half].astype(bf16)
                big_ref[k, slot, :, QKV + D :] = part_small[half].astype(bf16)


def attn_backward(with_grads, order, sums, g, x, saved, cosine, sine, w_all):
    seqs, length = x.shape[0], x.shape[1]
    rows = seqs * length
    shape = jax.ShapeDtypeStruct
    outs = [shape((seqs, length, D), bf16)]
    scratch = [
        pltpu.VMEM((16, 64, WCOLS), bf16),
        pltpu.SemaphoreType.DMA((48,)),
        pltpu.VMEM((rows, QKV), bf16),
    ]
    if with_grads:
        outs.append(shape((8, 2, 64, WCOLS), bf16))
        scratch.append(pltpu.VMEM((8, D), f32))
    return pl.pallas_call(
        functools.partial(attn_backward_kernel, with_grads),
        out_shape=outs,
        in_specs=[smem()] + [vmem()] * 14 + [hbm()],
        out_specs=[vmem()] * len(outs),
        scratch_shapes=scratch,
        compiler_params=pltpu.CompilerParams(vmem_limit_bytes=VMEM_LIMIT),
        cost_estimate=pl.CostEstimate(
            flops=4 * rows * D * 3400, bytes_accessed=20_000_000, transcendentals=0
        ),
        name="attn_backward",
    )(order, sums, g, x, *saved, cosine, sine, in_hbm(w_all))


def expert_kernel(mode, parts, which, *refs):
    refs = list(refs)
    take = lambda count: [refs.pop(0) for _ in range(count)]
    x_refs = take(parts)
    g_refs = take(parts) if mode else []
    w_in, w_down = take(2)
    out_refs = take(parts)
    saved_refs = take(5) if mode == 2 else []
    x_rows = take(1)[0]
    g_rows = take(1)[0] if mode else None
    if mode == 2:
        act_rows, gate_rows, up_rows, sems = take(4)
    hot_ref, scale_ref, result_ref = take(3)

    def send(n, j):
        source = (x_rows, g_rows, act_rows, gate_rows, up_rows)[n]
        return pltpu.make_async_copy(source.at[j], saved_refs[n].at[j], sems.at[n, j])

    per = x_rows.shape[0]
    hid = w_down.shape[0] // per
    first = which[0]
    spots = [(i, s) for i in range(parts) for s in range(x_refs[i].shape[0])]
    length = x_refs[0].shape[1]
    row8 = lax.broadcasted_iota(jnp.int32, (8, LANES), 0)
    lane8 = lanes_of((8, LANES))
    pick = jnp.where((lane8 == 64 + first + row8) & (row8 < per), 1.0, 0.0).astype(bf16)
    slot = lax.broadcasted_iota(jnp.int32, (SLOTS, length), 0).astype(f32)
    lane = lanes_of((SLOTS, LANES))
    for n, (i, s) in enumerate(spots):
        columns = x_refs[i][s, :, D:]
        places = nt(pick, columns)
        hot = jnp.concatenate(
            [jnp.where(places[j : j + 1] == slot, 1.0, 0.0) for j in range(per)], axis=0
        ).astype(bf16)
        hot_ref[n] = hot
        taken = nn(hot, x_refs[i][s])
        here = slice(n * SLOTS, (n + 1) * SLOTS)
        for j in range(per):
            block = taken[j * SLOTS : (j + 1) * SLOTS]
            x_rows[j, here] = block[:, :D].astype(bf16)
            own = (lane == first + j) | (lane == 32 + first + j)
            gate = jnp.sum(jnp.where(own, block[:, D:], 0.0), axis=-1, keepdims=True)
            scale_ref[j, here] = jnp.broadcast_to(gate, (SLOTS, LANES))
        if mode:
            taken = nn(hot, g_refs[i][s, :, :D])
            for j in range(per):
                g_rows[j, here] = taken[j * SLOTS : (j + 1) * SLOTS].astype(bf16)
    total = len(spots) * SLOTS
    lane = lanes_of((total, LANES))
    if mode == 2:
        for n in range(2):
            for j in range(per):
                send(n, j).start()
    for j in range(per):
        own_rows = slice(j * hid, (j + 1) * hid)
        rows = x_rows[j]
        gate_val = nt(rows, w_in[own_rows, :D])
        up_val = nt(rows, w_in[own_rows, D:])
        sig = jax.nn.sigmoid(gate_val)
        silu = gate_val * sig
        act = silu * up_val
        gate = scale_ref[j][:, 0:1]

        def forward():
            result_ref[j, :, :D] = (nn(act.astype(bf16), w_down[own_rows]) * gate).astype(bf16)

        def backward():
            inner = nt(g_rows[j], w_down[own_rows])
            grad_gw = jnp.sum(act.astype(bf16).astype(f32) * inner, axis=-1, keepdims=True)
            inner = inner * gate
            grad_gate = (inner * up_val * sig * (1.0 + gate_val * (1.0 - sig))).astype(bf16)
            grad_up = (inner * silu).astype(bf16)
            if mode == 2:
                act_rows[j] = (act * gate).astype(bf16)
                gate_rows[j] = grad_gate
                up_rows[j] = grad_up
                for n in range(2, 5):
                    send(n, j).start()
            grad_in = nn(grad_gate, w_in[own_rows, :D]) + nn(grad_up, w_in[own_rows, D:])
            high = grad_gw.astype(bf16).astype(f32)
            extra = jnp.where(
                lane == first + j, high, jnp.where(lane == 32 + first + j, grad_gw - high, 0.0)
            )
            result_ref[j, :, :D] = grad_in.astype(bf16)
            result_ref[j, :, D:] = extra.astype(bf16)

        if mode == 0:
            forward()
        else:
            backward()
            if mode == 2:

                @pl.when(which[1] != 0)
                def _():
                    forward()

    for n, (i, s) in enumerate(spots):
        here = slice(n * SLOTS, (n + 1) * SLOTS)
        block = jnp.concatenate([result_ref[j, here] for j in range(per)], axis=0)
        out_refs[i][s] = tn(hot_ref[n], block).astype(bf16)
    if mode == 2:
        for n in range(5):
            for j in range(per):
                send(n, j).wait()


def expert_call(mode, which, x_parts, g_parts, w_in, w_down, per):
    parts = len(x_parts)
    seqs = sum(x.shape[0] for x in x_parts)
    length = x_parts[0].shape[1]
    hid = w_down.shape[0] // per
    total = seqs * SLOTS
    out_width = WIDE if mode else D
    shape = jax.ShapeDtypeStruct
    outs = [shape((x.shape[0], length, out_width), bf16) for x in x_parts]
    out_specs = [vmem()] * parts
    wide, narrow = (per, total, D), (per, total, hid)
    scratch = [pltpu.VMEM(wide, bf16)] * (2 if mode else 1)
    if mode == 2:
        saved = [wide, wide, narrow, narrow, narrow]
        outs += [pltpu.HBM(a, bf16) for a in saved]
        out_specs += [hbm()] * 5
        scratch += [pltpu.VMEM(narrow, bf16)] * 3 + [pltpu.SemaphoreType.DMA((5, per))]
    scratch += [
        pltpu.VMEM((seqs, per * SLOTS, length), bf16),
        pltpu.VMEM((per, total, LANES), f32),
        pltpu.VMEM((per, total, out_width), bf16),
    ]
    units = (3, 5, 5)[mode]
    g_args = list(g_parts) if mode else []

    def body(which, *refs):
        expert_kernel(mode, parts, which, *refs)

    return pl.pallas_call(
        body,
        out_shape=outs,
        in_specs=[smem()] + [vmem()] * (parts + len(g_args) + 2),
        out_specs=out_specs,
        scratch_shapes=scratch,
        compiler_params=pltpu.CompilerParams(vmem_limit_bytes=VMEM_LIMIT),
        cost_estimate=pl.CostEstimate(
            flops=2 * units * per * total * D * hid,
            bytes_accessed=6_000_000 + 4 * seqs * length * WIDE,
            transcendentals=per * total * hid,
        ),
        name="experts_%d" % mode,
    )(which, *x_parts, *g_args, w_in, w_down)


def weight_grad_kernel(groups, tile, *refs):
    refs = list(refs)
    sets = [refs[5 * n : 5 * n + 5] for n in range(groups)]
    in_ref, down_ref = refs[5 * groups : 5 * groups + 2]
    rows = refs[5 * groups + 2 : 5 * groups + 7]
    in_tile, down_tile, load_sems, store_sems = refs[5 * groups + 7 :]
    per, hid = rows[2].shape[0], rows[2].shape[2]
    loads = []
    for j in range(per):
        loads.append([])
        for n in (3, 4, 0, 2, 1):
            offset = 0
            for g in range(groups):
                count = sets[g][n].shape[1]
                loads[j].append(
                    pltpu.make_async_copy(
                        sets[g][n].at[j],
                        rows[n].at[j, pl.ds(offset, count)],
                        load_sems.at[j, n * groups + g],
                    )
                )
                offset += count
        for load in loads[j]:
            load.start()
    stores = []
    for j in range(per):
        for load in loads[j]:
            load.wait()
        for h in range(hid // tile):
            turn_of = len(stores)
            slot = turn_of % 2
            if turn_of >= 2:
                for store in stores[turn_of - 2]:
                    store.wait()
            columns = slice(h * tile, (h + 1) * tile)
            in_tile[slot, :, :D] = tn(rows[3][j, :, columns], rows[0][j])
            in_tile[slot, :, D:] = tn(rows[4][j, :, columns], rows[0][j])
            down_tile[slot] = tn(rows[2][j, :, columns], rows[1][j])
            where = pl.ds(j * hid + h * tile, tile)
            stores.append(
                [
                    pltpu.make_async_copy(in_tile.at[slot], in_ref.at[where], store_sems.at[slot, 0]),
                    pltpu.make_async_copy(
                        down_tile.at[slot], down_ref.at[where], store_sems.at[slot, 1]
                    ),
                ]
            )
            for store in stores[-1]:
                store.start()
    for pair in stores[-2:]:
        for store in pair:
            store.wait()


def weight_grads(saved, hid, per):
    tile = min(hid, 256)
    groups = len(saved)
    args = [in_hbm(a) for group in saved for a in group]
    count = sum(group[0].shape[1] for group in saved)
    wide, narrow = pltpu.VMEM((per, count, D), bf16), pltpu.VMEM((per, count, hid), bf16)
    return pl.pallas_call(
        functools.partial(weight_grad_kernel, groups, tile),
        out_shape=[pltpu.HBM((per * hid, 2 * D), f32), pltpu.HBM((per * hid, D), f32)],
        in_specs=[hbm()] * len(args),
        out_specs=[hbm()] * 2,
        scratch_shapes=[
            wide,
            wide,
            narrow,
            narrow,
            narrow,
            pltpu.VMEM((2, tile, 2 * D), f32),
            pltpu.VMEM((2, tile, D), f32),
            pltpu.SemaphoreType.DMA((per, 5 * groups)),
            pltpu.SemaphoreType.DMA((2, 2)),
        ],
        compiler_params=pltpu.CompilerParams(vmem_limit_bytes=VMEM_LIMIT),
        cost_estimate=pl.CostEstimate(
            flops=6 * per * count * D * hid, bytes_accessed=27_000_000, transcendentals=0
        ),
        name="weight_grads",
    )(*args)


class Ring:
    def __init__(self):
        self.ahead, self.behind, self.core = [], [], [(i, i ^ 1) for i in range(16)]
        for p, chip in enumerate(PATH):
            for b in range(2):
                here = chip * 2 + b
                self.ahead.append((here, PATH[(p + 1) % 8] * 2 + b))
                self.behind.append((here, PATH[(p - 1) % 8] * 2 + b))
        index = lax.axis_index("fsdp")
        place = jnp.asarray(PLACE, jnp.int32)[index // 2]
        chips = jnp.asarray(PATH, jnp.int32)[(place + jnp.arange(8)) % 8]
        self.chips = chips
        self.order = jnp.stack([chips, jnp.broadcast_to(index % 2, (8,))]).astype(jnp.int32)

    def plus(self, a):
        return lax.ppermute(a, "fsdp", self.ahead)

    def minus(self, a):
        return lax.ppermute(a, "fsdp", self.behind)

    def swap(self, a):
        return lax.ppermute(a, "fsdp", self.core)

    def gather(self, own, work=None):
        half = own.shape[0] // 2
        group, out, kept = [own], [], []
        for r in range(5):
            if r < 3:
                coming = [self.plus(group[0]), self.minus(group[-1])]
            elif r == 3:
                coming = [self.plus(group[0][:half]), self.minus(group[1][half:])]
            full = group + [self.swap(a) for a in group]
            done = work(r, full) if work else full
            if work and r:
                kept.append(self.meet(out[-1]))
            if r < 4:
                if work:
                    coming, done, kept = lax.optimization_barrier((coming, done, kept))
                group = coming
            out.append(done)
        return (out, kept) if work else out

    def meet(self, done):
        payload = done[0]
        count = len(payload) // 2
        return list(zip(payload[:count], [self.swap(a) for a in payload[count:]]))

    def scatter(self, kept, beside=None):
        add = lambda terms: functools.reduce(jnp.add, [a.astype(f32) for a in terms])
        out = [add(pair).astype(bf16) for pair in kept[4]]
        for k in (3, 2, 1, 0):
            up, down = lax.optimization_barrier((out[0], out[1]))
            up, down = self.minus(up), self.plus(down)
            if k == 2 and beside is not None:
                up, down, beside = lax.optimization_barrier((up, down, beside))
            if k == 0:
                return add(list(kept[0][0]) + [up, down]), beside
            if k == 3:
                half = up.shape[0]
                top = [a[:half] for a in kept[3][0]], [a[half:] for a in kept[3][0]]
                low = [a[:half] for a in kept[3][1]], [a[half:] for a in kept[3][1]]
                out = [
                    jnp.concatenate([add(list(top[0]) + [up]), add(top[1])]).astype(bf16),
                    jnp.concatenate([add(low[0]), add(list(low[1]) + [down])]).astype(bf16),
                ]
            else:
                out = [add(list(pair) + [a]).astype(bf16) for pair, a in zip(kept[k], (up, down))]


def on_device(
    tokens,
    cotangent,
    routes,
    picture_start,
    w_qkv,
    w_out,
    w_router,
    gain_attn,
    gain_moe,
    w_gate_up,
    w_down,
):
    section = lax.axis_index("section")
    first_section = section == 0
    index = lax.axis_index("fsdp")
    devices = lax.axis_size("fsdp")
    seqs, length = tokens.shape[0], tokens.shape[1]
    rows = seqs * length
    w_in, w_down = w_gate_up[0], w_down[0]
    per = max(1, EXPERTS // devices)
    hid = w_down.shape[0] // per
    first_expert = index * EXPERTS // devices
    which = jnp.stack([first_expert, section]).astype(jnp.int32)
    ringed = devices == 16

    angles = np.arange(length)[:, None] * 10000.0 ** (-2.0 * (np.arange(LANES) % 32) / HEAD_SIZE)
    cosine = jnp.asarray(np.cos(angles), f32)
    sine = jnp.asarray(np.sin(angles), f32)
    starts = picture_start[:, 0]

    named = jnp.any(routes[0][..., None] == jnp.arange(LANES, dtype=jnp.int32), axis=2)
    earlier = jnp.asarray(np.tril(np.ones((length, length)), -1), bf16)
    place = jnp.einsum("ts,mse->mte", earlier, named.astype(bf16), preferred_element_type=f32)
    pos = jnp.where(named, place, 255.0).reshape(rows, LANES)

    if ringed:
        ring = Ring()
        order = jnp.concatenate([ring.order, jnp.broadcast_to(section, (1, 8)).astype(jnp.int32)])
        gains = jnp.concatenate([gain_attn, gain_moe])
        side = jnp.concatenate([gains, jnp.zeros((62, 64), bf16)])
        small = jnp.concatenate([w_router[0], jnp.zeros((64, 32), bf16), side], axis=1)
        groups = ring.gather(jnp.concatenate([w_qkv[0], w_out[0], small], axis=1))
        blocks = [[groups[0][0], groups[0][1]]]
        blocks += [[groups[k][1], groups[k][3]] for k in (1, 2, 3)]
        blocks += [[jnp.concatenate(groups[4][0:2]), jnp.concatenate(groups[4][2:4])]]
        blocks += [[groups[k][0], groups[k][2]] for k in (3, 2, 1)]
        w_all = jnp.stack([b for pair in blocks for b in pair]).reshape(8, 2, 64, WCOLS)
    else:
        order = jnp.stack([jnp.arange(8), jnp.zeros((8,)), jnp.broadcast_to(section, (8,))])
        order = order.astype(jnp.int32)
        gather = lambda a: lax.all_gather(a[0], "fsdp", axis=0, tiled=True)
        big = jnp.concatenate([gather(w_qkv), gather(w_out)], axis=1).reshape(16, 64, QKV + D)
        gains = jnp.stack([gather(gain_attn), gather(gain_moe)]).reshape(2, 16, 64)
        side = jnp.concatenate(
            [jnp.moveaxis(gains, 0, 1), jnp.zeros((16, 62, 64), bf16)], axis=1
        )
        router = gather(w_router).reshape(16, 64, EXPERTS)
        small = jnp.concatenate([router, jnp.zeros((16, 64, 32), bf16), side], axis=2)
        w_all = jnp.concatenate([big, small], axis=2).reshape(8, 2, 64, WCOLS)

    def gather_rows(own):
        every = lax.all_gather(own, "fsdp", axis=0, tiled=True)
        return every.reshape(-1, 8, length, own.shape[-1])

    def phase(mode, own, g, x_groups=None):
        if ringed:
            seen, kept_rows = [], []

            def work(r, group):
                seen.append(group)
                x, other = (group, None) if x_groups is None else (x_groups[r], group)
                if mode == 1:
                    other = g[r]
                out = expert_call(mode, which, x, other, w_in, w_down, per)
                return [out[: len(x)], out[len(x) :]]

            out, kept = ring.gather(own, work)
            kept.append(ring.meet(out[4]))
            grads = weight_grads([o[1] for o in out], hid, per) if mode == 2 else None
            sums, grads = ring.scatter(kept, grads)
            return sums, seen, grads

        every = gather_rows(own)
        x_all, g_all = (every, g) if x_groups is None else (x_groups, every)

        def step(total, both):
            out = expert_call(mode, which, [both[0]], [both[1]] if mode else None, w_in, w_down, per)
            if mode == 2:
                total = jax.tree.map(jnp.add, total, list(weight_grads([out[1:]], hid, per)))
            return total, out[0]

        zero = [jnp.zeros((per * hid, 2 * D), f32), jnp.zeros((per * hid, D), f32)]
        total, payload = lax.scan(
            step, zero if mode == 2 else None, (x_all, g_all if mode else x_all)
        )
        flat = payload.reshape((devices * seqs,) + payload.shape[2:])
        sums = lax.psum_scatter(flat, "fsdp", scatter_dimension=0, tiled=True).astype(f32)
        return sums, x_all, total

    payload, resid = attn_forward(
        False, order, starts, tokens, pos, cosine, sine, w_all, cotangent
    )
    mixture, g_second, _ = phase(0, payload, None)
    first_out = (resid.reshape(seqs, length, D) + mixture).astype(bf16)
    passed = lax.ppermute(first_out, "section", [(0, 1)])
    layer_in = jnp.where(first_section, tokens, passed)
    payload, resid, *saved = attn_forward(True, order, starts, layer_in, pos, cosine, sine, w_all)
    saved = [payload, resid] + saved
    sums_second, rows_all, _ = phase(1, payload, g_second)
    sums_second = sums_second.reshape(rows, WIDE)
    (grad_second,) = attn_backward(
        False, order, sums_second, cotangent, layer_in, saved, cosine, sine, w_all
    )

    passed_grad = lax.ppermute(grad_second, "section", [(1, 0)])
    g_third = jnp.where(first_section, passed_grad, cotangent)
    sums_third, _, (grad_in, grad_down) = phase(2, g_third, None, rows_all)
    second_out = (resid.reshape(seqs, length, D) + sums_third[..., :D]).astype(bf16)
    section_out = jnp.where(first_section, first_out, second_out)
    sums = jnp.where(first_section, sums_third.reshape(rows, WIDE), sums_second)
    section_grad, big = attn_backward(
        True, order, sums, g_third, layer_in, saved, cosine, sine, w_all
    )

    if ringed:
        part = lambda k, b: big[k, b]
        own_groups = [[[part(0, 0), part(0, 1)]]]
        for k in (1, 2, 3):
            own_groups.append([[part(8 - k, 0), part(k, 0), part(8 - k, 1), part(k, 1)]])
        own_groups.append(
            [[part(4, 0)[:32], part(4, 0)[32:], part(4, 1)[:32], part(4, 1)[32:]]]
        )
        summed, _ = ring.scatter([ring.meet(group) for group in own_groups])
        g_qkv, g_out = summed[:, :QKV], summed[:, QKV : QKV + D]
        small = summed[:, QKV + D :]
        g_router, g_gain_attn, g_gain_moe = small[:, :EXPERTS], small[0, 64:], small[1, 64:]
    else:
        total = big.reshape(D, WCOLS)
        sum_up = lambda a: lax.psum_scatter(a, "fsdp", scatter_dimension=0, tiled=True)
        small = total[:, QKV + D :].astype(f32)
        g_qkv, g_out = sum_up(total[:, :QKV].astype(f32)), sum_up(total[:, QKV : QKV + D].astype(f32))
        g_router = sum_up(small[:, :EXPERTS])
        gains = small.reshape(16, 64, LANES)
        g_gain_attn = sum_up(gains[:, 0, 64:].reshape(D))
        g_gain_moe = sum_up(gains[:, 1, 64:].reshape(D))
    return (
        section_out[None],
        section_grad[None],
        g_qkv[None],
        g_out[None],
        g_router[None],
        g_gain_attn[None],
        g_gain_moe[None],
        grad_in[None],
        grad_down[None],
    )


def solution(mesh):
    return jax.shard_map(
        on_device,
        mesh=mesh,
        in_specs=(
            P(None, "fsdp", None),
            P(None, "fsdp", None),
            P("section", None, "fsdp", None),
            P(None, "fsdp"),
            P("section", "fsdp", None),
            P("section", "fsdp", None),
            P("section", "fsdp", None),
            P("section", "fsdp"),
            P("section", "fsdp"),
            P("section", "fsdp", None),
            P("section", "fsdp", None),
        ),
        out_specs=(
            P("section", None, "fsdp", None),
            P("section", None, "fsdp", None),
            P("section", "fsdp", None),
            P("section", "fsdp", None),
            P("section", "fsdp", None),
            P("section", "fsdp"),
            P("section", "fsdp"),
            P("section", "fsdp", None),
            P("section", "fsdp", None),
        ),
        check_vma=False,
    )
```

```python
import functools

import jax
import jax.numpy as jnp
import numpy as np
from jax import lax
from jax.experimental import pallas as pl
from jax.experimental.pallas import tpu as pltpu
from jax.sharding import PartitionSpec as P

D = 1024
QUERY_HEADS = 16
KEY_VALUE_HEADS = 8
HEAD_SIZE = 64
EXPERTS = 32
TOP = 8
PIC = 64
SLOTS = 32
LANES = 128
QKV = 2048
TILE = 16
TILES = D // LANES
WCOLS = QKV + D + LANES
epsilon = 1e-05
scale = HEAD_SIZE ** (-0.5)
f32 = jnp.float32
bf16 = jnp.bfloat16
VMEM_LIMIT = 30 * 1024 * 1024

PATH = (0, 2, 4, 6, 7, 5, 3, 1)
PLACE = tuple(PATH.index(c) for c in range(8))


def dot(a, b, ca, cb):
    return lax.dot_general(a, b, (((ca,), (cb,)), ((), ())), preferred_element_type=f32)


def nn(a, b):
    return dot(a, b, 1, 0)


def nt(a, b):
    return dot(a, b, 1, 1)


def tn(a, b):
    return dot(a, b, 0, 0)


def lanes_of(shape):
    return lax.broadcasted_iota(jnp.int32, shape, len(shape) - 1)


def rms(values):
    return lax.rsqrt(jnp.mean(values * values, axis=-1, keepdims=True) + epsilon)


def norm_back(values, inv, gain, grad):
    scaled = grad * gain
    inner = jnp.mean(scaled * values, axis=-1, keepdims=True)
    return inv * scaled - values * (inv * inv * inv * inner)


def turn(chunk, cosine, sine, back):
    first = (lanes_of(chunk.shape) & 63) < 32
    ahead = pltpu.roll(chunk, 96, 1)
    behind = pltpu.roll(chunk, 32, 1)
    if back:
        swapped = jnp.where(first, ahead, -behind)
    else:
        swapped = jnp.where(first, -ahead, behind)
    return chunk * cosine + swapped * sine


def halves(chunk):
    low = lanes_of(chunk.shape) < 64
    return jnp.concatenate([jnp.where(low, chunk, 0.0), jnp.where(low, 0.0, chunk)], axis=0)


def join(stacked):
    rows = stacked.shape[0] // 2
    low = lanes_of((rows, LANES)) < 64
    return jnp.where(low, stacked[:rows], stacked[rows:])


def doubled(chunk, odd):
    low = lanes_of(chunk.shape) < 64
    other = pltpu.roll(chunk, 64, 1)
    return jnp.where(low, other, chunk) if odd else jnp.where(low, chunk, other)


PARTS = ((0, QKV), (QKV, QKV + D), (QKV + D, WCOLS))


def wide(length):
    return length * TILES + length // 2


def plain(tiles):
    count = tiles.shape[0] // (TILE * TILES)
    tiles = tiles.reshape(count, TILES, TILE, LANES)
    columns = [tiles[:, c].reshape(count * TILE, LANES) for c in range(TILES)]
    return jnp.concatenate(columns, axis=1)


def store_tiles(ref, s, rows):
    for r in range(rows.shape[0] // TILE):
        for c in range(TILES):
            place = (r * TILES + c) * TILE
            block = rows[r * TILE : (r + 1) * TILE, c * LANES : (c + 1) * LANES]
            ref[s, place : place + TILE] = block.astype(ref.dtype)


def fold(columns):
    half = columns.shape[0] // 2
    low = lanes_of((half, LANES)) < 64
    return jnp.where(low, columns[:half], pltpu.roll(columns[half:], 64, 1))


def unfold(folded):
    return jnp.concatenate([folded, pltpu.roll(folded, 64, 1)], axis=0)


def load_weights(order, blocks, w_vmem, sems, turn_of):
    copies = {}
    for part in turn_of:
        columns = pl.ds(PARTS[part][0], PARTS[part][1] - PARTS[part][0])
        copies[part] = []
        for k in range(8):
            for b in range(2):
                target = w_vmem.at[order[0, k] * 2 + (order[1, 0] ^ b), :, columns]
                if k != 4:
                    pairs = [(blocks[(k if k < 4 else k + 1) * 2 + b], target)]
                else:
                    pairs = [(blocks[8 + 2 * b + h], target.at[pl.ds(32 * h, 32)]) for h in range(2)]
                for block, target in pairs:
                    sem = sems.at[part * 18 + len(copies[part])]
                    copies[part].append(pltpu.make_async_copy(block.at[:, columns], target, sem))
        for copy in copies[part]:
            copy.start()

    def wait(part):
        for copy in copies[part]:
            copy.wait()

    return wait


def gains_of(w_vmem):
    pieces = ([], [])
    for c in range(8):
        even = w_vmem[2 * c, 0:16, QKV + D :].astype(f32)
        odd = w_vmem[2 * c + 1, 0:16, QKV + D :].astype(f32)
        even = pltpu.roll(even, 64, 1)
        both = jnp.where(lanes_of(even.shape) < 64, even, odd)
        for i in range(2):
            pieces[i].append(both[i : i + 1])
    return jnp.concatenate(pieces[0], axis=1), jnp.concatenate(pieces[1], axis=1)


def attn_forward_kernel(save, order, starts, table_hbm, pos_hbm, *refs):
    x_hbms, blocks, refs = refs[:2], refs[2:20], refs[20:]
    out_ref, resid_ref, refs = refs[0], refs[1], refs[2:]
    if save:
        x_ref, gate_ref, normed_ref, q_ref, k_ref, v_ref, probs_ref, mixed_ref = refs[:8]
        passed_ref, refs = refs[8], refs[9:]
    else:
        x_ref, cot_ref, mixed_ref = refs[:3]
        refs = refs[3:]
    w_vmem, table_ref, pos_ref, sems, side_sems = refs
    second = order[2, 0] != 0
    if save:
        loads = [
            pltpu.make_async_copy(x_hbms[0], x_ref, side_sems.at[0]),
            pltpu.make_async_copy(x_hbms[1], passed_ref, side_sems.at[3]),
        ]
        loads[0].start()
        loads[1].start()

    else:
        loads = [
            pltpu.make_async_copy(x_hbms[0], x_ref, side_sems.at[0]),
            pltpu.make_async_copy(x_hbms[1], cot_ref, side_sems.at[3]),
        ]
        loads[0].start()
        loads[1].start()
    load_table = pltpu.make_async_copy(table_hbm, table_ref, side_sems.at[1])
    load_table.start()
    wait = load_weights(order, blocks, w_vmem, sems, (2, 0, 1))
    load_pos = pltpu.make_async_copy(pos_hbm, pos_ref, side_sems.at[2])
    load_pos.start()
    seqs, length = x_ref.shape[0], x_ref.shape[1]
    rows = seqs * length
    loads[0].wait()
    if save:
        loads[1].wait()

        @pl.when(second)
        def _():
            for s in range(seqs):
                x_ref[s] = plain(passed_ref[s])

    wait(2)
    gain_attn, gain_moe = gains_of(w_vmem)
    x = x_ref[...].reshape(rows, D).astype(f32)
    normed = (x * rms(x) * gain_attn).astype(bf16)
    row_pos = lax.broadcasted_iota(jnp.int32, (length, length), 0)
    col_pos = lax.broadcasted_iota(jnp.int32, (length, length), 1)
    load_table.wait()
    cosine, sine = table_ref[:, :LANES], table_ref[:, LANES:]
    wait(0)
    w_qkv = w_vmem[:, :, :QKV].reshape(D, QKV)
    qkv = nn(normed, w_qkv)
    heads = range(KEY_VALUE_HEADS)
    for s in range(seqs):
        top = slice(s * length, (s + 1) * length)
        start = starts[s]
        both = (
            (row_pos >= start) & (row_pos < start + PIC) & (col_pos >= start) & (col_pos < start + PIC)
        )
        bias = jnp.where((col_pos <= row_pos) | both, 0.0, -1e30)
        bias = jnp.concatenate([bias, bias], axis=0)
        keys, values = [], []
        for c in range(4):
            key = turn(qkv[top, D + c * LANES : D + (c + 1) * LANES], cosine, sine, False)
            value = qkv[top, D + 512 + c * LANES : D + 512 + (c + 1) * LANES]
            if save:
                k_ref[top, c * LANES : (c + 1) * LANES] = key.astype(bf16)
                v_ref[top, c * LANES : (c + 1) * LANES] = value.astype(bf16)
            for odd in (False, True):
                keys.append(doubled(key, odd).astype(bf16))
                values.append(doubled(value, odd).astype(bf16))
        for j in heads:
            query = turn(qkv[top, j * LANES : (j + 1) * LANES], cosine, sine, False)
            if save:
                q_ref[top, j * LANES : (j + 1) * LANES] = query.astype(bf16)
            scores = nt(halves(query).astype(bf16), keys[j]) * scale + bias
            exponent = jnp.exp(scores - jnp.max(scores, axis=-1, keepdims=True))
            probs = exponent * (1.0 / jnp.sum(exponent, axis=-1, keepdims=True))
            if save:
                probs_ref[s * KEY_VALUE_HEADS + j] = probs
            mixed = join(nn(probs.astype(bf16), values[j]))
            mixed_ref[top, j * LANES : (j + 1) * LANES] = mixed.astype(bf16)
    wait(1)
    w_out = w_vmem[:, :, QKV : QKV + D].reshape(D, D)
    resid = x + nn(mixed_ref[...], w_out)
    normed_moe = (resid * rms(resid) * gain_moe).astype(bf16)
    w_small = w_vmem[:, :, QKV + D :].reshape(D, LANES)
    logits = nn(normed_moe, w_small)
    load_pos.wait()
    pos = pos_ref[...]
    routed = pos < 64.0
    logits = jnp.where(routed, logits, -1e30)
    exponent = jnp.where(routed, jnp.exp(logits - jnp.max(logits, axis=-1, keepdims=True)), 0.0)
    gate = exponent * (1.0 / jnp.sum(exponent, axis=-1, keepdims=True))
    lane = lanes_of(gate.shape)
    columns = jnp.where(lane < 32, gate, pltpu.roll(pos, 32, 1))
    for s in range(seqs):
        top = slice(s * length, (s + 1) * length)
        store_tiles(out_ref, s, normed_moe[top])
        out_ref[s, length * TILES :] = fold(columns[top]).astype(bf16)
    if save:
        resid_ref[...] = resid
        gate_ref[...] = gate
        normed_ref[...] = normed
    else:
        for s in range(seqs):
            store_tiles(resid_ref, s, resid[s * length : (s + 1) * length])
        loads[1].wait()

        @pl.when(second)
        def _():
            for s in range(seqs):
                store_tiles(out_ref, s, cot_ref[s])


def vmem():
    return pl.BlockSpec(memory_space=pltpu.VMEM)


def smem():
    return pl.BlockSpec(memory_space=pltpu.SMEM)


def hbm():
    return pl.BlockSpec(memory_space=pltpu.HBM)


def in_hbm(a):
    return pltpu.with_memory_space_constraint(a, pltpu.HBM)


def attn_forward(save, order, starts, table, pos, x, other, w_all):
    seqs, length = x.shape[0], x.shape[1]
    rows = seqs * length
    shape = jax.ShapeDtypeStruct
    tiles = (seqs, length * TILES, LANES)
    outs = [shape((seqs, wide(length), LANES), bf16), shape((rows, D) if save else tiles, f32)]
    probs = (seqs * KEY_VALUE_HEADS, 2 * length, length)
    scratch = []
    if save:
        outs += [
            shape((seqs, length, D), bf16),
            shape((rows, LANES), f32),
            shape((rows, D), bf16),
            shape((rows, D), bf16),
            shape((rows, 512), bf16),
            shape((rows, 512), bf16),
            shape(probs, f32),
            shape((rows, D), bf16),
        ]
        scratch = [pltpu.VMEM(tiles, bf16)]
    else:
        scratch = [pltpu.VMEM((seqs, length, D), bf16)] * 2
        scratch.append(pltpu.VMEM((rows, D), bf16))
    scratch += [
        pltpu.VMEM((16, 64, WCOLS), bf16),
        pltpu.VMEM((length, 2 * LANES), f32),
        pltpu.VMEM((rows, LANES), f32),
        pltpu.SemaphoreType.DMA((54,)),
        pltpu.SemaphoreType.DMA((4,)),
    ]
    return pl.pallas_call(
        functools.partial(attn_forward_kernel, save),
        out_shape=outs,
        in_specs=[smem(), smem()] + [hbm()] * 22,
        out_specs=[vmem()] * len(outs),
        scratch_shapes=scratch,
        compiler_params=pltpu.CompilerParams(vmem_limit_bytes=VMEM_LIMIT),
        cost_estimate=pl.CostEstimate(
            flops=2 * rows * D * 3400, bytes_accessed=12_000_000, transcendentals=rows * 2048
        ),
        name="attn_forward",
    )(order, starts, *map(in_hbm, [table, pos, x, other] + w_all))


def attn_backward_kernel(
    with_grads,
    order,
    sum_ref,
    g_ref,
    x_ref,
    wide_ref,
    resid_ref,
    gate_ref,
    normed_ref,
    q_ref,
    k_ref,
    v_ref,
    probs_ref,
    mixed_ref,
    table_ref,
    *rest,
):
    blocks, rest = rest[:18], rest[18:]
    if with_grads:
        grad_ref, big_refs, rest = rest[0], rest[1:11], rest[11:]
        w_vmem, sems, back_ref, gains_ref = rest
    else:
        grad_ref, w_vmem, sems, back_ref = rest
    wait = load_weights(order, blocks, w_vmem, sems, (2, 1, 0))
    seqs, length = x_ref.shape[0], x_ref.shape[1]
    rows = seqs * length
    wait(2)
    gain_attn, gain_moe = gains_of(w_vmem)
    gate = gate_ref[...]
    tiles = length * TILES
    high_low = jnp.concatenate([unfold(sum_ref[s, tiles:]) for s in range(seqs)], axis=0)
    grad_gate = high_low + pltpu.roll(high_low, 96, 1)
    inner = jnp.sum(gate * grad_gate, axis=-1, keepdims=True)
    grad_logits = jnp.where(lanes_of(gate.shape) < 32, gate * (grad_gate - inner), 0.0)
    grad_logits = grad_logits.astype(bf16)
    w_small = w_vmem[:, :, QKV + D :].reshape(D, LANES)
    summed = jnp.concatenate([plain(sum_ref[s, :tiles]) for s in range(seqs)], axis=0)
    grad_normed_moe = summed + nt(grad_logits, w_small)
    resid = resid_ref[...]
    inv_moe = rms(resid)
    if with_grads:
        g = jnp.concatenate([plain(g_ref[s]) for s in range(seqs)], axis=0)
    else:
        g = g_ref[...].reshape(rows, D)
    grad_resid = g.astype(f32) + norm_back(resid, inv_moe, gain_moe, grad_normed_moe)
    grad_branch = grad_resid.astype(bf16)
    wait(1)
    w_out = w_vmem[:, :, QKV : QKV + D].reshape(D, D)
    grad_mixed = nt(grad_branch, w_out)
    cosine, sine = table_ref[:, :LANES], table_ref[:, LANES:]
    low = lanes_of((length, LANES)) < 64
    for s in range(seqs):
        top = slice(s * length, (s + 1) * length)
        key_parts, value_parts = [], []
        for j in range(KEY_VALUE_HEADS):
            here = slice(j * LANES, (j + 1) * LANES)
            pair = slice((j // 2) * LANES, (j // 2 + 1) * LANES)
            query = halves(q_ref[top, here].astype(f32)).astype(bf16)
            key = doubled(k_ref[top, pair].astype(f32), j % 2 == 1).astype(bf16)
            value = doubled(v_ref[top, pair].astype(f32), j % 2 == 1).astype(bf16)
            grad_heads = halves(grad_mixed[top, here]).astype(bf16)
            probs = probs_ref[s * KEY_VALUE_HEADS + j]
            grad_probs = nt(grad_heads, value)
            grad_value = tn(probs.astype(bf16), grad_heads)
            grad_scores = probs * (grad_probs - jnp.sum(probs * grad_probs, axis=-1, keepdims=True))
            grad_scores = grad_scores.astype(bf16)
            grad_query = join(nn(grad_scores, key)) * scale
            grad_key = tn(grad_scores, query) * scale
            back_ref[top, here] = turn(grad_query, cosine, sine, True).astype(bf16)
            key_parts.append(grad_key + pltpu.roll(grad_key, 64, 1))
            value_parts.append(grad_value + pltpu.roll(grad_value, 64, 1))
        for c in range(4):
            grad_key = jnp.where(low, key_parts[2 * c], key_parts[2 * c + 1])
            grad_value = jnp.where(low, value_parts[2 * c], value_parts[2 * c + 1])
            back_ref[top, D + c * LANES : D + (c + 1) * LANES] = turn(
                grad_key, cosine, sine, True
            ).astype(bf16)
            back_ref[top, D + 512 + c * LANES : D + 512 + (c + 1) * LANES] = grad_value.astype(bf16)
    wait(0)
    w_qkv = w_vmem[:, :, :QKV].reshape(D, QKV)
    grad_rows = back_ref[...]
    grad_normed = nt(grad_rows, w_qkv)
    x = x_ref[...].reshape(rows, D).astype(f32)
    inv_attn = rms(x)
    grad_in = grad_resid + norm_back(x, inv_attn, gain_attn, grad_normed)
    if with_grads:
        grad_ref[...] = grad_in.astype(bf16).reshape(seqs, length, D)
    else:
        for s in range(seqs):
            store_tiles(grad_ref, s, grad_in[s * length : (s + 1) * length])

        @pl.when(order[2, 0] == 0)
        def _():
            for s in range(seqs):
                store_tiles(grad_ref, s, g_ref[s])

    if with_grads:
        gains_ref[0:1] = jnp.sum(grad_normed * x * inv_attn, axis=0, keepdims=True)
        gains_ref[1:2] = jnp.sum(grad_normed_moe * resid * inv_moe, axis=0, keepdims=True)
        row = lax.broadcasted_iota(jnp.int32, (LANES, LANES), 0)
        lane = lanes_of((LANES, LANES))
        for k in range(8):
            columns = pl.ds(pl.multiple_of(order[0, k] * LANES, LANES), LANES)
            part_qkv = tn(normed_ref[:, columns], grad_rows)
            part_out = tn(mixed_ref[:, columns], grad_branch)
            places = [(r * TILES + order[0, k]) * TILE for r in range(length // TILE)]
            moe_rows = jnp.concatenate(
                [
                    wide_ref[s, pl.ds(pl.multiple_of(place, TILE), TILE)]
                    for s in range(seqs)
                    for place in places
                ],
                axis=0,
            )
            part_small = tn(moe_rows, grad_logits)
            for i in range(2):
                piece = gains_ref[i : i + 1, columns]
                turned = pltpu.roll(piece, 64, 1)
                part_small = part_small + jnp.where((row == i) & (lane >= 64), turned, 0.0)
                part_small = part_small + jnp.where((row == 64 + i) & (lane >= 64), piece, 0.0)
            n = min(k, 8 - k)
            place = slice(64, 128) if 0 < k < 4 else slice(0, 64)
            for part, columns in (
                (part_qkv, slice(0, QKV)),
                (part_out, slice(QKV, QKV + D)),
                (part_small, slice(QKV + D, WCOLS)),
            ):
                first_core = order[1, 0] == 0
                upper, lower = part[:64], part[64:]
                mine = jnp.where(first_core, upper, lower)
                big_refs[n][place, columns] = mine.astype(bf16)
                other = jnp.where(first_core, lower, upper)
                big_refs[5 + n][place, columns] = other.astype(bf16)


def attn_backward(with_grads, order, sums, g, saved, table, w_all):
    payload, resid, x, gate, normed, q, k, v, probs, mixed = saved
    seqs, length = x.shape[0], x.shape[1]
    rows = seqs * length
    shape = jax.ShapeDtypeStruct
    outs = [shape((seqs, length, D) if with_grads else (seqs, length * TILES, LANES), bf16)]
    scratch = [
        pltpu.VMEM((16, 64, WCOLS), bf16),
        pltpu.SemaphoreType.DMA((54,)),
        pltpu.VMEM((rows, QKV), bf16),
    ]
    if with_grads:
        outs += [shape((n, WCOLS), bf16) for n in (64, 128, 128, 128, 64)] * 2
        scratch.append(pltpu.VMEM((8, D), f32))
    return pl.pallas_call(
        functools.partial(attn_backward_kernel, with_grads),
        out_shape=outs,
        in_specs=[smem()] + [vmem()] * 13 + [hbm()] * 18,
        out_specs=[vmem()] * len(outs),
        scratch_shapes=scratch,
        compiler_params=pltpu.CompilerParams(vmem_limit_bytes=VMEM_LIMIT),
        cost_estimate=pl.CostEstimate(
            flops=4 * rows * D * 3400, bytes_accessed=20_000_000, transcendentals=0
        ),
        name="attn_backward",
    )(
        order, sums, g, x, payload, resid, gate, normed, q, k, v, probs, mixed, table, *map(in_hbm, w_all)
    )


def expert_kernel(mode, parts, which, *refs):
    refs = list(refs)
    take = lambda count: [refs.pop(0) for _ in range(count)]
    x_refs = take(parts)
    g_refs = take(parts) if mode else []
    w_in, w_down = take(2)
    out_refs = take(parts)
    saved_refs = take(5) if mode == 2 else []
    x_rows = take(1)[0]
    g_rows = take(1)[0] if mode else None
    if mode == 2:
        act_rows, gate_rows, up_rows, sems = take(4)
    hot_ref, scale_ref, result_ref = take(3)

    def send(n, j):
        source = (x_rows, g_rows, act_rows, gate_rows, up_rows)[n]
        return pltpu.make_async_copy(source.at[j], saved_refs[n].at[j], sems.at[n, j])

    per = x_rows.shape[0]
    hid = w_down.shape[0] // per
    first = which[0]
    spots = [(i, s) for i in range(parts) for s in range(x_refs[i].shape[0])]
    tiles = x_refs[0].shape[1] // 17 * 16
    length = tiles // TILES
    row8 = lax.broadcasted_iota(jnp.int32, (8, LANES), 0)
    lane8 = lanes_of((8, LANES))
    pick = jnp.where((lane8 == 32 + first + row8) & (row8 < per), 1.0, 0.0).astype(bf16)
    slot = lax.broadcasted_iota(jnp.int32, (SLOTS, length), 0).astype(f32)
    lane = lanes_of((SLOTS, LANES))
    for n, (i, s) in enumerate(spots):
        columns = unfold(x_refs[i][s, tiles:].astype(f32)).astype(bf16)
        places = nt(pick, columns)
        hot = jnp.concatenate(
            [jnp.where(places[j : j + 1] == slot, 1.0, 0.0) for j in range(per)], axis=0
        ).astype(bf16)
        hot_ref[n] = hot
        taken = nn(hot, jnp.concatenate([plain(x_refs[i][s, :tiles]), columns], axis=1))
        here = slice(n * SLOTS, (n + 1) * SLOTS)
        for j in range(per):
            block = taken[j * SLOTS : (j + 1) * SLOTS]
            x_rows[j, here] = block[:, :D].astype(bf16)
            gate = jnp.sum(jnp.where(lane == first + j, block[:, D:], 0.0), axis=-1, keepdims=True)
            scale_ref[j, here] = jnp.broadcast_to(gate, (SLOTS, LANES))
        if mode:
            taken = nn(hot, plain(g_refs[i][s, :tiles]))
            for j in range(per):
                g_rows[j, here] = taken[j * SLOTS : (j + 1) * SLOTS].astype(bf16)
    total = len(spots) * SLOTS
    lane = lanes_of((total, LANES))
    if mode == 2:
        for n in range(2):
            for j in range(per):
                send(n, j).start()
    for j in range(per):
        own_rows = slice(j * hid, (j + 1) * hid)
        rows = x_rows[j]
        gate_val = nt(rows, w_in[own_rows, :D])
        up_val = nt(rows, w_in[own_rows, D:])
        sig = jax.nn.sigmoid(gate_val)
        silu = gate_val * sig
        act = silu * up_val
        gate = scale_ref[j][:, 0:1]

        def forward():
            result_ref[j, :, :D] = (nn(act.astype(bf16), w_down[own_rows]) * gate).astype(bf16)

        def backward():
            inner = nt(g_rows[j], w_down[own_rows])
            grad_gw = jnp.sum(act.astype(bf16).astype(f32) * inner, axis=-1, keepdims=True)
            inner = inner * gate
            grad_gate = (inner * up_val * sig * (1.0 + gate_val * (1.0 - sig))).astype(bf16)
            grad_up = (inner * silu).astype(bf16)
            if mode == 2:
                act_rows[j] = (act * gate).astype(bf16)
                gate_rows[j] = grad_gate
                up_rows[j] = grad_up
                for n in range(2, 5):
                    send(n, j).start()
            grad_in = nn(grad_gate, w_in[own_rows, :D]) + nn(grad_up, w_in[own_rows, D:])
            high = grad_gw.astype(bf16).astype(f32)
            extra = jnp.where(
                lane == first + j, high, jnp.where(lane == 32 + first + j, grad_gw - high, 0.0)
            )
            result_ref[j, :, :D] = grad_in.astype(bf16)
            result_ref[j, :, D:] = extra.astype(bf16)

        if mode == 0:
            forward()
        else:
            backward()
            if mode == 2:

                @pl.when(which[1] != 0)
                def _():
                    forward()

    for n, (i, s) in enumerate(spots):
        here = slice(n * SLOTS, (n + 1) * SLOTS)
        block = jnp.concatenate([result_ref[j, here] for j in range(per)], axis=0)
        block = tn(hot_ref[n], block)
        store_tiles(out_refs[i], s, block[:, :D])
        if mode:
            out_refs[i][s, tiles:] = fold(block[:, D:]).astype(bf16)
    if mode == 2:
        for n in range(5):
            for j in range(per):
                send(n, j).wait()


def expert_call(mode, which, x_parts, g_parts, w_in, w_down, per):
    parts = len(x_parts)
    seqs = sum(x.shape[0] for x in x_parts)
    whole = x_parts[0].shape[1]
    length = whole // 17 * 16 // TILES
    hid = w_down.shape[0] // per
    total = seqs * SLOTS
    out_width = D + LANES if mode else D
    out_rows = whole if mode else length * TILES
    shape = jax.ShapeDtypeStruct
    outs = [shape((x.shape[0], out_rows, LANES), bf16) for x in x_parts]
    out_specs = [vmem()] * parts
    wide, narrow = (per, total, D), (per, total, hid)
    scratch = [pltpu.VMEM(wide, bf16)] * (2 if mode else 1)
    if mode == 2:
        saved = [wide, wide, narrow, narrow, narrow]
        outs += [pltpu.HBM(a, bf16) for a in saved]
        out_specs += [hbm()] * 5
        scratch += [pltpu.VMEM(narrow, bf16)] * 3 + [pltpu.SemaphoreType.DMA((5, per))]
    scratch += [
        pltpu.VMEM((seqs, per * SLOTS, length), bf16),
        pltpu.VMEM((per, total, LANES), f32),
        pltpu.VMEM((per, total, out_width), bf16),
    ]
    units = (3, 5, 5)[mode]
    g_args = list(g_parts) if mode else []

    def body(which, *refs):
        expert_kernel(mode, parts, which, *refs)

    return pl.pallas_call(
        body,
        out_shape=outs,
        in_specs=[smem()] + [vmem()] * (parts + len(g_args) + 2),
        out_specs=out_specs,
        scratch_shapes=scratch,
        compiler_params=pltpu.CompilerParams(vmem_limit_bytes=VMEM_LIMIT),
        cost_estimate=pl.CostEstimate(
            flops=2 * units * per * total * D * hid,
            bytes_accessed=6_000_000 + 4 * seqs * length * D,
            transcendentals=per * total * hid,
        ),
        name="experts_%d" % mode,
    )(which, *x_parts, *g_args, w_in, w_down)


def weight_grad_kernel(groups, tile, j, *refs):
    refs = list(refs)
    sets = [refs[5 * n : 5 * n + 5] for n in range(groups)]
    refs = refs[5 * groups + (2 if j else 0) :]
    in_ref, down_ref, rows = refs[0], refs[1], refs[2:7]
    in_tile, down_tile, load_sems, store_sems = refs[7:]
    hid = rows[2].shape[1]
    loads = []
    for n in (3, 0, 4, 2, 1):
        offset = 0
        for g in range(groups):
            count = sets[g][n].shape[1]
            loads.append(
                pltpu.make_async_copy(
                    sets[g][n].at[j],
                    rows[n].at[pl.ds(offset, count)],
                    load_sems.at[n * groups + g],
                )
            )
            offset += count
    for load in loads:
        load.start()
    tiles = hid // tile
    stores = []

    def store(source, target, sem):
        stores.append(pltpu.make_async_copy(source, target, sem))
        stores[-1].start()

    waited = 0
    for h in range(tiles):
        columns = slice(h * tile, (h + 1) * tile)
        where = pl.ds(j * hid + h * tile, tile)
        for n, upto, target in ((3, 2, 0), (4, 3, 1), (2, 5, 2)):
            for load in loads[waited : upto * groups]:
                load.wait()
            waited = max(waited, upto * groups)
            if target < 2:
                part = pl.ds(target * D, D)
                in_tile[h, :, part] = tn(rows[n][:, columns], rows[0][...])
                store(in_tile.at[h, :, part], in_ref.at[where, part], store_sems.at[h, target])
            else:
                down_tile[h] = tn(rows[n][:, columns], rows[1][...])
                store(down_tile.at[h], down_ref.at[where], store_sems.at[h, 2])
    for copy in stores:
        copy.wait()


def weight_grads(saved, hid, per, j, earlier=()):
    tile = min(hid, 256)
    groups = len(saved)
    args = [in_hbm(a) for group in saved for a in group]
    count = sum(group[0].shape[1] for group in saved)
    wide, narrow = pltpu.VMEM((count, D), bf16), pltpu.VMEM((count, hid), bf16)
    earlier = [in_hbm(a) for a in earlier]
    return pl.pallas_call(
        functools.partial(weight_grad_kernel, groups, tile, j),
        out_shape=[pltpu.HBM((per * hid, 2 * D), f32), pltpu.HBM((per * hid, D), f32)],
        in_specs=[hbm()] * (len(args) + len(earlier)),
        out_specs=[hbm()] * 2,
        scratch_shapes=[
            wide,
            wide,
            narrow,
            narrow,
            narrow,
            pltpu.VMEM((hid // tile, tile, 2 * D), f32),
            pltpu.VMEM((hid // tile, tile, D), f32),
            pltpu.SemaphoreType.DMA((5 * groups,)),
            pltpu.SemaphoreType.DMA((hid // tile, 3)),
        ],
        input_output_aliases={len(args) + n: n for n in range(len(earlier))},
        compiler_params=pltpu.CompilerParams(vmem_limit_bytes=VMEM_LIMIT),
        cost_estimate=pl.CostEstimate(
            flops=6 * count * D * hid, bytes_accessed=14_000_000, transcendentals=0
        ),
        name="weight_grads_%d" % j,
    )(*args, *earlier)


def last_sum_kernel(*refs):
    terms, (qkv_ref, out_ref, router_ref, attn_ref, moe_ref) = refs[:-5], refs[-5:]
    columns = lambda low, high: total([ref[:, low:high] for ref in terms])
    qkv_ref[...] = columns(0, QKV)
    out_ref[...] = columns(QKV, QKV + D)
    small = columns(QKV + D, WCOLS)
    router_ref[...] = small[:, :EXPERTS]
    attn_ref[...] = small[0:1, 64:]
    moe_ref[...] = small[1:2, 64:]


def last_sum(terms):
    rows = terms[0].shape[0]
    shape = lambda *dims: jax.ShapeDtypeStruct(dims, f32)
    return pl.pallas_call(
        last_sum_kernel,
        out_shape=[shape(rows, QKV), shape(rows, D), shape(rows, EXPERTS), shape(1, 64), shape(1, 64)],
        in_specs=[vmem()] * len(terms),
        out_specs=[vmem()] * 5,
        compiler_params=pltpu.CompilerParams(vmem_limit_bytes=VMEM_LIMIT),
        cost_estimate=pl.CostEstimate(
            flops=rows * WCOLS * 4, bytes_accessed=rows * WCOLS * 12, transcendentals=0
        ),
        name="last_sum",
    )(*terms)


class Ring:
    def __init__(self):
        self.ahead, self.behind, self.core = [], [], [(i, i ^ 1) for i in range(16)]
        for p, chip in enumerate(PATH):
            for b in range(2):
                here = chip * 2 + b
                self.ahead.append((here, PATH[(p + 1) % 8] * 2 + b))
                self.behind.append((here, PATH[(p - 1) % 8] * 2 + b))
        index = lax.axis_index("fsdp")
        place = jnp.asarray(PLACE, jnp.int32)[index // 2]
        chips = jnp.asarray(PATH, jnp.int32)[(place + jnp.arange(8)) % 8]
        self.chips = chips
        self.order = jnp.stack([chips, jnp.broadcast_to(index % 2, (8,))]).astype(jnp.int32)

    def plus(self, a):
        return lax.ppermute(a, "fsdp", self.ahead)

    def minus(self, a):
        return lax.ppermute(a, "fsdp", self.behind)

    def swap(self, a):
        return lax.ppermute(a, "fsdp", self.core)

    def gather(self, own, work):
        half = own.shape[0] // 2
        group, terms, more, done = [own], [], [], None
        for r in range(5):
            if r < 3:
                coming = [self.plus(group[0]), self.minus(group[-1])]
            elif r == 3:
                coming = [self.plus(group[0][:half]), self.minus(group[1][half:])]
            if r:
                terms.append(self.meet(done, len(old)))
                more.append(done[2 * len(old) :])
            old = group
            done = work(r, group + [self.swap(a) for a in group])
            if r < 4:
                coming, done, terms = lax.optimization_barrier((coming, done, terms))
                group = coming
        terms.append(self.meet(done, 2))
        more.append(done[4:])
        return terms, more

    def meet(self, payload, count):
        return [(payload[n], self.swap(payload[count + n])) for n in range(count)]

    def gather_whole(self, own, beside):
        half = own.shape[0] // 2
        behind, ahead = [own], [own]
        for r in range(3):
            new = self.plus(behind[-1]), self.minus(ahead[-1])
            if r == 1:
                new, beside = lax.optimization_barrier((new, beside))
            else:
                new = lax.optimization_barrier(new)
            behind.append(new[0])
            ahead.append(new[1])
        far = [self.plus(behind[3][:half]), self.minus(ahead[3][half:])]
        both = lambda a: [a, self.swap(a)]
        out = [both(a) for a in ahead]
        out += [far + [self.swap(a) for a in far]]
        out += [both(a) for a in behind[:0:-1]]
        return sum(out, []), beside

    def scatter(self, terms, work=()):
        work, beside = list(work), ()
        out = [total(values).astype(bf16) for values in terms[4]]
        half = out[0].shape[0]
        for k in (3, 2, 1, 0):
            up, down = lax.optimization_barrier((out[0], out[1]))
            up, down = self.minus(up), self.plus(down)
            if len(work) > 0 and k < 3:
                up, down, beside = lax.optimization_barrier((up, down, work.pop(0)(beside)))
            if k == 0:
                return list(terms[0][0]) + [up, down], beside
            behind, ahead = terms[k]
            if k == 3:
                upper = lambda values: [a[:half] for a in values]
                lower = lambda values: [a[half:] for a in values]
                out = [
                    jnp.concatenate([total(upper(behind) + [up]), total(lower(behind))]),
                    jnp.concatenate([total(upper(ahead)), total(lower(ahead) + [down])]),
                ]
            else:
                out = [total(list(behind) + [up]), total(list(ahead) + [down])]
            out = [a.astype(bf16) for a in out]


def total(values):
    return functools.reduce(jnp.add, [a.astype(f32) for a in values])


def on_device(
    tokens,
    cotangent,
    routes,
    picture_start,
    w_qkv,
    w_out,
    w_router,
    gain_attn,
    gain_moe,
    w_gate_up,
    w_down,
):
    section = lax.axis_index("section")
    first_section = section == 0
    index = lax.axis_index("fsdp")
    devices = lax.axis_size("fsdp")
    seqs, length = tokens.shape[0], tokens.shape[1]
    rows = seqs * length
    w_in, w_down = w_gate_up[0], w_down[0]
    per = max(1, EXPERTS // devices)
    hid = w_down.shape[0] // per
    first_expert = index * EXPERTS // devices
    which = jnp.stack([first_expert, section]).astype(jnp.int32)
    ringed = devices == 16

    angles = np.arange(length)[:, None] * 10000.0 ** (-2.0 * (np.arange(LANES) % 32) / HEAD_SIZE)
    table = jnp.asarray(np.concatenate([np.cos(angles), np.sin(angles)], axis=1), f32)
    starts = picture_start[:, 0]

    named = jnp.any(routes[0][..., None] == jnp.arange(LANES, dtype=jnp.int32), axis=2)
    earlier = jnp.asarray(np.tril(np.ones((length, length)), -1), bf16)
    place = jnp.einsum("ts,mse->mte", earlier, named.astype(bf16), preferred_element_type=f32)
    pos = jnp.where(named, place, 255.0).reshape(rows, LANES)

    if ringed:
        ring = Ring()
        order = jnp.concatenate([ring.order, jnp.broadcast_to(section, (1, 8)).astype(jnp.int32)])
        gains = jnp.concatenate([gain_attn, gain_moe])
        side = jnp.concatenate([gains, jnp.zeros((62, 64), bf16)])
        small = jnp.concatenate([w_out[0], w_router[0], jnp.zeros((64, 32), bf16), side], axis=1)
        whole = jnp.concatenate([w_qkv[0], small], axis=1)
        w_all, (pos, order, starts) = ring.gather_whole(whole, (pos, order, starts))
    else:
        order = jnp.stack([jnp.arange(8), jnp.zeros((8,)), jnp.broadcast_to(section, (8,))])
        order = order.astype(jnp.int32)
        gather = lambda a: lax.all_gather(a[0], "fsdp", axis=0, tiled=True)
        big = jnp.concatenate([gather(w_qkv), gather(w_out)], axis=1).reshape(16, 64, QKV + D)
        gains = jnp.stack([gather(gain_attn), gather(gain_moe)]).reshape(2, 16, 64)
        side = jnp.concatenate(
            [jnp.moveaxis(gains, 0, 1), jnp.zeros((16, 62, 64), bf16)], axis=1
        )
        router = gather(w_router).reshape(16, 64, EXPERTS)
        small = jnp.concatenate([router, jnp.zeros((16, 64, 32), bf16), side], axis=2)
        w_all = jnp.concatenate([big, small], axis=2)
        far = [w_all[i, h : h + 32] for i in (8, 9) for h in (0, 32)]
        w_all = [w_all[i] for i in range(8)] + far + [w_all[i] for i in range(10, 16)]

    def gather_rows(own):
        every = lax.all_gather(own, "fsdp", axis=0, tiled=True)
        return every.reshape((-1, 8) + own.shape[1:])

    def phase(mode, own, g, x_groups=None):
        if ringed:
            seen = []

            def work(r, group):
                seen.append(group)
                x, beside = (group, g and g[r]) if x_groups is None else (x_groups[r], group)
                return expert_call(mode, which, x, beside, w_in, w_down, per)

            terms, saved = ring.gather(own, work)
            last = [functools.partial(weight_grads, saved, hid, per, j) for j in range(per)]
            sums, grads = ring.scatter(terms, last if mode == 2 else ())
            return total(sums), seen, grads

        every = gather_rows(own)
        x_all, g_all = (every, g) if x_groups is None else (x_groups, every)

        def step(grads, both):
            out = expert_call(mode, which, [both[0]], [both[1]] if mode else None, w_in, w_down, per)
            if mode == 2:
                grads = jax.tree.map(jnp.add, grads, list(weight_grads([out[1:]], hid, per, 0)))
            return grads, out[0]

        zero = [jnp.zeros((per * hid, 2 * D), f32), jnp.zeros((per * hid, D), f32)]
        grads, payload = lax.scan(
            step, zero if mode == 2 else None, (x_all, g_all if mode else x_all)
        )
        flat = payload.reshape((devices * seqs,) + payload.shape[2:])
        sums = lax.psum_scatter(flat, "fsdp", scatter_dimension=0, tiled=True).astype(f32)
        return sums, x_all, grads

    payload, resid = attn_forward(False, order, starts, table, pos, tokens, cotangent, w_all)
    mixture, g_second, _ = phase(0, payload, None)
    first_out = (resid + mixture).astype(bf16)
    passed = lax.ppermute(first_out, "section", [(0, 1), (1, 0)])
    payload, resid, *saved = attn_forward(True, order, starts, table, pos, tokens, passed, w_all)
    saved = [payload, resid] + saved
    sums_second, rows_all, _ = phase(1, payload, g_second)
    (grad_second,) = attn_backward(False, order, sums_second, cotangent, saved, table, w_all)

    g_third = lax.ppermute(grad_second, "section", [(0, 1), (1, 0)])
    sums_third, _, (grad_in, grad_down) = phase(2, g_third, None, rows_all)
    tiles = length * TILES

    def rows_of(array):
        array = array.reshape(seqs, length // TILE, TILES, TILE, LANES)
        return jnp.swapaxes(array, 2, 3).reshape(seqs, length, D)

    second_out = (resid.reshape(seqs, length, D) + rows_of(sums_third[:, :tiles])).astype(bf16)
    section_out = jnp.where(first_section, rows_of(first_out), second_out)
    sums = jnp.where(first_section, sums_third, sums_second)
    section_grad, *big = attn_backward(True, order, sums, g_third, saved, table, w_all)

    if ringed:
        pairs = [(a, ring.swap(b)) for a, b in zip(big[:5], big[5:])]
        part = lambda pair, low, high: [a[low:high] for a in pair]
        terms = [[pairs[0]]]
        terms += [[part(pair, 0, 64), part(pair, 64, 128)] for pair in pairs[1:4]]
        terms += [[part(pairs[4], 0, 32), part(pairs[4], 32, 64)]]
        summed, _ = ring.scatter(terms)
        g_qkv, g_out, g_router, g_gain_attn, g_gain_moe = last_sum(summed)
        g_gain_attn, g_gain_moe = g_gain_attn[0], g_gain_moe[0]
    else:
        chips = [(big[0], big[5])] + [(big[k][64:], big[5 + k][64:]) for k in (1, 2, 3)]
        chips += [(big[4], big[9])] + [(big[k][:64], big[5 + k][:64]) for k in (3, 2, 1)]
        whole = jnp.concatenate([a for chip in chips for a in chip]).astype(f32)
        sum_up = lambda a: lax.psum_scatter(a, "fsdp", scatter_dimension=0, tiled=True)
        small = whole[:, QKV + D :]
        g_qkv, g_out = sum_up(whole[:, :QKV]), sum_up(whole[:, QKV : QKV + D])
        g_router = sum_up(small[:, :EXPERTS])
        gains = small.reshape(16, 64, LANES)
        g_gain_attn = sum_up(gains[:, 0, 64:].reshape(D))
        g_gain_moe = sum_up(gains[:, 1, 64:].reshape(D))
    return (
        section_out[None],
        section_grad[None],
        g_qkv[None],
        g_out[None],
        g_router[None],
        g_gain_attn[None],
        g_gain_moe[None],
        grad_in[None],
        grad_down[None],
    )


def solution(mesh):
    return jax.shard_map(
        on_device,
        mesh=mesh,
        in_specs=(
            P(None, "fsdp", None),
            P(None, "fsdp", None),
            P("section", None, "fsdp", None),
            P(None, "fsdp"),
            P("section", "fsdp", None),
            P("section", "fsdp", None),
            P("section", "fsdp", None),
            P("section", "fsdp"),
            P("section", "fsdp"),
            P("section", "fsdp", None),
            P("section", "fsdp", None),
        ),
        out_specs=(
            P("section", None, "fsdp", None),
            P("section", None, "fsdp", None),
            P("section", "fsdp", None),
            P("section", "fsdp", None),
            P("section", "fsdp", None),
            P("section", "fsdp"),
            P("section", "fsdp"),
            P("section", "fsdp", None),
            P("section", "fsdp", None),
        ),
        check_vma=False,
    )
```

```python
import functools

import jax
import jax.numpy as jnp
import numpy as np
from jax import lax
from jax.experimental import pallas as pl
from jax.experimental.pallas import tpu as pltpu
from jax.sharding import PartitionSpec as P

D = 1024
QUERY_HEADS = 16
KEY_VALUE_HEADS = 8
HEAD_SIZE = 64
EXPERTS = 32
TOP = 8
PIC = 64
SLOTS = 32
LANES = 128
QKV = 2048
TILE = 16
TILES = D // LANES
WCOLS = QKV + D + LANES
epsilon = 1e-05
scale = HEAD_SIZE ** (-0.5)
f32 = jnp.float32
bf16 = jnp.bfloat16
VMEM_LIMIT = 20 * 1024 * 1024

PATH = (0, 2, 4, 6, 7, 5, 3, 1)
PLACE = tuple(PATH.index(c) for c in range(8))


def dot(a, b, ca, cb):
    return lax.dot_general(a, b, (((ca,), (cb,)), ((), ())), preferred_element_type=f32)


def nn(a, b):
    return dot(a, b, 1, 0)


def nt(a, b):
    return dot(a, b, 1, 1)


def tn(a, b):
    return dot(a, b, 0, 0)


def lanes_of(shape):
    return lax.broadcasted_iota(jnp.int32, shape, len(shape) - 1)


def rms(values):
    return lax.rsqrt(jnp.mean(values * values, axis=-1, keepdims=True) + epsilon)


def norm_back(values, inv, gain, grad):
    scaled = grad * gain
    inner = jnp.mean(scaled * values, axis=-1, keepdims=True)
    return inv * scaled - values * (inv * inv * inv * inner)


def turn(chunk, cosine, sine, back):
    first = (lanes_of(chunk.shape) & 63) < 32
    ahead = pltpu.roll(chunk, 96, 1)
    behind = pltpu.roll(chunk, 32, 1)
    if back:
        swapped = jnp.where(first, ahead, -behind)
    else:
        swapped = jnp.where(first, -ahead, behind)
    return chunk * cosine + swapped * sine


def halves(chunk):
    low = lanes_of(chunk.shape) < 64
    return jnp.concatenate([jnp.where(low, chunk, 0.0), jnp.where(low, 0.0, chunk)], axis=0)


def join(stacked):
    rows = stacked.shape[0] // 2
    low = lanes_of((rows, LANES)) < 64
    return jnp.where(low, stacked[:rows], stacked[rows:])


def doubled(chunk, odd):
    low = lanes_of(chunk.shape) < 64
    other = pltpu.roll(chunk, 64, 1)
    return jnp.where(low, other, chunk) if odd else jnp.where(low, chunk, other)


PARTS = ((0, QKV), (QKV, QKV + D), (QKV + D, WCOLS))


def wide(length):
    return length * TILES + length // 2


def plain(tiles):
    count = tiles.shape[0] // (TILE * TILES)
    tiles = tiles.reshape(count, TILES, TILE, LANES)
    columns = [tiles[:, c].reshape(count * TILE, LANES) for c in range(TILES)]
    return jnp.concatenate(columns, axis=1)


def store_tiles(ref, s, rows):
    for r in range(rows.shape[0] // TILE):
        for c in range(TILES):
            place = (r * TILES + c) * TILE
            block = rows[r * TILE : (r + 1) * TILE, c * LANES : (c + 1) * LANES]
            ref[s, place : place + TILE] = block.astype(ref.dtype)


def fold(columns):
    half = columns.shape[0] // 2
    low = lanes_of((half, LANES)) < 64
    return jnp.where(low, columns[:half], pltpu.roll(columns[half:], 64, 1))


def unfold(folded):
    return jnp.concatenate([folded, pltpu.roll(folded, 64, 1)], axis=0)


def load_weights(order, blocks, w_vmem, sems, turn_of):
    copies = {}
    for part in turn_of:
        columns = pl.ds(PARTS[part][0], PARTS[part][1] - PARTS[part][0])
        copies[part] = []
        for k in range(8):
            for b in range(2):
                target = w_vmem.at[order[0, k] * 2 + (order[1, 0] ^ b), :, columns]
                if k != 4:
                    pairs = [(blocks[(k if k < 4 else k + 1) * 2 + b], target)]
                else:
                    pairs = [(blocks[8 + 2 * b + h], target.at[pl.ds(32 * h, 32)]) for h in range(2)]
                for block, target in pairs:
                    sem = sems.at[part * 18 + len(copies[part])]
                    copies[part].append(pltpu.make_async_copy(block.at[:, columns], target, sem))
        for copy in copies[part]:
            copy.start()

    def wait(part):
        for copy in copies[part]:
            copy.wait()

    return wait


def gains_of(w_vmem):
    pieces = ([], [])
    for c in range(8):
        even = w_vmem[2 * c, 0:16, QKV + D :].astype(f32)
        odd = w_vmem[2 * c + 1, 0:16, QKV + D :].astype(f32)
        even = pltpu.roll(even, 64, 1)
        both = jnp.where(lanes_of(even.shape) < 64, even, odd)
        for i in range(2):
            pieces[i].append(both[i : i + 1])
    return jnp.concatenate(pieces[0], axis=1), jnp.concatenate(pieces[1], axis=1)


def attn_forward_kernel(save, order, table_hbm, pos_hbm, *refs):
    x_hbms, refs = refs[:2], refs[2:]
    if save:
        w_vmem, refs = refs[0], refs[1:]
    else:
        blocks, w_hbm, refs = refs[:18], refs[20], refs[18:20] + refs[21:]
    out_ref, resid_ref, refs = refs[0], refs[1], refs[2:]
    if save:
        x_ref, gate_ref, normed_ref, q_ref, k_ref, v_ref, probs_ref, mixed_ref = refs[:8]
        passed_ref, refs = refs[8], refs[9:]
    else:
        x_ref, cot_ref, mixed_ref = refs[:3]
        refs = refs[3:]
    if save:
        table_ref, pos_ref, side_sems = refs
    else:
        table_ref, pos_ref, side_sems, sems, w_vmem, resid_vmem = refs
    second = order[2, 0] != 0
    if save:
        loads = [
            pltpu.make_async_copy(x_hbms[0], x_ref, side_sems.at[0]),
            pltpu.make_async_copy(x_hbms[1], passed_ref, side_sems.at[3]),
        ]
        loads[0].start()
        loads[1].start()

    else:
        loads = [
            pltpu.make_async_copy(x_hbms[0], x_ref, side_sems.at[0]),
            pltpu.make_async_copy(x_hbms[1], cot_ref, side_sems.at[3]),
        ]
        loads[0].start()
        loads[1].start()
    load_table = pltpu.make_async_copy(table_hbm, table_ref, side_sems.at[1])
    load_table.start()
    wait = keep = lambda part: None
    if not save:
        kept = []

        def keep(part):
            columns = pl.ds(PARTS[part][0], PARTS[part][1] - PARTS[part][0])
            source, target = w_vmem.at[:, :, columns], w_hbm.at[:, :, columns]
            kept.append(pltpu.make_async_copy(source, target, side_sems.at[4 + part]))
            kept[-1].start()

        wait = load_weights(order, blocks, w_vmem, sems, (2, 0, 1))
    load_pos = pltpu.make_async_copy(pos_hbm, pos_ref, side_sems.at[2])
    load_pos.start()
    seqs, length = x_ref.shape[0], x_ref.shape[1]
    rows = seqs * length
    loads[0].wait()
    if save:
        loads[1].wait()

        @pl.when(second)
        def _():
            for s in range(seqs):
                x_ref[s] = plain(passed_ref[s])

    wait(2)
    keep(2)
    gain_attn, gain_moe = gains_of(w_vmem)
    x = x_ref[...].reshape(rows, D).astype(f32)
    normed = (x * rms(x) * gain_attn).astype(bf16)
    row_pos = lax.broadcasted_iota(jnp.int32, (length, length), 0)
    col_pos = lax.broadcasted_iota(jnp.int32, (length, length), 1)
    load_table.wait()
    cosine, sine = table_ref[:, :LANES], table_ref[:, LANES:]
    wait(0)
    keep(0)
    w_qkv = w_vmem[:, :, :QKV].reshape(D, QKV)
    qkv = nn(normed, w_qkv)
    wait(1)
    keep(1)
    heads = range(KEY_VALUE_HEADS)
    for s in range(seqs):
        top = slice(s * length, (s + 1) * length)
        start = order[3, s]
        both = (
            (row_pos >= start) & (row_pos < start + PIC) & (col_pos >= start) & (col_pos < start + PIC)
        )
        bias = jnp.where((col_pos <= row_pos) | both, 0.0, -1e30)
        bias = jnp.concatenate([bias, bias], axis=0)
        keys, values = [], []
        for c in range(4):
            key = turn(qkv[top, D + c * LANES : D + (c + 1) * LANES], cosine, sine, False)
            value = qkv[top, D + 512 + c * LANES : D + 512 + (c + 1) * LANES]
            if save:
                k_ref[top, c * LANES : (c + 1) * LANES] = key.astype(bf16)
                v_ref[top, c * LANES : (c + 1) * LANES] = value.astype(bf16)
            for odd in (False, True):
                keys.append(doubled(key, odd).astype(bf16))
                values.append(doubled(value, odd).astype(bf16))
        for j in heads:
            query = turn(qkv[top, j * LANES : (j + 1) * LANES], cosine, sine, False)
            if save:
                q_ref[top, j * LANES : (j + 1) * LANES] = query.astype(bf16)
            scores = nt(halves(query).astype(bf16), keys[j]) * scale + bias
            exponent = jnp.exp(scores - jnp.max(scores, axis=-1, keepdims=True))
            probs = exponent * (1.0 / jnp.sum(exponent, axis=-1, keepdims=True))
            if save:
                probs_ref[s * KEY_VALUE_HEADS + j] = probs
            mixed = join(nn(probs.astype(bf16), values[j]))
            mixed_ref[top, j * LANES : (j + 1) * LANES] = mixed.astype(bf16)
    w_out = w_vmem[:, :, QKV : QKV + D].reshape(D, D)
    resid = x + nn(mixed_ref[...], w_out)
    if not save:
        for s in range(seqs):
            store_tiles(resid_vmem, s, resid[s * length : (s + 1) * length])
        kept.append(pltpu.make_async_copy(resid_vmem, resid_ref, side_sems.at[7]))
        kept[-1].start()
    normed_moe = (resid * rms(resid) * gain_moe).astype(bf16)
    w_small = w_vmem[:, :, QKV + D :].reshape(D, LANES)
    logits = nn(normed_moe, w_small)
    load_pos.wait()
    pos = pos_ref[...]
    routed = pos < 64.0
    logits = jnp.where(routed, logits, -1e30)
    exponent = jnp.where(routed, jnp.exp(logits - jnp.max(logits, axis=-1, keepdims=True)), 0.0)
    gate = exponent * (1.0 / jnp.sum(exponent, axis=-1, keepdims=True))
    lane = lanes_of(gate.shape)
    columns = jnp.where(lane < 32, gate, pltpu.roll(pos, 32, 1))
    for s in range(seqs):
        top = slice(s * length, (s + 1) * length)
        store_tiles(out_ref, s, normed_moe[top])
        out_ref[s, length * TILES :] = fold(columns[top]).astype(bf16)
    if save:
        resid_ref[...] = resid
        gate_ref[...] = gate
        normed_ref[...] = normed
    else:
        loads[1].wait()

        @pl.when(second)
        def _():
            for s in range(seqs):
                store_tiles(out_ref, s, cot_ref[s])

        for copy in kept:
            copy.wait()


def vmem():
    return pl.BlockSpec(memory_space=pltpu.VMEM)


def smem():
    return pl.BlockSpec(memory_space=pltpu.SMEM)


def in_vmem(a):
    return pltpu.with_memory_space_constraint(a, pltpu.VMEM)


def hbm():
    return pl.BlockSpec(memory_space=pltpu.HBM)


def in_hbm(a):
    return pltpu.with_memory_space_constraint(a, pltpu.HBM)


def attn_forward(save, order, table, pos, x, other, w_all):
    seqs, length = x.shape[0], x.shape[1]
    rows = seqs * length
    shape = jax.ShapeDtypeStruct
    tiles = (seqs, length * TILES, LANES)
    outs = [shape((seqs, wide(length), LANES), bf16)]
    outs.append(shape((rows, D), f32) if save else pltpu.HBM(tiles, f32))
    probs = (seqs * KEY_VALUE_HEADS, 2 * length, length)
    scratch = []
    if save:
        outs += [
            shape((seqs, length, D), bf16),
            shape((rows, LANES), f32),
            shape((rows, D), bf16),
            shape((rows, D), bf16),
            shape((rows, 512), bf16),
            shape((rows, 512), bf16),
            shape(probs, f32),
            shape((rows, D), bf16),
        ]
        scratch = [pltpu.VMEM(tiles, bf16)]
        w_specs, w_args = [vmem()], [in_vmem(w_all)]
    else:
        outs.append(pltpu.HBM((16, 64, WCOLS), bf16))
        w_specs, w_args = [pl.BlockSpec(memory_space=pl.ANY)] * 18, w_all
        scratch = [pltpu.VMEM((seqs, length, D), bf16)] * 2
        scratch.append(pltpu.VMEM((rows, D), bf16))
    scratch += [
        pltpu.VMEM((length, 2 * LANES), f32),
        pltpu.VMEM((rows, LANES), f32),
        pltpu.SemaphoreType.DMA((8,)),
    ]
    if not save:
        scratch += [
            pltpu.SemaphoreType.DMA((54,)),
            pltpu.VMEM((16, 64, WCOLS), bf16),
            pltpu.VMEM(tiles, f32),
        ]
    return pl.pallas_call(
        functools.partial(attn_forward_kernel, save),
        out_shape=outs,
        in_specs=[smem()] + [hbm()] * 4 + w_specs,
        out_specs=[vmem()] * len(outs) if save else [vmem(), hbm(), hbm()],
        scratch_shapes=scratch,
        compiler_params=pltpu.CompilerParams(vmem_limit_bytes=VMEM_LIMIT),
        cost_estimate=pl.CostEstimate(
            flops=2 * rows * D * 3400, bytes_accessed=12_000_000, transcendentals=rows * 2048
        ),
        name="attn_forward",
    )(order, *map(in_hbm, [table, pos, x, other]), *w_args)


def attn_backward_kernel(
    with_grads,
    order,
    sum_ref,
    g_ref,
    x_ref,
    wide_ref,
    resid_ref,
    gate_ref,
    normed_ref,
    q_ref,
    k_ref,
    v_ref,
    probs_ref,
    mixed_ref,
    table_ref,
    *rest,
):
    w_vmem, rest = rest[0], rest[1:]
    loads = [None] * 3
    if with_grads:
        grad_ref, big_refs, rest = rest[0], rest[1:11], rest[11:]
        back_ref, gains_ref, w_scratch, k_scratch, v_scratch, sems = rest
        for part in (2, 1, 0):
            columns = pl.ds(PARTS[part][0], PARTS[part][1] - PARTS[part][0])
            loads[part] = pltpu.make_async_copy(
                w_vmem.at[:, :, columns], w_scratch.at[:, :, columns], sems.at[part]
            )
            loads[part].start()
        w_vmem = w_scratch
        k_load = pltpu.make_async_copy(k_ref, k_scratch, sems.at[3])
        v_load = pltpu.make_async_copy(v_ref, v_scratch, sems.at[4])
        k_load.start()
        v_load.start()
        k_ref, v_ref = k_scratch, v_scratch
        loads[2].wait()
    else:
        grad_ref, back_ref = rest
    seqs, length = x_ref.shape[0], x_ref.shape[1]
    rows = seqs * length
    gain_attn, gain_moe = gains_of(w_vmem)
    gate = gate_ref[...]
    tiles = length * TILES
    high_low = jnp.concatenate([unfold(sum_ref[s, tiles:]) for s in range(seqs)], axis=0)
    grad_gate = high_low + pltpu.roll(high_low, 96, 1)
    inner = jnp.sum(gate * grad_gate, axis=-1, keepdims=True)
    grad_logits = jnp.where(lanes_of(gate.shape) < 32, gate * (grad_gate - inner), 0.0)
    grad_logits = grad_logits.astype(bf16)
    w_small = w_vmem[:, :, QKV + D :].reshape(D, LANES)
    summed = jnp.concatenate([plain(sum_ref[s, :tiles]) for s in range(seqs)], axis=0)
    grad_normed_moe = summed + nt(grad_logits, w_small)
    resid = resid_ref[...]
    inv_moe = rms(resid)
    if with_grads:
        g = jnp.concatenate([plain(g_ref[s]) for s in range(seqs)], axis=0)
    else:
        g = g_ref[...].reshape(rows, D)
    grad_resid = g.astype(f32) + norm_back(resid, inv_moe, gain_moe, grad_normed_moe)
    grad_branch = grad_resid.astype(bf16)
    if with_grads:
        loads[1].wait()
    w_out = w_vmem[:, :, QKV : QKV + D].reshape(D, D)
    grad_mixed = nt(grad_branch, w_out)
    if with_grads:
        k_load.wait()
        v_load.wait()
    cosine, sine = table_ref[:, :LANES], table_ref[:, LANES:]
    low = lanes_of((length, LANES)) < 64
    for s in range(seqs):
        top = slice(s * length, (s + 1) * length)
        key_parts, value_parts = [], []
        for j in range(KEY_VALUE_HEADS):
            here = slice(j * LANES, (j + 1) * LANES)
            pair = slice((j // 2) * LANES, (j // 2 + 1) * LANES)
            query = halves(q_ref[top, here].astype(f32)).astype(bf16)
            key = doubled(k_ref[top, pair].astype(f32), j % 2 == 1).astype(bf16)
            value = doubled(v_ref[top, pair].astype(f32), j % 2 == 1).astype(bf16)
            grad_heads = halves(grad_mixed[top, here]).astype(bf16)
            probs = probs_ref[s * KEY_VALUE_HEADS + j]
            grad_probs = nt(grad_heads, value)
            grad_value = tn(probs.astype(bf16), grad_heads)
            grad_scores = probs * (grad_probs - jnp.sum(probs * grad_probs, axis=-1, keepdims=True))
            grad_scores = grad_scores.astype(bf16)
            grad_query = join(nn(grad_scores, key)) * scale
            grad_key = tn(grad_scores, query) * scale
            back_ref[top, here] = turn(grad_query, cosine, sine, True).astype(bf16)
            key_parts.append(grad_key + pltpu.roll(grad_key, 64, 1))
            value_parts.append(grad_value + pltpu.roll(grad_value, 64, 1))
        for c in range(4):
            grad_key = jnp.where(low, key_parts[2 * c], key_parts[2 * c + 1])
            grad_value = jnp.where(low, value_parts[2 * c], value_parts[2 * c + 1])
            back_ref[top, D + c * LANES : D + (c + 1) * LANES] = turn(
                grad_key, cosine, sine, True
            ).astype(bf16)
            back_ref[top, D + 512 + c * LANES : D + 512 + (c + 1) * LANES] = grad_value.astype(bf16)
    if with_grads:
        loads[0].wait()
    w_qkv = w_vmem[:, :, :QKV].reshape(D, QKV)
    grad_rows = back_ref[...]
    grad_normed = nt(grad_rows, w_qkv)
    x = x_ref[...].reshape(rows, D).astype(f32)
    inv_attn = rms(x)
    grad_in = grad_resid + norm_back(x, inv_attn, gain_attn, grad_normed)
    if with_grads:
        grad_ref[...] = grad_in.astype(bf16).reshape(seqs, length, D)
    else:
        for s in range(seqs):
            store_tiles(grad_ref, s, grad_in[s * length : (s + 1) * length])

        @pl.when(order[2, 0] == 0)
        def _():
            for s in range(seqs):
                store_tiles(grad_ref, s, g_ref[s])

    if with_grads:
        gains_ref[0:1] = jnp.sum(grad_normed * x * inv_attn, axis=0, keepdims=True)
        gains_ref[1:2] = jnp.sum(grad_normed_moe * resid * inv_moe, axis=0, keepdims=True)
        row = lax.broadcasted_iota(jnp.int32, (LANES, LANES), 0)
        lane = lanes_of((LANES, LANES))
        for k in range(8):
            columns = pl.ds(pl.multiple_of(order[0, k] * LANES, LANES), LANES)
            part_qkv = tn(normed_ref[:, columns], grad_rows)
            part_out = tn(mixed_ref[:, columns], grad_branch)
            places = [(r * TILES + order[0, k]) * TILE for r in range(length // TILE)]
            moe_rows = jnp.concatenate(
                [
                    wide_ref[s, pl.ds(pl.multiple_of(place, TILE), TILE)]
                    for s in range(seqs)
                    for place in places
                ],
                axis=0,
            )
            part_small = tn(moe_rows, grad_logits)
            for i in range(2):
                piece = gains_ref[i : i + 1, columns]
                turned = pltpu.roll(piece, 64, 1)
                part_small = part_small + jnp.where((row == i) & (lane >= 64), turned, 0.0)
                part_small = part_small + jnp.where((row == 64 + i) & (lane >= 64), piece, 0.0)
            n = min(k, 8 - k)
            place = slice(64, 128) if 0 < k < 4 else slice(0, 64)
            for part, columns in (
                (part_qkv, slice(0, QKV)),
                (part_out, slice(QKV, QKV + D)),
                (part_small, slice(QKV + D, WCOLS)),
            ):
                first_core = order[1, 0] == 0
                upper, lower = part[:64], part[64:]
                mine = jnp.where(first_core, upper, lower)
                big_refs[n][place, columns] = mine.astype(bf16)
                other = jnp.where(first_core, lower, upper)
                big_refs[5 + n][place, columns] = other.astype(bf16)


def attn_backward(with_grads, order, sums, g, saved, table, w_all):
    payload, resid, x, gate, normed, q, k, v, probs, mixed = saved
    late = hbm if with_grads else vmem
    seqs, length = x.shape[0], x.shape[1]
    rows = seqs * length
    shape = jax.ShapeDtypeStruct
    outs = [shape((seqs, length, D) if with_grads else (seqs, length * TILES, LANES), bf16)]
    scratch = [pltpu.VMEM((rows, QKV), bf16)]
    if with_grads:
        outs += [shape((n, WCOLS), bf16) for n in (64, 128, 128, 128, 64)] * 2
        scratch += [
            pltpu.VMEM((8, D), f32),
            pltpu.VMEM((16, 64, WCOLS), bf16),
            pltpu.VMEM((rows, 512), bf16),
            pltpu.VMEM((rows, 512), bf16),
            pltpu.SemaphoreType.DMA((5,)),
        ]
    return pl.pallas_call(
        functools.partial(attn_backward_kernel, with_grads),
        out_shape=outs,
        in_specs=[smem()] + [vmem()] * 8 + [late()] * 2 + [vmem()] * 3 + [late()],
        out_specs=[vmem()] * len(outs),
        scratch_shapes=scratch,
        compiler_params=pltpu.CompilerParams(vmem_limit_bytes=VMEM_LIMIT),
        cost_estimate=pl.CostEstimate(
            flops=4 * rows * D * 3400, bytes_accessed=20_000_000, transcendentals=0
        ),
        name="attn_backward",
    )(
        order,
        *(sums, g, x, payload, resid, gate, normed, q),
        *((in_hbm(k), in_hbm(v)) if with_grads else (k, v)),
        *(probs, mixed, table, (in_hbm if with_grads else in_vmem)(w_all)),
    )


def expert_kernel(mode, parts, which, *refs):
    refs = list(refs)
    take = lambda count: [refs.pop(0) for _ in range(count)]
    x_refs = take(parts)
    g_refs = take(parts) if mode else []
    w_in, w_down = take(2)
    out_refs = take(parts)
    saved_refs = take(5) if mode == 2 else []
    x_rows = take(1)[0]
    g_rows = take(1)[0] if mode else None
    if mode == 2:
        act_rows, gate_rows, up_rows, sems = take(4)
    hot_ref, scale_ref, result_ref = take(3)

    def send(n, j):
        source = (x_rows, g_rows, act_rows, gate_rows, up_rows)[n]
        return pltpu.make_async_copy(source.at[j], saved_refs[n].at[j], sems.at[n, j])

    per = x_rows.shape[0]
    hid = w_down.shape[0] // per
    first = which[0]
    spots = [(i, s) for i in range(parts) for s in range(x_refs[i].shape[0])]
    tiles = x_refs[0].shape[1] // 17 * 16
    length = tiles // TILES
    row8 = lax.broadcasted_iota(jnp.int32, (8, LANES), 0)
    lane8 = lanes_of((8, LANES))
    pick = jnp.where((lane8 == 32 + first + row8) & (row8 < per), 1.0, 0.0).astype(bf16)
    slot = lax.broadcasted_iota(jnp.int32, (SLOTS, length), 0).astype(f32)
    lane = lanes_of((SLOTS, LANES))
    for n, (i, s) in enumerate(spots):
        columns = unfold(x_refs[i][s, tiles:].astype(f32)).astype(bf16)
        places = nt(pick, columns)
        hot = jnp.concatenate(
            [jnp.where(places[j : j + 1] == slot, 1.0, 0.0) for j in range(per)], axis=0
        ).astype(bf16)
        hot_ref[n] = hot
        taken = nn(hot, jnp.concatenate([plain(x_refs[i][s, :tiles]), columns], axis=1))
        here = slice(n * SLOTS, (n + 1) * SLOTS)
        for j in range(per):
            block = taken[j * SLOTS : (j + 1) * SLOTS]
            x_rows[j, here] = block[:, :D].astype(bf16)
            gate = jnp.sum(jnp.where(lane == first + j, block[:, D:], 0.0), axis=-1, keepdims=True)
            scale_ref[j, here] = jnp.broadcast_to(gate, (SLOTS, LANES))
        if mode:
            taken = nn(hot, plain(g_refs[i][s, :tiles]))
            for j in range(per):
                g_rows[j, here] = taken[j * SLOTS : (j + 1) * SLOTS].astype(bf16)
    total = len(spots) * SLOTS
    lane = lanes_of((total, LANES))
    if mode == 2:
        for n in range(2):
            for j in range(per):
                send(n, j).start()
    for j in range(per):
        own_rows = slice(j * hid, (j + 1) * hid)
        rows = x_rows[j]
        gate_val = nt(rows, w_in[own_rows, :D])
        up_val = nt(rows, w_in[own_rows, D:])
        sig = jax.nn.sigmoid(gate_val)
        silu = gate_val * sig
        act = silu * up_val
        gate = scale_ref[j][:, 0:1]

        def forward():
            result_ref[j, :, :D] = (nn(act.astype(bf16), w_down[own_rows]) * gate).astype(bf16)

        def backward():
            inner = nt(g_rows[j], w_down[own_rows])
            grad_gw = jnp.sum(act.astype(bf16).astype(f32) * inner, axis=-1, keepdims=True)
            inner = inner * gate
            grad_gate = (inner * up_val * sig * (1.0 + gate_val * (1.0 - sig))).astype(bf16)
            grad_up = (inner * silu).astype(bf16)
            if mode == 2:
                act_rows[j] = (act * gate).astype(bf16)
                gate_rows[j] = grad_gate
                up_rows[j] = grad_up
                for n in range(2, 5):
                    send(n, j).start()
            grad_in = nn(grad_gate, w_in[own_rows, :D]) + nn(grad_up, w_in[own_rows, D:])
            high = grad_gw.astype(bf16).astype(f32)
            extra = jnp.where(
                lane == first + j, high, jnp.where(lane == 32 + first + j, grad_gw - high, 0.0)
            )
            result_ref[j, :, :D] = grad_in.astype(bf16)
            result_ref[j, :, D:] = extra.astype(bf16)

        if mode == 0:
            forward()
        else:
            backward()
            if mode == 2:

                @pl.when(which[1] != 0)
                def _():
                    forward()

    for n, (i, s) in enumerate(spots):
        here = slice(n * SLOTS, (n + 1) * SLOTS)
        block = jnp.concatenate([result_ref[j, here] for j in range(per)], axis=0)
        block = tn(hot_ref[n], block)
        store_tiles(out_refs[i], s, block[:, :D])
        if mode:
            out_refs[i][s, tiles:] = fold(block[:, D:]).astype(bf16)
    if mode == 2:
        for n in range(5):
            for j in range(per):
                send(n, j).wait()


def expert_call(mode, which, x_parts, g_parts, w_in, w_down, per):
    parts = len(x_parts)
    seqs = sum(x.shape[0] for x in x_parts)
    whole = x_parts[0].shape[1]
    length = whole // 17 * 16 // TILES
    hid = w_down.shape[0] // per
    total = seqs * SLOTS
    out_width = D + LANES if mode else D
    out_rows = whole if mode else length * TILES
    shape = jax.ShapeDtypeStruct
    outs = [shape((x.shape[0], out_rows, LANES), bf16) for x in x_parts]
    out_specs = [vmem()] * parts
    wide, narrow = (per, total, D), (per, total, hid)
    scratch = [pltpu.VMEM(wide, bf16)] * (2 if mode else 1)
    if mode == 2:
        saved = [wide, wide, narrow, narrow, narrow]
        outs += [pltpu.HBM(a, bf16) for a in saved]
        out_specs += [hbm()] * 5
        scratch += [pltpu.VMEM(narrow, bf16)] * 3 + [pltpu.SemaphoreType.DMA((5, per))]
    scratch += [
        pltpu.VMEM((seqs, per * SLOTS, length), bf16),
        pltpu.VMEM((per, total, LANES), f32),
        pltpu.VMEM((per, total, out_width), bf16),
    ]
    units = (3, 5, 5)[mode]
    g_args = list(g_parts) if mode else []

    def body(which, *refs):
        expert_kernel(mode, parts, which, *refs)

    return pl.pallas_call(
        body,
        out_shape=outs,
        in_specs=[smem()] + [vmem()] * (parts + len(g_args) + 2),
        out_specs=out_specs,
        scratch_shapes=scratch,
        compiler_params=pltpu.CompilerParams(vmem_limit_bytes=VMEM_LIMIT),
        cost_estimate=pl.CostEstimate(
            flops=2 * units * per * total * D * hid,
            bytes_accessed=6_000_000 + 4 * seqs * length * D,
            transcendentals=per * total * hid,
        ),
        name="experts_%d" % mode,
    )(which, *x_parts, *g_args, w_in, w_down)


def weight_grad_kernel(groups, tile, j, *refs):
    refs = list(refs)
    sets = [refs[5 * n : 5 * n + 5] for n in range(groups)]
    refs = refs[5 * groups + (2 if j else 0) :]
    in_ref, down_ref, rows = refs[0], refs[1], refs[2:7]
    in_tile, down_tile, load_sems, store_sems = refs[7:]
    hid = rows[2].shape[1]
    loads = []
    for n in (3, 0, 4, 2, 1):
        offset = 0
        for g in range(groups):
            count = sets[g][n].shape[1]
            loads.append(
                pltpu.make_async_copy(
                    sets[g][n].at[j],
                    rows[n].at[pl.ds(offset, count)],
                    load_sems.at[n * groups + g],
                )
            )
            offset += count
    for load in loads:
        load.start()
    tiles = hid // tile
    stores = []

    def store(source, target, sem):
        stores.append(pltpu.make_async_copy(source, target, sem))
        stores[-1].start()

    waited = 0
    for h in range(tiles):
        columns = slice(h * tile, (h + 1) * tile)
        where = pl.ds(j * hid + h * tile, tile)
        for n, upto, target in ((3, 2, 0), (4, 3, 1), (2, 5, 2)):
            for load in loads[waited : upto * groups]:
                load.wait()
            waited = max(waited, upto * groups)
            if target < 2:
                part = pl.ds(target * D, D)
                in_tile[h, :, part] = tn(rows[n][:, columns], rows[0][...])
                store(in_tile.at[h, :, part], in_ref.at[where, part], store_sems.at[h, target])
            else:
                down_tile[h] = tn(rows[n][:, columns], rows[1][...])
                store(down_tile.at[h], down_ref.at[where], store_sems.at[h, 2])
    for copy in stores:
        copy.wait()


def weight_grads(saved, hid, per, j, earlier=()):
    tile = min(hid, 256)
    groups = len(saved)
    args = [in_hbm(a) for group in saved for a in group]
    count = sum(group[0].shape[1] for group in saved)
    wide, narrow = pltpu.VMEM((count, D), bf16), pltpu.VMEM((count, hid), bf16)
    earlier = [in_hbm(a) for a in earlier]
    return pl.pallas_call(
        functools.partial(weight_grad_kernel, groups, tile, j),
        out_shape=[pltpu.HBM((per * hid, 2 * D), f32), pltpu.HBM((per * hid, D), f32)],
        in_specs=[hbm()] * (len(args) + len(earlier)),
        out_specs=[hbm()] * 2,
        scratch_shapes=[
            wide,
            wide,
            narrow,
            narrow,
            narrow,
            pltpu.VMEM((hid // tile, tile, 2 * D), f32),
            pltpu.VMEM((hid // tile, tile, D), f32),
            pltpu.SemaphoreType.DMA((5 * groups,)),
            pltpu.SemaphoreType.DMA((hid // tile, 3)),
        ],
        input_output_aliases={len(args) + n: n for n in range(len(earlier))},
        compiler_params=pltpu.CompilerParams(vmem_limit_bytes=VMEM_LIMIT),
        cost_estimate=pl.CostEstimate(
            flops=6 * count * D * hid, bytes_accessed=14_000_000, transcendentals=0
        ),
        name="weight_grads_%d" % j,
    )(*args, *earlier)


def last_sum_kernel(plans, *refs):
    refs, (qkv_ref, out_ref, router_ref, attn_ref, moe_ref) = refs[:-5], refs[-5:]
    for n, plan in enumerate(plans):
        columns = lambda first, last: total([refs[m][low:high, first:last] for m, low, high in plan])
        rows = plan[0][2] - plan[0][1]
        place = slice(n * rows, (n + 1) * rows)
        qkv_ref[place] = columns(0, QKV)
        out_ref[place] = columns(QKV, QKV + D)
        small = columns(QKV + D, WCOLS)
        router_ref[place] = small[:, :EXPERTS]
        if n == 0:
            attn_ref[...] = small[0:1, 64:]
            moe_ref[...] = small[1:2, 64:]


def last_sum(halves):
    args, plans = [], []
    for terms in halves:
        plans.append([(len(args) + n, low, high) for n, (a, low, high) in enumerate(terms)])
        args += [a for a, low, high in terms]
    rows = sum(terms[0][2] - terms[0][1] for terms in halves)
    shape = lambda *dims: jax.ShapeDtypeStruct(dims, f32)
    return pl.pallas_call(
        functools.partial(last_sum_kernel, plans),
        out_shape=[shape(rows, QKV), shape(rows, D), shape(rows, EXPERTS), shape(1, 64), shape(1, 64)],
        in_specs=[vmem()] * len(args),
        out_specs=[vmem()] * 5,
        compiler_params=pltpu.CompilerParams(vmem_limit_bytes=VMEM_LIMIT),
        cost_estimate=pl.CostEstimate(
            flops=rows * WCOLS * 4, bytes_accessed=rows * WCOLS * 12, transcendentals=0
        ),
        name="last_sum",
    )(*args)


def add_kernel(plans, *refs):
    outs = refs[len(refs) - len(plans) :]
    for out_ref, plan in zip(outs, plans):
        out_ref[...] = total([refs[n][low:high] for n, low, high in plan]).astype(out_ref.dtype)


def add_call(sums, dtype=bf16, stated=16_000_000):
    args, plans, shapes = [], [], []
    for terms in sums:
        plan = []
        for array, low, high in terms:
            found = [n for n, a in enumerate(args) if a is array]
            plan.append((found[0] if found else len(args), low, high))
            if not found:
                args.append(array)
        plans.append(plan)
        array, low, high = terms[0]
        shapes.append(jax.ShapeDtypeStruct((high - low,) + array.shape[1:], dtype))
    return pl.pallas_call(
        functools.partial(add_kernel, plans),
        out_shape=shapes,
        in_specs=[vmem()] * len(args),
        out_specs=[vmem()] * len(shapes),
        compiler_params=pltpu.CompilerParams(vmem_limit_bytes=VMEM_LIMIT),
        cost_estimate=pl.CostEstimate(flops=0, bytes_accessed=stated, transcendentals=0),
        name="add",
    )(*args)


class Ring:
    def __init__(self):
        self.ahead, self.behind, self.core = [], [], [(i, i ^ 1) for i in range(16)]
        for p, chip in enumerate(PATH):
            for b in range(2):
                here = chip * 2 + b
                self.ahead.append((here, PATH[(p + 1) % 8] * 2 + b))
                self.behind.append((here, PATH[(p - 1) % 8] * 2 + b))
        index = lax.axis_index("fsdp")
        place = jnp.asarray(PLACE, jnp.int32)[index // 2]
        chips = jnp.asarray(PATH, jnp.int32)[(place + jnp.arange(8)) % 8]
        self.chips = chips
        self.order = jnp.stack([chips, jnp.broadcast_to(index % 2, (8,))]).astype(jnp.int32)

    def plus(self, a):
        return lax.ppermute(a, "fsdp", self.ahead)

    def minus(self, a):
        return lax.ppermute(a, "fsdp", self.behind)

    def swap(self, a):
        return lax.ppermute(a, "fsdp", self.core)

    def gather(self, own, work):
        half = own.shape[0] // 2
        group, terms, more, done = [own], [], [], None
        for r in range(5):
            if r < 3:
                coming = [self.plus(group[0]), self.minus(group[-1])]
            elif r == 3:
                coming = [self.plus(group[0][:half]), self.minus(group[1][half:])]
            if r:
                terms.append(self.meet(done, len(old)))
                more.append(done[2 * len(old) :])
            old = group
            done = work(r, group + [self.swap(a) for a in group])
            if r < 4:
                coming, done, terms = lax.optimization_barrier((coming, done, terms))
                group = coming
        terms.append(self.meet(done, 2))
        more.append(done[4:])
        return terms, more

    def meet(self, payload, count):
        return [(payload[n], self.swap(payload[count + n])) for n in range(count)]

    def gather_whole(self, own, beside):
        half = own.shape[0] // 2
        behind, ahead = [own], [own]
        for r in range(3):
            new = self.plus(behind[-1]), self.minus(ahead[-1])
            if r == 1:
                new, beside = lax.optimization_barrier((new, beside))
            else:
                new = lax.optimization_barrier(new)
            behind.append(new[0])
            ahead.append(new[1])
        far = [self.plus(behind[3][:half]), self.minus(ahead[3][half:])]
        both = lambda a: [a, self.swap(a)]
        out = [both(a) for a in ahead]
        out += [far + [self.swap(a) for a in far]]
        out += [both(a) for a in behind[:0:-1]]
        return sum(out, []), beside

    def scatter_halves(self, terms):
        half = terms[4][0][0].shape[0]
        came = [[[], []], [[], []]]
        last = ()
        for r in range(4):
            for c in range(2):
                low, high = c * half, (c + 1) * half
                whole = lambda values: [(a, 0, half) for a in values]
                part = lambda values: [(a, low, high) for a in values]
                came[c], last = lax.optimization_barrier((came[c], last))
                if r == 0:
                    last = add_call([whole(terms[4][c])])
                else:
                    behind, ahead = terms[4 - r]
                    last = add_call(
                        [part(behind) + whole(came[c][0]), part(ahead) + whole(came[c][1])]
                    )
                if r:
                    came[c] = [[self.minus(last[0])], [self.plus(last[1])]]
                else:
                    came[c] = [[], [self.plus(last[0])]] if c else [[self.minus(last[0])], []]
        return [
            [(a, c * half, (c + 1) * half) for a in terms[0][0]] + [(a, 0, half) for a in sum(came[c], [])]
            for c in range(2)
        ]

    def scatter(self, terms, work=()):
        work, beside = list(work), ()
        out = [total(values).astype(bf16) for values in terms[4]]
        half = out[0].shape[0]
        for k in (3, 2, 1, 0):
            up, down = lax.optimization_barrier((out[0], out[1]))
            up, down = self.minus(up), self.plus(down)
            if len(work) > 0 and k < 3:
                up, down, beside = lax.optimization_barrier((up, down, work.pop(0)(beside)))
            if k == 0:
                return list(terms[0][0]) + [up, down], beside
            behind, ahead = terms[k]
            if k == 3:
                upper = lambda values: [a[:half] for a in values]
                lower = lambda values: [a[half:] for a in values]
                out = [
                    jnp.concatenate([total(upper(behind) + [up]), total(lower(behind))]),
                    jnp.concatenate([total(upper(ahead)), total(lower(ahead) + [down])]),
                ]
            else:
                out = [total(list(behind) + [up]), total(list(ahead) + [down])]
            out = [a.astype(bf16) for a in out]


def total(values):
    return functools.reduce(jnp.add, [a.astype(f32) for a in values])


def on_device(
    tokens,
    cotangent,
    routes,
    picture_start,
    w_qkv,
    w_out,
    w_router,
    gain_attn,
    gain_moe,
    w_gate_up,
    w_down,
):
    section = lax.axis_index("section")
    first_section = section == 0
    index = lax.axis_index("fsdp")
    devices = lax.axis_size("fsdp")
    seqs, length = tokens.shape[0], tokens.shape[1]
    rows = seqs * length
    w_in, w_down = w_gate_up[0], w_down[0]
    per = max(1, EXPERTS // devices)
    hid = w_down.shape[0] // per
    first_expert = index * EXPERTS // devices
    which = jnp.stack([first_expert, section]).astype(jnp.int32)
    ringed = devices == 16

    angles = np.arange(length)[:, None] * 10000.0 ** (-2.0 * (np.arange(LANES) % 32) / HEAD_SIZE)
    table = jnp.asarray(np.concatenate([np.cos(angles), np.sin(angles)], axis=1), f32)
    starts = jnp.pad(picture_start[:, 0], (0, 6))[None]

    named = jnp.any(routes[0][..., None] == jnp.arange(LANES, dtype=jnp.int32), axis=2)
    earlier = jnp.asarray(np.tril(np.ones((length, length)), -1), bf16)
    place = jnp.einsum("ts,mse->mte", earlier, named.astype(bf16), preferred_element_type=f32)
    pos = jnp.where(named, place, 255.0).reshape(rows, LANES)

    if ringed:
        ring = Ring()
        order = jnp.concatenate([ring.order, jnp.broadcast_to(section, (1, 8)).astype(jnp.int32), starts])
        gains = jnp.concatenate([gain_attn, gain_moe])
        side = jnp.concatenate([gains, jnp.zeros((62, 64), bf16)])
        whole = jnp.concatenate([w_qkv[0], w_out[0], w_router[0], jnp.zeros((64, 32), bf16), side], axis=1)
        w_all, (pos, order) = ring.gather_whole(whole, (pos, order))
    else:
        order = jnp.stack([jnp.arange(8), jnp.zeros((8,)), jnp.broadcast_to(section, (8,))])
        order = jnp.concatenate([order.astype(jnp.int32), starts])
        gather = lambda a: lax.all_gather(a[0], "fsdp", axis=0, tiled=True)
        big = jnp.concatenate([gather(w_qkv), gather(w_out)], axis=1).reshape(16, 64, QKV + D)
        gains = jnp.stack([gather(gain_attn), gather(gain_moe)]).reshape(2, 16, 64)
        side = jnp.concatenate(
            [jnp.moveaxis(gains, 0, 1), jnp.zeros((16, 62, 64), bf16)], axis=1
        )
        router = gather(w_router).reshape(16, 64, EXPERTS)
        small = jnp.concatenate([router, jnp.zeros((16, 64, 32), bf16), side], axis=2)
        w_all = jnp.concatenate([big, small], axis=2)
        far = [w_all[i, h : h + 32] for i in (8, 9) for h in (0, 32)]
        w_all = [w_all[i] for i in range(8)] + far + [w_all[i] for i in range(10, 16)]

    def gather_rows(own):
        every = lax.all_gather(own, "fsdp", axis=0, tiled=True)
        return every.reshape((-1, 8) + own.shape[1:])

    def phase(mode, own, g, x_groups=None):
        if ringed:
            seen = []

            def work(r, group):
                seen.append(group)
                x, beside = (group, g and g[r]) if x_groups is None else (x_groups[r], group)
                return expert_call(mode, which, x, beside, w_in, w_down, per)

            terms, saved = ring.gather(own, work)
            last = [functools.partial(weight_grads, saved, hid, per, j) for j in range(per)]
            if mode == 2:
                sums, grads = ring.scatter(terms, last)
                return total(sums), seen, grads
            sums = ring.scatter_halves(terms)
            sums = [total([a[low:high] for a, low, high in half]) for half in sums]
            return jnp.concatenate(sums), seen, ()

        every = gather_rows(own)
        x_all, g_all = (every, g) if x_groups is None else (x_groups, every)

        def step(grads, both):
            out = expert_call(mode, which, [both[0]], [both[1]] if mode else None, w_in, w_down, per)
            if mode == 2:
                grads = jax.tree.map(jnp.add, grads, list(weight_grads([out[1:]], hid, per, 0)))
            return grads, out[0]

        zero = [jnp.zeros((per * hid, 2 * D), f32), jnp.zeros((per * hid, D), f32)]
        grads, payload = lax.scan(
            step, zero if mode == 2 else None, (x_all, g_all if mode else x_all)
        )
        flat = payload.reshape((devices * seqs,) + payload.shape[2:])
        sums = lax.psum_scatter(flat, "fsdp", scatter_dimension=0, tiled=True).astype(f32)
        return sums, x_all, grads

    payload, resid, w_all = attn_forward(False, order, table, pos, tokens, cotangent, w_all)
    mixture, g_second, _ = phase(0, payload, None)
    first_out = (resid + mixture).astype(bf16)
    passed = lax.ppermute(first_out, "section", [(0, 1), (1, 0)])
    payload, resid, *saved = attn_forward(True, order, table, pos, tokens, passed, w_all)
    saved = [payload, resid] + saved
    sums_second, rows_all, _ = phase(1, payload, g_second)
    (grad_second,) = attn_backward(False, order, sums_second, cotangent, saved, table, w_all)

    g_third = lax.ppermute(grad_second, "section", [(0, 1), (1, 0)])
    sums_third, _, (grad_in, grad_down) = phase(2, g_third, None, rows_all)
    tiles = length * TILES

    def rows_of(array):
        array = array.reshape(seqs, length // TILE, TILES, TILE, LANES)
        return jnp.swapaxes(array, 2, 3).reshape(seqs, length, D)

    second_out = (resid.reshape(seqs, length, D) + rows_of(sums_third[:, :tiles])).astype(bf16)
    section_out = jnp.where(first_section, rows_of(first_out), second_out)
    sums = jnp.where(first_section, sums_third, sums_second)
    section_grad, *big = attn_backward(True, order, sums, g_third, saved, table, w_all)

    if ringed:
        pairs, came = [None] * 5, ()
        for n in (4, 3, 2, 1, 0):
            going, came = lax.optimization_barrier((big[5 + n], came))
            came = ring.swap(going)
            pairs[n] = (big[n], came)
        part = lambda pair, low, high: [a[low:high] for a in pair]
        terms = [[pairs[0]]]
        terms += [[part(pair, 0, 64), part(pair, 64, 128)] for pair in pairs[1:4]]
        terms += [[part(pairs[4], 0, 32), part(pairs[4], 32, 64)]]
        g_qkv, g_out, g_router, g_gain_attn, g_gain_moe = last_sum(ring.scatter_halves(terms))
        g_gain_attn, g_gain_moe = g_gain_attn[0], g_gain_moe[0]
    else:
        chips = [(big[0], big[5])] + [(big[k][64:], big[5 + k][64:]) for k in (1, 2, 3)]
        chips += [(big[4], big[9])] + [(big[k][:64], big[5 + k][:64]) for k in (3, 2, 1)]
        whole = jnp.concatenate([a for chip in chips for a in chip]).astype(f32)
        sum_up = lambda a: lax.psum_scatter(a, "fsdp", scatter_dimension=0, tiled=True)
        small = whole[:, QKV + D :]
        g_qkv, g_out = sum_up(whole[:, :QKV]), sum_up(whole[:, QKV : QKV + D])
        g_router = sum_up(small[:, :EXPERTS])
        gains = small.reshape(16, 64, LANES)
        g_gain_attn = sum_up(gains[:, 0, 64:].reshape(D))
        g_gain_moe = sum_up(gains[:, 1, 64:].reshape(D))
    return (
        section_out[None],
        section_grad[None],
        g_qkv[None],
        g_out[None],
        g_router[None],
        g_gain_attn[None],
        g_gain_moe[None],
        grad_in[None],
        grad_down[None],
    )


def solution(mesh):
    return jax.shard_map(
        on_device,
        mesh=mesh,
        in_specs=(
            P(None, "fsdp", None),
            P(None, "fsdp", None),
            P("section", None, "fsdp", None),
            P(None, "fsdp"),
            P("section", "fsdp", None),
            P("section", "fsdp", None),
            P("section", "fsdp", None),
            P("section", "fsdp"),
            P("section", "fsdp"),
            P("section", "fsdp", None),
            P("section", "fsdp", None),
        ),
        out_specs=(
            P("section", None, "fsdp", None),
            P("section", None, "fsdp", None),
            P("section", "fsdp", None),
            P("section", "fsdp", None),
            P("section", "fsdp", None),
            P("section", "fsdp"),
            P("section", "fsdp"),
            P("section", "fsdp", None),
            P("section", "fsdp", None),
        ),
        check_vma=False,
    )
```

```python
import functools

import jax
import jax.numpy as jnp
import numpy as np
from jax import lax
from jax.experimental import pallas as pl
from jax.experimental.pallas import tpu as pltpu
from jax.sharding import PartitionSpec as P

D = 1024
QUERY_HEADS = 16
KEY_VALUE_HEADS = 8
HEAD_SIZE = 64
EXPERTS = 32
TOP = 8
PIC = 64
SLOTS = 32
LANES = 128
QKV = 2048
TILE = 16
TILES = D // LANES
WCOLS = QKV + D + LANES
epsilon = 1e-05
scale = HEAD_SIZE ** (-0.5)
f32 = jnp.float32
bf16 = jnp.bfloat16
VMEM_LIMIT = 20 * 1024 * 1024

PATH = (0, 2, 4, 6, 7, 5, 3, 1)
PLACE = tuple(PATH.index(c) for c in range(8))


def dot(a, b, ca, cb):
    return lax.dot_general(a, b, (((ca,), (cb,)), ((), ())), preferred_element_type=f32)


def nn(a, b):
    return dot(a, b, 1, 0)


def nt(a, b):
    return dot(a, b, 1, 1)


def tn(a, b):
    return dot(a, b, 0, 0)


def lanes_of(shape):
    return lax.broadcasted_iota(jnp.int32, shape, len(shape) - 1)


def rms(values):
    return lax.rsqrt(jnp.mean(values * values, axis=-1, keepdims=True) + epsilon)


def norm_back(values, inv, gain, grad):
    scaled = grad * gain
    inner = jnp.mean(scaled * values, axis=-1, keepdims=True)
    return inv * scaled - values * (inv * inv * inv * inner)


def turn(chunk, cosine, sine, back):
    first = (lanes_of(chunk.shape) & 63) < 32
    ahead = pltpu.roll(chunk, 96, 1)
    behind = pltpu.roll(chunk, 32, 1)
    if back:
        swapped = jnp.where(first, ahead, -behind)
    else:
        swapped = jnp.where(first, -ahead, behind)
    return chunk * cosine + swapped * sine


def halves(chunk):
    low = lanes_of(chunk.shape) < 64
    return jnp.concatenate([jnp.where(low, chunk, 0.0), jnp.where(low, 0.0, chunk)], axis=0)


def join(stacked):
    rows = stacked.shape[0] // 2
    low = lanes_of((rows, LANES)) < 64
    return jnp.where(low, stacked[:rows], stacked[rows:])


def doubled(chunk, odd):
    low = lanes_of(chunk.shape) < 64
    other = pltpu.roll(chunk, 64, 1)
    return jnp.where(low, other, chunk) if odd else jnp.where(low, chunk, other)


PARTS = ((0, QKV), (QKV, QKV + D), (QKV + D, WCOLS))


def wide(length):
    return length * TILES + length // 2


def plain(tiles):
    count = tiles.shape[0] // (TILE * TILES)
    tiles = tiles.reshape(count, TILES, TILE, LANES)
    columns = [tiles[:, c].reshape(count * TILE, LANES) for c in range(TILES)]
    return jnp.concatenate(columns, axis=1)


def store_tiles(ref, s, rows):
    for r in range(rows.shape[0] // TILE):
        for c in range(TILES):
            place = (r * TILES + c) * TILE
            block = rows[r * TILE : (r + 1) * TILE, c * LANES : (c + 1) * LANES]
            ref[s, place : place + TILE] = block.astype(ref.dtype)


def fold(columns):
    half = columns.shape[0] // 2
    low = lanes_of((half, LANES)) < 64
    return jnp.where(low, columns[:half], pltpu.roll(columns[half:], 64, 1))


def unfold(folded):
    return jnp.concatenate([folded, pltpu.roll(folded, 64, 1)], axis=0)


def load_weights(order, blocks, w_vmem, sems, turn_of):
    copies = {}
    for part in turn_of:
        columns = pl.ds(PARTS[part][0], PARTS[part][1] - PARTS[part][0])
        copies[part] = []
        for k in range(8):
            for b in range(2):
                target = w_vmem.at[order[0, k] * 2 + (order[1, 0] ^ b), :, columns]
                if k != 4:
                    pairs = [(blocks[(k if k < 4 else k + 1) * 2 + b], target)]
                else:
                    pairs = [(blocks[8 + 2 * b + h], target.at[pl.ds(32 * h, 32)]) for h in range(2)]
                for block, target in pairs:
                    sem = sems.at[part * 18 + len(copies[part])]
                    copies[part].append(pltpu.make_async_copy(block.at[:, columns], target, sem))
        for copy in copies[part]:
            copy.start()

    def wait(part):
        for copy in copies[part]:
            copy.wait()

    return wait


def gains_of(w_vmem):
    pieces = ([], [])
    for c in range(8):
        even = w_vmem[2 * c, 0:16, QKV + D :].astype(f32)
        odd = w_vmem[2 * c + 1, 0:16, QKV + D :].astype(f32)
        even = pltpu.roll(even, 64, 1)
        both = jnp.where(lanes_of(even.shape) < 64, even, odd)
        for i in range(2):
            pieces[i].append(both[i : i + 1])
    return jnp.concatenate(pieces[0], axis=1), jnp.concatenate(pieces[1], axis=1)


def attn_forward_kernel(save, order, table_hbm, pos_hbm, *refs):
    x_hbms, refs = refs[:2], refs[2:]
    if save:
        w_vmem, refs = refs[0], refs[1:]
    else:
        blocks, w_hbm, refs = refs[:18], refs[20], refs[18:20] + refs[21:]
    out_ref, resid_ref, refs = refs[0], refs[1], refs[2:]
    if save:
        x_ref, gate_ref, normed_ref, q_ref, k_ref, v_ref, probs_ref, mixed_ref = refs[:8]
        passed_ref, refs = refs[8], refs[9:]
    else:
        x_ref, cot_ref, mixed_ref = refs[:3]
        refs = refs[3:]
    if save:
        table_ref, pos_ref, side_sems = refs
    else:
        table_ref, pos_ref, side_sems, sems, w_vmem, resid_vmem = refs
    second = order[2, 0] != 0
    if save:
        loads = [
            pltpu.make_async_copy(x_hbms[0], x_ref, side_sems.at[0]),
            pltpu.make_async_copy(x_hbms[1], passed_ref, side_sems.at[3]),
        ]
        loads[0].start()
        loads[1].start()

    else:
        loads = [
            pltpu.make_async_copy(x_hbms[0], x_ref, side_sems.at[0]),
            pltpu.make_async_copy(x_hbms[1], cot_ref, side_sems.at[3]),
        ]
        loads[0].start()
        loads[1].start()
    load_table = pltpu.make_async_copy(table_hbm, table_ref, side_sems.at[1])
    load_table.start()
    wait = keep = lambda part: None
    if not save:
        kept = []

        def keep(part):
            columns = pl.ds(PARTS[part][0], PARTS[part][1] - PARTS[part][0])
            source, target = w_vmem.at[:, :, columns], w_hbm.at[:, :, columns]
            kept.append(pltpu.make_async_copy(source, target, side_sems.at[4 + part]))
            kept[-1].start()

        wait = load_weights(order, blocks, w_vmem, sems, (2, 0, 1))
    load_pos = pltpu.make_async_copy(pos_hbm, pos_ref, side_sems.at[2])
    load_pos.start()
    seqs, length = x_ref.shape[0], x_ref.shape[1]
    rows = seqs * length
    loads[0].wait()
    if save:
        loads[1].wait()

        @pl.when(second)
        def _():
            for s in range(seqs):
                x_ref[s] = plain(passed_ref[s])

    wait(2)
    keep(2)
    gain_attn, gain_moe = gains_of(w_vmem)
    x = x_ref[...].reshape(rows, D).astype(f32)
    normed = (x * rms(x) * gain_attn).astype(bf16)
    row_pos = lax.broadcasted_iota(jnp.int32, (length, length), 0)
    col_pos = lax.broadcasted_iota(jnp.int32, (length, length), 1)
    load_table.wait()
    cosine, sine = table_ref[:, :LANES], table_ref[:, LANES:]
    wait(0)
    keep(0)
    w_qkv = w_vmem[:, :, :QKV].reshape(D, QKV)
    qkv = nn(normed, w_qkv)
    wait(1)
    keep(1)
    heads = range(KEY_VALUE_HEADS)
    for s in range(seqs):
        top = slice(s * length, (s + 1) * length)
        start = order[3, s]
        both = (
            (row_pos >= start) & (row_pos < start + PIC) & (col_pos >= start) & (col_pos < start + PIC)
        )
        bias = jnp.where((col_pos <= row_pos) | both, 0.0, -1e30)
        bias = jnp.concatenate([bias, bias], axis=0)
        keys, values = [], []
        for c in range(4):
            key = turn(qkv[top, D + c * LANES : D + (c + 1) * LANES], cosine, sine, False)
            value = qkv[top, D + 512 + c * LANES : D + 512 + (c + 1) * LANES]
            if save:
                k_ref[top, c * LANES : (c + 1) * LANES] = key.astype(bf16)
                v_ref[top, c * LANES : (c + 1) * LANES] = value.astype(bf16)
            for odd in (False, True):
                keys.append(doubled(key, odd).astype(bf16))
                values.append(doubled(value, odd).astype(bf16))
        for j in heads:
            query = turn(qkv[top, j * LANES : (j + 1) * LANES], cosine, sine, False)
            if save:
                q_ref[top, j * LANES : (j + 1) * LANES] = query.astype(bf16)
            scores = nt(halves(query).astype(bf16), keys[j]) * scale + bias
            exponent = jnp.exp(scores - jnp.max(scores, axis=-1, keepdims=True))
            probs = exponent * (1.0 / jnp.sum(exponent, axis=-1, keepdims=True))
            if save:
                probs_ref[s * KEY_VALUE_HEADS + j] = probs
            mixed = join(nn(probs.astype(bf16), values[j]))
            mixed_ref[top, j * LANES : (j + 1) * LANES] = mixed.astype(bf16)
    w_out = w_vmem[:, :, QKV : QKV + D].reshape(D, D)
    resid = x + nn(mixed_ref[...], w_out)
    if not save:
        for s in range(seqs):
            store_tiles(resid_vmem, s, resid[s * length : (s + 1) * length])
        kept.append(pltpu.make_async_copy(resid_vmem, resid_ref, side_sems.at[7]))
        kept[-1].start()
    normed_moe = (resid * rms(resid) * gain_moe).astype(bf16)
    w_small = w_vmem[:, :, QKV + D :].reshape(D, LANES)
    logits = nn(normed_moe, w_small)
    load_pos.wait()
    pos = pos_ref[...]
    routed = pos < 64.0
    logits = jnp.where(routed, logits, -1e30)
    exponent = jnp.where(routed, jnp.exp(logits - jnp.max(logits, axis=-1, keepdims=True)), 0.0)
    gate = exponent * (1.0 / jnp.sum(exponent, axis=-1, keepdims=True))
    lane = lanes_of(gate.shape)
    columns = jnp.where(lane < 32, gate, pltpu.roll(pos, 32, 1))
    for s in range(seqs):
        top = slice(s * length, (s + 1) * length)
        store_tiles(out_ref, s, normed_moe[top])
        out_ref[s, length * TILES :] = fold(columns[top]).astype(bf16)
    if save:
        resid_ref[...] = resid
        gate_ref[...] = gate
        normed_ref[...] = normed
    else:
        loads[1].wait()

        @pl.when(second)
        def _():
            for s in range(seqs):
                store_tiles(out_ref, s, cot_ref[s])

        for copy in kept:
            copy.wait()


def vmem():
    return pl.BlockSpec(memory_space=pltpu.VMEM)


def smem():
    return pl.BlockSpec(memory_space=pltpu.SMEM)


def in_vmem(a):
    return pltpu.with_memory_space_constraint(a, pltpu.VMEM)


def hbm():
    return pl.BlockSpec(memory_space=pltpu.HBM)


def in_hbm(a):
    return pltpu.with_memory_space_constraint(a, pltpu.HBM)


def attn_forward(save, order, table, pos, x, other, w_all):
    seqs, length = x.shape[0], x.shape[1]
    rows = seqs * length
    shape = jax.ShapeDtypeStruct
    tiles = (seqs, length * TILES, LANES)
    outs = [shape((seqs, wide(length), LANES), bf16)]
    outs.append(shape((rows, D), f32) if save else pltpu.HBM(tiles, f32))
    probs = (seqs * KEY_VALUE_HEADS, 2 * length, length)
    scratch = []
    if save:
        outs += [
            shape((seqs, length, D), bf16),
            shape((rows, LANES), f32),
            shape((rows, D), bf16),
            shape((rows, D), bf16),
            shape((rows, 512), bf16),
            shape((rows, 512), bf16),
            shape(probs, f32),
            shape((rows, D), bf16),
        ]
        scratch = [pltpu.VMEM(tiles, bf16)]
        w_specs, w_args = [vmem()], [in_vmem(w_all)]
    else:
        outs.append(pltpu.HBM((16, 64, WCOLS), bf16))
        w_specs, w_args = [pl.BlockSpec(memory_space=pl.ANY)] * 18, w_all
        scratch = [pltpu.VMEM((seqs, length, D), bf16)] * 2
        scratch.append(pltpu.VMEM((rows, D), bf16))
    scratch += [
        pltpu.VMEM((length, 2 * LANES), f32),
        pltpu.VMEM((rows, LANES), f32),
        pltpu.SemaphoreType.DMA((8,)),
    ]
    if not save:
        scratch += [
            pltpu.SemaphoreType.DMA((54,)),
            pltpu.VMEM((16, 64, WCOLS), bf16),
            pltpu.VMEM(tiles, f32),
        ]
    return pl.pallas_call(
        functools.partial(attn_forward_kernel, save),
        out_shape=outs,
        in_specs=[smem()] + [hbm()] * 4 + w_specs,
        out_specs=[vmem()] * len(outs) if save else [vmem(), hbm(), hbm()],
        scratch_shapes=scratch,
        compiler_params=pltpu.CompilerParams(vmem_limit_bytes=VMEM_LIMIT),
        cost_estimate=pl.CostEstimate(
            flops=2 * rows * D * 3400, bytes_accessed=12_000_000, transcendentals=rows * 2048
        ),
        name="attn_forward",
    )(order, *map(in_hbm, [table, pos, x, other]), *w_args)


def attn_backward_kernel(
    with_grads,
    order,
    sum_ref,
    g_ref,
    x_ref,
    wide_ref,
    resid_ref,
    gate_ref,
    normed_ref,
    q_ref,
    k_ref,
    v_ref,
    probs_ref,
    mixed_ref,
    table_ref,
    *rest,
):
    w_vmem, rest = rest[0], rest[1:]
    loads = [None] * 3
    if with_grads:
        second_ref, first_ref, grad_ref, section_ref, rest = rest[0], rest[1], rest[2], rest[3], rest[4:]
        big_refs, rest = rest[:10], rest[10:]
        back_ref, gains_ref, w_scratch, k_scratch, v_scratch, sems = rest
        for part in (2, 1, 0):
            columns = pl.ds(PARTS[part][0], PARTS[part][1] - PARTS[part][0])
            loads[part] = pltpu.make_async_copy(
                w_vmem.at[:, :, columns], w_scratch.at[:, :, columns], sems.at[part]
            )
            loads[part].start()
        w_vmem = w_scratch
        k_load = pltpu.make_async_copy(k_ref, k_scratch, sems.at[3])
        v_load = pltpu.make_async_copy(v_ref, v_scratch, sems.at[4])
        k_load.start()
        v_load.start()
        k_ref, v_ref = k_scratch, v_scratch
        loads[2].wait()
    else:
        grad_ref, back_ref = rest
    seqs, length = x_ref.shape[0], x_ref.shape[1]
    rows = seqs * length
    gain_attn, gain_moe = gains_of(w_vmem)
    gate = gate_ref[...]
    tiles = length * TILES
    sums = [sum_ref[s] for s in range(seqs)]
    if with_grads:
        lower = order[2, 0] == 0
        sums = [jnp.where(lower, a, second_ref[s]) for s, a in enumerate(sums)]
    high_low = jnp.concatenate([unfold(a[tiles:]) for a in sums], axis=0)
    grad_gate = high_low + pltpu.roll(high_low, 96, 1)
    inner = jnp.sum(gate * grad_gate, axis=-1, keepdims=True)
    grad_logits = jnp.where(lanes_of(gate.shape) < 32, gate * (grad_gate - inner), 0.0)
    grad_logits = grad_logits.astype(bf16)
    w_small = w_vmem[:, :, QKV + D :].reshape(D, LANES)
    summed = jnp.concatenate([plain(a[:tiles]) for a in sums], axis=0)
    grad_normed_moe = summed + nt(grad_logits, w_small)
    resid = resid_ref[...]
    inv_moe = rms(resid)
    if with_grads:
        g = jnp.concatenate([plain(g_ref[s]) for s in range(seqs)], axis=0)
    else:
        g = g_ref[...].reshape(rows, D)
    grad_resid = g.astype(f32) + norm_back(resid, inv_moe, gain_moe, grad_normed_moe)
    grad_branch = grad_resid.astype(bf16)
    if with_grads:
        loads[1].wait()
    w_out = w_vmem[:, :, QKV : QKV + D].reshape(D, D)
    grad_mixed = nt(grad_branch, w_out)
    if with_grads:
        k_load.wait()
        v_load.wait()
    cosine, sine = table_ref[:, :LANES], table_ref[:, LANES:]
    low = lanes_of((length, LANES)) < 64
    for s in range(seqs):
        top = slice(s * length, (s + 1) * length)
        key_parts, value_parts = [], []
        for j in range(KEY_VALUE_HEADS):
            here = slice(j * LANES, (j + 1) * LANES)
            pair = slice((j // 2) * LANES, (j // 2 + 1) * LANES)
            query = halves(q_ref[top, here].astype(f32)).astype(bf16)
            key = doubled(k_ref[top, pair].astype(f32), j % 2 == 1).astype(bf16)
            value = doubled(v_ref[top, pair].astype(f32), j % 2 == 1).astype(bf16)
            grad_heads = halves(grad_mixed[top, here]).astype(bf16)
            probs = probs_ref[s * KEY_VALUE_HEADS + j]
            grad_probs = nt(grad_heads, value)
            grad_value = tn(probs.astype(bf16), grad_heads)
            grad_scores = probs * (grad_probs - jnp.sum(probs * grad_probs, axis=-1, keepdims=True))
            grad_scores = grad_scores.astype(bf16)
            grad_query = join(nn(grad_scores, key)) * scale
            grad_key = tn(grad_scores, query) * scale
            back_ref[top, here] = turn(grad_query, cosine, sine, True).astype(bf16)
            key_parts.append(grad_key + pltpu.roll(grad_key, 64, 1))
            value_parts.append(grad_value + pltpu.roll(grad_value, 64, 1))
        for c in range(4):
            grad_key = jnp.where(low, key_parts[2 * c], key_parts[2 * c + 1])
            grad_value = jnp.where(low, value_parts[2 * c], value_parts[2 * c + 1])
            back_ref[top, D + c * LANES : D + (c + 1) * LANES] = turn(
                grad_key, cosine, sine, True
            ).astype(bf16)
            back_ref[top, D + 512 + c * LANES : D + 512 + (c + 1) * LANES] = grad_value.astype(bf16)
    if with_grads:
        loads[0].wait()
    w_qkv = w_vmem[:, :, :QKV].reshape(D, QKV)
    grad_rows = back_ref[...]
    grad_normed = nt(grad_rows, w_qkv)
    x = x_ref[...].reshape(rows, D).astype(f32)
    inv_attn = rms(x)
    grad_in = grad_resid + norm_back(x, inv_attn, gain_attn, grad_normed)
    if with_grads:
        grad_ref[...] = grad_in.astype(bf16).reshape(seqs, length, D)

        @pl.when(lower)
        def _():
            for s in range(seqs):
                section_ref[s] = plain(first_ref[s])

        @pl.when(jnp.logical_not(lower))
        def _():
            for s in range(seqs):
                top = slice(s * length, (s + 1) * length)
                section_ref[s] = (resid_ref[top] + plain(sum_ref[s, :tiles])).astype(bf16)

    else:
        for s in range(seqs):
            store_tiles(grad_ref, s, grad_in[s * length : (s + 1) * length])

        @pl.when(order[2, 0] == 0)
        def _():
            for s in range(seqs):
                store_tiles(grad_ref, s, g_ref[s])

    if with_grads:
        gains_ref[0:1] = jnp.sum(grad_normed * x * inv_attn, axis=0, keepdims=True)
        gains_ref[1:2] = jnp.sum(grad_normed_moe * resid * inv_moe, axis=0, keepdims=True)
        row = lax.broadcasted_iota(jnp.int32, (LANES, LANES), 0)
        lane = lanes_of((LANES, LANES))
        for k in range(8):
            columns = pl.ds(pl.multiple_of(order[0, k] * LANES, LANES), LANES)
            part_qkv = tn(normed_ref[:, columns], grad_rows)
            part_out = tn(mixed_ref[:, columns], grad_branch)
            places = [(r * TILES + order[0, k]) * TILE for r in range(length // TILE)]
            moe_rows = jnp.concatenate(
                [
                    wide_ref[s, pl.ds(pl.multiple_of(place, TILE), TILE)]
                    for s in range(seqs)
                    for place in places
                ],
                axis=0,
            )
            part_small = tn(moe_rows, grad_logits)
            for i in range(2):
                piece = gains_ref[i : i + 1, columns]
                turned = pltpu.roll(piece, 64, 1)
                part_small = part_small + jnp.where((row == i) & (lane >= 64), turned, 0.0)
                part_small = part_small + jnp.where((row == 64 + i) & (lane >= 64), piece, 0.0)
            n = min(k, 8 - k)
            place = slice(64, 128) if 0 < k < 4 else slice(0, 64)
            for part, columns in (
                (part_qkv, slice(0, QKV)),
                (part_out, slice(QKV, QKV + D)),
                (part_small, slice(QKV + D, WCOLS)),
            ):
                first_core = order[1, 0] == 0
                upper, lower = part[:64], part[64:]
                mine = jnp.where(first_core, upper, lower)
                big_refs[n][place, columns] = mine.astype(bf16)
                other = jnp.where(first_core, lower, upper)
                big_refs[5 + n][place, columns] = other.astype(bf16)


def attn_backward(with_grads, order, sums, g, saved, table, w_all, others=()):
    payload, resid, x, gate, normed, q, k, v, probs, mixed = saved
    late = hbm if with_grads else vmem
    seqs, length = x.shape[0], x.shape[1]
    rows = seqs * length
    shape = jax.ShapeDtypeStruct
    outs = [shape((seqs, length, D) if with_grads else (seqs, length * TILES, LANES), bf16)]
    scratch = [pltpu.VMEM((rows, QKV), bf16)]
    if with_grads:
        outs.append(shape((seqs, length, D), bf16))
        outs += [shape((n, WCOLS), bf16) for n in (64, 128, 128, 128, 64)] * 2
        scratch += [
            pltpu.VMEM((8, D), f32),
            pltpu.VMEM((16, 64, WCOLS), bf16),
            pltpu.VMEM((rows, 512), bf16),
            pltpu.VMEM((rows, 512), bf16),
            pltpu.SemaphoreType.DMA((5,)),
        ]
    return pl.pallas_call(
        functools.partial(attn_backward_kernel, with_grads),
        out_shape=outs,
        in_specs=[smem()] + [vmem()] * 8 + [late()] * 2 + [vmem()] * 3 + [late()] + [vmem()] * len(others),
        out_specs=[vmem()] * len(outs),
        scratch_shapes=scratch,
        compiler_params=pltpu.CompilerParams(vmem_limit_bytes=VMEM_LIMIT),
        cost_estimate=pl.CostEstimate(
            flops=4 * rows * D * 3400, bytes_accessed=20_000_000, transcendentals=0
        ),
        name="attn_backward",
    )(
        order,
        *(sums, g, x, payload, resid, gate, normed, q),
        *((in_hbm(k), in_hbm(v)) if with_grads else (k, v)),
        *(probs, mixed, table, (in_hbm if with_grads else in_vmem)(w_all)),
        *others,
    )


def expert_kernel(mode, parts, which, *refs):
    refs = list(refs)
    take = lambda count: [refs.pop(0) for _ in range(count)]
    x_refs = take(parts)
    g_refs = take(parts) if mode else []
    w_in, w_down = take(2)
    out_refs = take(parts)
    saved_refs = take(5) if mode == 2 else []
    x_rows = take(1)[0]
    g_rows = take(1)[0] if mode else None
    if mode == 2:
        act_rows, gate_rows, up_rows, sems = take(4)
    hot_ref, scale_ref, result_ref = take(3)

    def send(n, j):
        source = (x_rows, g_rows, act_rows, gate_rows, up_rows)[n]
        return pltpu.make_async_copy(source.at[j], saved_refs[n].at[j], sems.at[n, j])

    per = x_rows.shape[0]
    hid = w_down.shape[0] // per
    first = which[0]
    spots = [(i, s) for i in range(parts) for s in range(x_refs[i].shape[0])]
    tiles = x_refs[0].shape[1] // 17 * 16
    length = tiles // TILES
    row8 = lax.broadcasted_iota(jnp.int32, (8, LANES), 0)
    lane8 = lanes_of((8, LANES))
    pick = jnp.where((lane8 == 32 + first + row8) & (row8 < per), 1.0, 0.0).astype(bf16)
    slot = lax.broadcasted_iota(jnp.int32, (SLOTS, length), 0).astype(f32)
    lane = lanes_of((SLOTS, LANES))
    for n, (i, s) in enumerate(spots):
        columns = unfold(x_refs[i][s, tiles:].astype(f32)).astype(bf16)
        places = nt(pick, columns)
        hot = jnp.concatenate(
            [jnp.where(places[j : j + 1] == slot, 1.0, 0.0) for j in range(per)], axis=0
        ).astype(bf16)
        hot_ref[n] = hot
        taken = nn(hot, jnp.concatenate([plain(x_refs[i][s, :tiles]), columns], axis=1))
        here = slice(n * SLOTS, (n + 1) * SLOTS)
        for j in range(per):
            block = taken[j * SLOTS : (j + 1) * SLOTS]
            x_rows[j, here] = block[:, :D].astype(bf16)
            gate = jnp.sum(jnp.where(lane == first + j, block[:, D:], 0.0), axis=-1, keepdims=True)
            scale_ref[j, here] = jnp.broadcast_to(gate, (SLOTS, LANES))
        if mode:
            taken = nn(hot, plain(g_refs[i][s, :tiles]))
            for j in range(per):
                g_rows[j, here] = taken[j * SLOTS : (j + 1) * SLOTS].astype(bf16)
    total = len(spots) * SLOTS
    lane = lanes_of((total, LANES))
    if mode == 2:
        for n in range(2):
            for j in range(per):
                send(n, j).start()
    for j in range(per):
        own_rows = slice(j * hid, (j + 1) * hid)
        rows = x_rows[j]
        gate_val = nt(rows, w_in[own_rows, :D])
        up_val = nt(rows, w_in[own_rows, D:])
        sig = jax.nn.sigmoid(gate_val)
        silu = gate_val * sig
        act = silu * up_val
        gate = scale_ref[j][:, 0:1]

        def forward():
            result_ref[j, :, :D] = (nn(act.astype(bf16), w_down[own_rows]) * gate).astype(bf16)

        def backward():
            inner = nt(g_rows[j], w_down[own_rows])
            grad_gw = jnp.sum(act.astype(bf16).astype(f32) * inner, axis=-1, keepdims=True)
            inner = inner * gate
            grad_gate = (inner * up_val * sig * (1.0 + gate_val * (1.0 - sig))).astype(bf16)
            grad_up = (inner * silu).astype(bf16)
            if mode == 2:
                act_rows[j] = (act * gate).astype(bf16)
                gate_rows[j] = grad_gate
                up_rows[j] = grad_up
                for n in range(2, 5):
                    send(n, j).start()
            grad_in = nn(grad_gate, w_in[own_rows, :D]) + nn(grad_up, w_in[own_rows, D:])
            high = grad_gw.astype(bf16).astype(f32)
            extra = jnp.where(
                lane == first + j, high, jnp.where(lane == 32 + first + j, grad_gw - high, 0.0)
            )
            result_ref[j, :, :D] = grad_in.astype(bf16)
            result_ref[j, :, D:] = extra.astype(bf16)

        if mode == 0:
            forward()
        else:
            backward()
            if mode == 2:

                @pl.when(which[1] != 0)
                def _():
                    forward()

    for n, (i, s) in enumerate(spots):
        here = slice(n * SLOTS, (n + 1) * SLOTS)
        block = jnp.concatenate([result_ref[j, here] for j in range(per)], axis=0)
        block = tn(hot_ref[n], block)
        store_tiles(out_refs[i], s, block[:, :D])
        if mode:
            out_refs[i][s, tiles:] = fold(block[:, D:]).astype(bf16)
    if mode == 2:
        for n in range(5):
            for j in range(per):
                send(n, j).wait()


def expert_call(mode, which, x_parts, g_parts, w_in, w_down, per):
    parts = len(x_parts)
    seqs = sum(x.shape[0] for x in x_parts)
    whole = x_parts[0].shape[1]
    length = whole // 17 * 16 // TILES
    hid = w_down.shape[0] // per
    total = seqs * SLOTS
    out_width = D + LANES if mode else D
    out_rows = whole if mode else length * TILES
    shape = jax.ShapeDtypeStruct
    outs = [shape((x.shape[0], out_rows, LANES), bf16) for x in x_parts]
    out_specs = [vmem()] * parts
    wide, narrow = (per, total, D), (per, total, hid)
    scratch = [pltpu.VMEM(wide, bf16)] * (2 if mode else 1)
    if mode == 2:
        saved = [wide, wide, narrow, narrow, narrow]
        outs += [pltpu.HBM(a, bf16) for a in saved]
        out_specs += [hbm()] * 5
        scratch += [pltpu.VMEM(narrow, bf16)] * 3 + [pltpu.SemaphoreType.DMA((5, per))]
    scratch += [
        pltpu.VMEM((seqs, per * SLOTS, length), bf16),
        pltpu.VMEM((per, total, LANES), f32),
        pltpu.VMEM((per, total, out_width), bf16),
    ]
    units = (3, 5, 5)[mode]
    g_args = list(g_parts) if mode else []

    def body(which, *refs):
        expert_kernel(mode, parts, which, *refs)

    return pl.pallas_call(
        body,
        out_shape=outs,
        in_specs=[smem()] + [vmem()] * (parts + len(g_args) + 2),
        out_specs=out_specs,
        scratch_shapes=scratch,
        compiler_params=pltpu.CompilerParams(vmem_limit_bytes=VMEM_LIMIT),
        cost_estimate=pl.CostEstimate(
            flops=2 * units * per * total * D * hid,
            bytes_accessed=6_000_000 + 4 * seqs * length * D,
            transcendentals=per * total * hid,
        ),
        name="experts_%d" % mode,
    )(which, *x_parts, *g_args, w_in, w_down)


def weight_grad_kernel(groups, tile, j, *refs):
    refs = list(refs)
    sets = [refs[5 * n : 5 * n + 5] for n in range(groups)]
    refs = refs[5 * groups + (2 if j else 0) :]
    in_ref, down_ref, rows = refs[0], refs[1], refs[2:7]
    in_tile, down_tile, load_sems, store_sems = refs[7:]
    hid = rows[2].shape[1]
    loads = []
    for n in (3, 0, 4, 2, 1):
        offset = 0
        for g in range(groups):
            count = sets[g][n].shape[1]
            loads.append(
                pltpu.make_async_copy(
                    sets[g][n].at[j],
                    rows[n].at[pl.ds(offset, count)],
                    load_sems.at[n * groups + g],
                )
            )
            offset += count
    for load in loads:
        load.start()
    tiles = hid // tile
    stores = []

    def store(source, target, sem):
        stores.append(pltpu.make_async_copy(source, target, sem))
        stores[-1].start()

    waited = 0
    for h in range(tiles):
        columns = slice(h * tile, (h + 1) * tile)
        where = pl.ds(j * hid + h * tile, tile)
        for n, upto, target in ((3, 2, 0), (4, 3, 1), (2, 5, 2)):
            for load in loads[waited : upto * groups]:
                load.wait()
            waited = max(waited, upto * groups)
            if target < 2:
                part = pl.ds(target * D, D)
                in_tile[h, :, part] = tn(rows[n][:, columns], rows[0][...])
                store(in_tile.at[h, :, part], in_ref.at[where, part], store_sems.at[h, target])
            else:
                down_tile[h] = tn(rows[n][:, columns], rows[1][...])
                store(down_tile.at[h], down_ref.at[where], store_sems.at[h, 2])
    for copy in stores:
        copy.wait()


def weight_grads(saved, hid, per, j, earlier=()):
    tile = min(hid, 256)
    groups = len(saved)
    args = [in_hbm(a) for group in saved for a in group]
    count = sum(group[0].shape[1] for group in saved)
    wide, narrow = pltpu.VMEM((count, D), bf16), pltpu.VMEM((count, hid), bf16)
    earlier = [in_hbm(a) for a in earlier]
    return pl.pallas_call(
        functools.partial(weight_grad_kernel, groups, tile, j),
        out_shape=[pltpu.HBM((per * hid, 2 * D), f32), pltpu.HBM((per * hid, D), f32)],
        in_specs=[hbm()] * (len(args) + len(earlier)),
        out_specs=[hbm()] * 2,
        scratch_shapes=[
            wide,
            wide,
            narrow,
            narrow,
            narrow,
            pltpu.VMEM((hid // tile, tile, 2 * D), f32),
            pltpu.VMEM((hid // tile, tile, D), f32),
            pltpu.SemaphoreType.DMA((5 * groups,)),
            pltpu.SemaphoreType.DMA((hid // tile, 3)),
        ],
        input_output_aliases={len(args) + n: n for n in range(len(earlier))},
        compiler_params=pltpu.CompilerParams(vmem_limit_bytes=VMEM_LIMIT),
        cost_estimate=pl.CostEstimate(
            flops=6 * count * D * hid, bytes_accessed=14_000_000, transcendentals=0
        ),
        name="weight_grads_%d" % j,
    )(*args, *earlier)


def last_sum_kernel(plans, *refs):
    refs, (qkv_ref, out_ref, router_ref, attn_ref, moe_ref) = refs[:-5], refs[-5:]
    for n, plan in enumerate(plans):
        columns = lambda first, last: total([refs[m][low:high, first:last] for m, low, high in plan])
        rows = plan[0][2] - plan[0][1]
        place = slice(n * rows, (n + 1) * rows)
        qkv_ref[place] = columns(0, QKV)
        out_ref[place] = columns(QKV, QKV + D)
        small = columns(QKV + D, WCOLS)
        router_ref[place] = small[:, :EXPERTS]
        if n == 0:
            attn_ref[...] = small[0:1, 64:]
            moe_ref[...] = small[1:2, 64:]


def last_sum(halves):
    args, plans = [], []
    for terms in halves:
        plans.append([(len(args) + n, low, high) for n, (a, low, high) in enumerate(terms)])
        args += [a for a, low, high in terms]
    rows = sum(terms[0][2] - terms[0][1] for terms in halves)
    shape = lambda *dims: jax.ShapeDtypeStruct(dims, f32)
    return pl.pallas_call(
        functools.partial(last_sum_kernel, plans),
        out_shape=[shape(rows, QKV), shape(rows, D), shape(rows, EXPERTS), shape(1, 64), shape(1, 64)],
        in_specs=[vmem()] * len(args),
        out_specs=[vmem()] * 5,
        compiler_params=pltpu.CompilerParams(vmem_limit_bytes=VMEM_LIMIT),
        cost_estimate=pl.CostEstimate(
            flops=rows * WCOLS * 4, bytes_accessed=rows * WCOLS * 12, transcendentals=0
        ),
        name="last_sum",
    )(*args)


def add_kernel(plans, *refs):
    outs = refs[len(refs) - len(plans) :]
    for out_ref, plan in zip(outs, plans):
        out_ref[...] = total([refs[n][low:high] for n, low, high in plan]).astype(out_ref.dtype)


def add_call(sums, dtype=bf16, stated=16_000_000):
    args, plans, shapes = [], [], []
    for terms in sums:
        plan = []
        for array, low, high in terms:
            found = [n for n, a in enumerate(args) if a is array]
            plan.append((found[0] if found else len(args), low, high))
            if not found:
                args.append(array)
        plans.append(plan)
        array, low, high = terms[0]
        shapes.append(jax.ShapeDtypeStruct((high - low,) + array.shape[1:], dtype))
    return pl.pallas_call(
        functools.partial(add_kernel, plans),
        out_shape=shapes,
        in_specs=[vmem()] * len(args),
        out_specs=[vmem()] * len(shapes),
        compiler_params=pltpu.CompilerParams(vmem_limit_bytes=VMEM_LIMIT),
        cost_estimate=pl.CostEstimate(flops=0, bytes_accessed=stated, transcendentals=0),
        name="add",
    )(*args)


class Ring:
    def __init__(self):
        self.ahead, self.behind, self.core = [], [], [(i, i ^ 1) for i in range(16)]
        for p, chip in enumerate(PATH):
            for b in range(2):
                here = chip * 2 + b
                self.ahead.append((here, PATH[(p + 1) % 8] * 2 + b))
                self.behind.append((here, PATH[(p - 1) % 8] * 2 + b))
        index = lax.axis_index("fsdp")
        place = jnp.asarray(PLACE, jnp.int32)[index // 2]
        chips = jnp.asarray(PATH, jnp.int32)[(place + jnp.arange(8)) % 8]
        self.chips = chips
        self.order = jnp.stack([chips, jnp.broadcast_to(index % 2, (8,))]).astype(jnp.int32)

    def plus(self, a):
        return lax.ppermute(a, "fsdp", self.ahead)

    def minus(self, a):
        return lax.ppermute(a, "fsdp", self.behind)

    def swap(self, a):
        return lax.ppermute(a, "fsdp", self.core)

    def gather(self, own, work):
        half = own.shape[0] // 2
        group, terms, more, done = [own], [], [], None
        for r in range(5):
            if r < 3:
                coming = [self.plus(group[0]), self.minus(group[-1])]
            elif r == 3:
                coming = [self.plus(group[0][:half]), self.minus(group[1][half:])]
            if r:
                terms.append(self.meet(done, len(old)))
                more.append(done[2 * len(old) :])
            old = group
            done = work(r, group + [self.swap(a) for a in group])
            if r < 4:
                coming, done, terms = lax.optimization_barrier((coming, done, terms))
                group = coming
        terms.append(self.meet(done, 2))
        more.append(done[4:])
        return terms, more

    def meet(self, payload, count):
        return [(payload[n], self.swap(payload[count + n])) for n in range(count)]

    def gather_whole(self, own, beside):
        half = own.shape[0] // 2
        behind, ahead = [own], [own]
        for r in range(3):
            new = self.plus(behind[-1]), self.minus(ahead[-1])
            if r == 1:
                new, beside = lax.optimization_barrier((new, beside))
            else:
                new = lax.optimization_barrier(new)
            behind.append(new[0])
            ahead.append(new[1])
        far = [self.plus(behind[3][:half]), self.minus(ahead[3][half:])]
        both = lambda a: [a, self.swap(a)]
        out = [both(a) for a in ahead]
        out += [far + [self.swap(a) for a in far]]
        out += [both(a) for a in behind[:0:-1]]
        return sum(out, []), beside

    def scatter_halves(self, terms, beside=(), work=None):
        half = terms[4][0][0].shape[0]
        came = [[[], []], [[], []]]
        last = ()
        for r in range(4):
            for c in range(2):
                low, high = c * half, (c + 1) * half
                whole = lambda values: [(a, 0, half) for a in values]
                part = lambda values: [(a, low, high) for a in values]
                if r == 1 and c == 0:
                    if work:
                        beside, last = lax.optimization_barrier((beside, last))
                        beside = work(beside)
                    came[c], last, beside = lax.optimization_barrier((came[c], last, beside))
                else:
                    came[c], last = lax.optimization_barrier((came[c], last))
                if r == 0:
                    last = add_call([whole(terms[4][c])])
                else:
                    behind, ahead = terms[4 - r]
                    last = add_call(
                        [part(behind) + whole(came[c][0]), part(ahead) + whole(came[c][1])]
                    )
                if r:
                    came[c] = [[self.minus(last[0])], [self.plus(last[1])]]
                else:
                    came[c] = [[], [self.plus(last[0])]] if c else [[self.minus(last[0])], []]
        return [
            [(a, c * half, (c + 1) * half) for a in terms[0][0]] + [(a, 0, half) for a in sum(came[c], [])]
            for c in range(2)
        ], beside


def total(values):
    return functools.reduce(jnp.add, [a.astype(f32) for a in values])


def on_device(
    tokens,
    cotangent,
    routes,
    picture_start,
    w_qkv,
    w_out,
    w_router,
    gain_attn,
    gain_moe,
    w_gate_up,
    w_down,
):
    section = lax.axis_index("section")
    first_section = section == 0
    index = lax.axis_index("fsdp")
    devices = lax.axis_size("fsdp")
    seqs, length = tokens.shape[0], tokens.shape[1]
    rows = seqs * length
    w_in, w_down = w_gate_up[0], w_down[0]
    per = max(1, EXPERTS // devices)
    hid = w_down.shape[0] // per
    first_expert = index * EXPERTS // devices
    which = jnp.stack([first_expert, section]).astype(jnp.int32)
    ringed = devices == 16

    angles = np.arange(length)[:, None] * 10000.0 ** (-2.0 * (np.arange(LANES) % 32) / HEAD_SIZE)
    table = jnp.asarray(np.concatenate([np.cos(angles), np.sin(angles)], axis=1), f32)
    starts = jnp.pad(picture_start[:, 0], (0, 6))[None]

    named = jnp.any(routes[0][..., None] == jnp.arange(LANES, dtype=jnp.int32), axis=2)
    earlier = jnp.asarray(np.tril(np.ones((length, length)), -1), bf16)
    place = jnp.einsum("ts,mse->mte", earlier, named.astype(bf16), preferred_element_type=f32)
    pos = jnp.where(named, place, 255.0).reshape(rows, LANES)

    if ringed:
        ring = Ring()
        order = jnp.concatenate([ring.order, jnp.broadcast_to(section, (1, 8)).astype(jnp.int32), starts])
        gains = jnp.concatenate([gain_attn, gain_moe])
        side = jnp.concatenate([gains, jnp.zeros((62, 64), bf16)])
        whole = jnp.concatenate([w_qkv[0], w_out[0], w_router[0], jnp.zeros((64, 32), bf16), side], axis=1)
        w_all, (pos, order) = ring.gather_whole(whole, (pos, order))
    else:
        order = jnp.stack([jnp.arange(8), jnp.zeros((8,)), jnp.broadcast_to(section, (8,))])
        order = jnp.concatenate([order.astype(jnp.int32), starts])
        gather = lambda a: lax.all_gather(a[0], "fsdp", axis=0, tiled=True)
        big = jnp.concatenate([gather(w_qkv), gather(w_out)], axis=1).reshape(16, 64, QKV + D)
        gains = jnp.stack([gather(gain_attn), gather(gain_moe)]).reshape(2, 16, 64)
        side = jnp.concatenate(
            [jnp.moveaxis(gains, 0, 1), jnp.zeros((16, 62, 64), bf16)], axis=1
        )
        router = gather(w_router).reshape(16, 64, EXPERTS)
        small = jnp.concatenate([router, jnp.zeros((16, 64, 32), bf16), side], axis=2)
        w_all = jnp.concatenate([big, small], axis=2)
        far = [w_all[i, h : h + 32] for i in (8, 9) for h in (0, 32)]
        w_all = [w_all[i] for i in range(8)] + far + [w_all[i] for i in range(10, 16)]

    def gather_rows(own):
        every = lax.all_gather(own, "fsdp", axis=0, tiled=True)
        return every.reshape((-1, 8) + own.shape[1:])

    def phase(mode, own, g, x_groups=None):
        if ringed:
            seen = []

            def work(r, group):
                seen.append(group)
                x, beside = (group, g and g[r]) if x_groups is None else (x_groups[r], group)
                return expert_call(mode, which, x, beside, w_in, w_down, per)

            terms, saved = ring.gather(own, work)
            grads = ()
            if mode == 2:
                grads = weight_grads(saved, hid, per, 0)
            sums, grads = ring.scatter_halves(terms, grads)
            if mode == 2:
                grads = (saved, grads)
            sums = [total([a[low:high] for a, low, high in half]) for half in sums]
            return jnp.concatenate(sums), seen, grads

        every = gather_rows(own)
        x_all, g_all = (every, g) if x_groups is None else (x_groups, every)

        def step(grads, both):
            out = expert_call(mode, which, [both[0]], [both[1]] if mode else None, w_in, w_down, per)
            if mode == 2:
                grads = jax.tree.map(jnp.add, grads, list(weight_grads([out[1:]], hid, per, 0)))
            return grads, out[0]

        zero = [jnp.zeros((per * hid, 2 * D), f32), jnp.zeros((per * hid, D), f32)]
        grads, payload = lax.scan(
            step, zero if mode == 2 else None, (x_all, g_all if mode else x_all)
        )
        flat = payload.reshape((devices * seqs,) + payload.shape[2:])
        sums = lax.psum_scatter(flat, "fsdp", scatter_dimension=0, tiled=True).astype(f32)
        return sums, x_all, grads

    payload, resid, w_all = attn_forward(False, order, table, pos, tokens, cotangent, w_all)
    mixture, g_second, _ = phase(0, payload, None)
    first_out = (resid + mixture).astype(bf16)
    passed = lax.ppermute(first_out, "section", [(0, 1), (1, 0)])
    payload, resid, *saved = attn_forward(True, order, table, pos, tokens, passed, w_all)
    saved = [payload, resid] + saved
    sums_second, rows_all, _ = phase(1, payload, g_second)
    (grad_second,) = attn_backward(False, order, sums_second, cotangent, saved, table, w_all)

    g_third = lax.ppermute(grad_second, "section", [(0, 1), (1, 0)])
    sums_third, _, grads = phase(2, g_third, None, rows_all)
    section_grad, section_out, *big = attn_backward(
        True, order, sums_third, g_third, saved, table, w_all, (sums_second, first_out)
    )

    if ringed:
        pairs, came = [None] * 5, ()
        for n in (4, 3, 2, 1, 0):
            going, came = lax.optimization_barrier((big[5 + n], came))
            came = ring.swap(going)
            pairs[n] = (big[n], came)
        part = lambda pair, low, high: [a[low:high] for a in pair]
        terms = [[pairs[0]]]
        terms += [[part(pair, 0, 64), part(pair, 64, 128)] for pair in pairs[1:4]]
        terms += [[part(pairs[4], 0, 32), part(pairs[4], 32, 64)]]

        def other_experts(given):
            saved_rows, done = given
            for j in range(1, per):
                done = weight_grads(saved_rows, hid, per, j, done)
            return done

        halves_of, grads = ring.scatter_halves(terms, grads, other_experts)
        g_qkv, g_out, g_router, g_gain_attn, g_gain_moe = last_sum(halves_of)
        g_gain_attn, g_gain_moe = g_gain_attn[0], g_gain_moe[0]
    else:
        chips = [(big[0], big[5])] + [(big[k][64:], big[5 + k][64:]) for k in (1, 2, 3)]
        chips += [(big[4], big[9])] + [(big[k][:64], big[5 + k][:64]) for k in (3, 2, 1)]
        whole = jnp.concatenate([a for chip in chips for a in chip]).astype(f32)
        sum_up = lambda a: lax.psum_scatter(a, "fsdp", scatter_dimension=0, tiled=True)
        small = whole[:, QKV + D :]
        g_qkv, g_out = sum_up(whole[:, :QKV]), sum_up(whole[:, QKV : QKV + D])
        g_router = sum_up(small[:, :EXPERTS])
        gains = small.reshape(16, 64, LANES)
        g_gain_attn = sum_up(gains[:, 0, 64:].reshape(D))
        g_gain_moe = sum_up(gains[:, 1, 64:].reshape(D))
    grad_in, grad_down = grads
    return (
        section_out[None],
        section_grad[None],
        g_qkv[None],
        g_out[None],
        g_router[None],
        g_gain_attn[None],
        g_gain_moe[None],
        grad_in[None],
        grad_down[None],
    )


def solution(mesh):
    return jax.shard_map(
        on_device,
        mesh=mesh,
        in_specs=(
            P(None, "fsdp", None),
            P(None, "fsdp", None),
            P("section", None, "fsdp", None),
            P(None, "fsdp"),
            P("section", "fsdp", None),
            P("section", "fsdp", None),
            P("section", "fsdp", None),
            P("section", "fsdp"),
            P("section", "fsdp"),
            P("section", "fsdp", None),
            P("section", "fsdp", None),
        ),
        out_specs=(
            P("section", None, "fsdp", None),
            P("section", None, "fsdp", None),
            P("section", "fsdp", None),
            P("section", "fsdp", None),
            P("section", "fsdp", None),
            P("section", "fsdp"),
            P("section", "fsdp"),
            P("section", "fsdp", None),
            P("section", "fsdp", None),
        ),
        check_vma=False,
    )
```

```python
import functools

import jax
import jax.numpy as jnp
import numpy as np
from jax import lax
from jax.experimental import pallas as pl
from jax.experimental.pallas import tpu as pltpu
from jax.sharding import PartitionSpec as P

D = 1024
QUERY_HEADS = 16
KEY_VALUE_HEADS = 8
HEAD_SIZE = 64
EXPERTS = 32
TOP = 8
PIC = 64
SLOTS = 32
LANES = 128
QKV = 2048
TILE = 16
TILES = D // LANES
WCOLS = QKV + D + LANES
epsilon = 1e-05
scale = HEAD_SIZE ** (-0.5)
f32 = jnp.float32
bf16 = jnp.bfloat16
VMEM_LIMIT = 20 * 1024 * 1024

PATH = (0, 2, 4, 6, 7, 5, 3, 1)
PLACE = tuple(PATH.index(c) for c in range(8))


def dot(a, b, ca, cb):
    return lax.dot_general(a, b, (((ca,), (cb,)), ((), ())), preferred_element_type=f32)


def nn(a, b):
    return dot(a, b, 1, 0)


def nt(a, b):
    return dot(a, b, 1, 1)


def tn(a, b):
    return dot(a, b, 0, 0)


def lanes_of(shape):
    return lax.broadcasted_iota(jnp.int32, shape, len(shape) - 1)


def rms(values):
    return lax.rsqrt(jnp.mean(values * values, axis=-1, keepdims=True) + epsilon)


def norm_back(values, inv, gain, grad):
    scaled = grad * gain
    inner = jnp.mean(scaled * values, axis=-1, keepdims=True)
    return inv * scaled - values * (inv * inv * inv * inner)


def turn(chunk, cosine, sine, back):
    first = (lanes_of(chunk.shape) & 63) < 32
    ahead = pltpu.roll(chunk, 96, 1)
    behind = pltpu.roll(chunk, 32, 1)
    if back:
        swapped = jnp.where(first, ahead, -behind)
    else:
        swapped = jnp.where(first, -ahead, behind)
    return chunk * cosine + swapped * sine


def halves(chunk):
    low = lanes_of(chunk.shape) < 64
    return jnp.concatenate([jnp.where(low, chunk, 0.0), jnp.where(low, 0.0, chunk)], axis=0)


def join(stacked):
    rows = stacked.shape[0] // 2
    low = lanes_of((rows, LANES)) < 64
    return jnp.where(low, stacked[:rows], stacked[rows:])


def doubled(chunk, odd):
    low = lanes_of(chunk.shape) < 64
    other = pltpu.roll(chunk, 64, 1)
    return jnp.where(low, other, chunk) if odd else jnp.where(low, chunk, other)


PARTS = ((0, QKV), (QKV, QKV + D), (QKV + D, WCOLS))


def wide(length):
    return length * TILES + length // 2


def plain(tiles):
    count = tiles.shape[0] // (TILE * TILES)
    tiles = tiles.reshape(count, TILES, TILE, LANES)
    columns = [tiles[:, c].reshape(count * TILE, LANES) for c in range(TILES)]
    return jnp.concatenate(columns, axis=1)


def store_tiles(ref, s, rows):
    for r in range(rows.shape[0] // TILE):
        for c in range(TILES):
            place = (r * TILES + c) * TILE
            block = rows[r * TILE : (r + 1) * TILE, c * LANES : (c + 1) * LANES]
            ref[s, place : place + TILE] = block.astype(ref.dtype)


def fold(columns):
    half = columns.shape[0] // 2
    low = lanes_of((half, LANES)) < 64
    return jnp.where(low, columns[:half], pltpu.roll(columns[half:], 64, 1))


def unfold(folded):
    return jnp.concatenate([folded, pltpu.roll(folded, 64, 1)], axis=0)


def load_weights(order, blocks, w_vmem, sems, turn_of):
    copies = {}
    for part in turn_of:
        columns = pl.ds(PARTS[part][0], PARTS[part][1] - PARTS[part][0])
        copies[part] = []
        for k in range(8):
            for b in range(2):
                target = w_vmem.at[order[0, k] * 2 + (order[1, 0] ^ b), :, columns]
                if k != 4:
                    pairs = [(blocks[(k if k < 4 else k + 1) * 2 + b], target)]
                else:
                    pairs = [(blocks[8 + 2 * b + h], target.at[pl.ds(32 * h, 32)]) for h in range(2)]
                for block, target in pairs:
                    sem = sems.at[part * 18 + len(copies[part])]
                    copies[part].append(pltpu.make_async_copy(block.at[:, columns], target, sem))
        for copy in copies[part]:
            copy.start()

    def wait(part):
        for copy in copies[part]:
            copy.wait()

    return wait


def gains_of(w_vmem):
    pieces = ([], [])
    for c in range(8):
        even = w_vmem[2 * c, 0:16, QKV + D :].astype(f32)
        odd = w_vmem[2 * c + 1, 0:16, QKV + D :].astype(f32)
        even = pltpu.roll(even, 64, 1)
        both = jnp.where(lanes_of(even.shape) < 64, even, odd)
        for i in range(2):
            pieces[i].append(both[i : i + 1])
    return jnp.concatenate(pieces[0], axis=1), jnp.concatenate(pieces[1], axis=1)


def attn_forward_kernel(save, order, table_hbm, pos_hbm, *refs):
    x_hbms, refs = refs[:2], refs[2:]
    if save:
        w_vmem, refs = refs[0], refs[1:]
    else:
        blocks, w_hbm, refs = refs[:18], refs[20], refs[18:20] + refs[21:]
    out_ref, resid_ref, refs = refs[0], refs[1], refs[2:]
    if save:
        x_ref, gate_ref, normed_ref, q_ref, k_ref, v_ref, probs_ref, mixed_ref = refs[:8]
        passed_ref, refs = refs[8], refs[9:]
    else:
        x_ref, cot_ref, mixed_ref = refs[:3]
        refs = refs[3:]
    if save:
        table_ref, pos_ref, side_sems = refs
    else:
        table_ref, pos_ref, side_sems, sems, w_vmem, resid_vmem = refs
    second = order[2, 0] != 0
    if save:
        loads = [
            pltpu.make_async_copy(x_hbms[0], x_ref, side_sems.at[0]),
            pltpu.make_async_copy(x_hbms[1], passed_ref, side_sems.at[3]),
        ]
        loads[0].start()
        loads[1].start()

    else:
        loads = [
            pltpu.make_async_copy(x_hbms[0], x_ref, side_sems.at[0]),
            pltpu.make_async_copy(x_hbms[1], cot_ref, side_sems.at[3]),
        ]
        loads[0].start()
        loads[1].start()
    load_table = pltpu.make_async_copy(table_hbm, table_ref, side_sems.at[1])
    load_table.start()
    wait = keep = lambda part: None
    if not save:
        kept = []

        def keep(part):
            columns = pl.ds(PARTS[part][0], PARTS[part][1] - PARTS[part][0])
            source, target = w_vmem.at[:, :, columns], w_hbm.at[:, :, columns]
            kept.append(pltpu.make_async_copy(source, target, side_sems.at[4 + part]))
            kept[-1].start()

        wait = load_weights(order, blocks, w_vmem, sems, (2, 0, 1))
    load_pos = pltpu.make_async_copy(pos_hbm, pos_ref, side_sems.at[2])
    load_pos.start()
    seqs, length = x_ref.shape[0], x_ref.shape[1]
    rows = seqs * length
    loads[0].wait()
    if save:
        loads[1].wait()

        @pl.when(second)
        def _():
            for s in range(seqs):
                x_ref[s] = plain(passed_ref[s])

    wait(2)
    keep(2)
    gain_attn, gain_moe = gains_of(w_vmem)
    x = x_ref[...].reshape(rows, D).astype(f32)
    normed = (x * rms(x) * gain_attn).astype(bf16)
    row_pos = lax.broadcasted_iota(jnp.int32, (length, length), 0)
    col_pos = lax.broadcasted_iota(jnp.int32, (length, length), 1)
    load_table.wait()
    cosine, sine = table_ref[:, :LANES], table_ref[:, LANES:]
    wait(0)
    keep(0)
    w_qkv = w_vmem[:, :, :QKV].reshape(D, QKV)
    qkv = nn(normed, w_qkv)
    wait(1)
    keep(1)
    heads = range(KEY_VALUE_HEADS)
    for s in range(seqs):
        top = slice(s * length, (s + 1) * length)
        start = order[3, s]
        both = (
            (row_pos >= start) & (row_pos < start + PIC) & (col_pos >= start) & (col_pos < start + PIC)
        )
        bias = jnp.where((col_pos <= row_pos) | both, 0.0, -1e30)
        bias = jnp.concatenate([bias, bias], axis=0)
        keys, values = [], []
        for c in range(4):
            key = turn(qkv[top, D + c * LANES : D + (c + 1) * LANES], cosine, sine, False)
            value = qkv[top, D + 512 + c * LANES : D + 512 + (c + 1) * LANES]
            if save:
                k_ref[top, c * LANES : (c + 1) * LANES] = key.astype(bf16)
                v_ref[top, c * LANES : (c + 1) * LANES] = value.astype(bf16)
            for odd in (False, True):
                keys.append(doubled(key, odd).astype(bf16))
                values.append(doubled(value, odd).astype(bf16))
        for j in heads:
            query = turn(qkv[top, j * LANES : (j + 1) * LANES], cosine, sine, False)
            if save:
                q_ref[top, j * LANES : (j + 1) * LANES] = query.astype(bf16)
            scores = nt(halves(query).astype(bf16), keys[j]) * scale + bias
            exponent = jnp.exp(scores - jnp.max(scores, axis=-1, keepdims=True))
            probs = exponent * (1.0 / jnp.sum(exponent, axis=-1, keepdims=True))
            if save:
                probs_ref[s * KEY_VALUE_HEADS + j] = probs
            mixed = join(nn(probs.astype(bf16), values[j]))
            mixed_ref[top, j * LANES : (j + 1) * LANES] = mixed.astype(bf16)
    w_out = w_vmem[:, :, QKV : QKV + D].reshape(D, D)
    resid = x + nn(mixed_ref[...], w_out)
    if not save:
        for s in range(seqs):
            store_tiles(resid_vmem, s, resid[s * length : (s + 1) * length])
        kept.append(pltpu.make_async_copy(resid_vmem, resid_ref, side_sems.at[7]))
        kept[-1].start()
    normed_moe = (resid * rms(resid) * gain_moe).astype(bf16)
    w_small = w_vmem[:, :, QKV + D :].reshape(D, LANES)
    logits = nn(normed_moe, w_small)
    load_pos.wait()
    pos = pos_ref[...]
    routed = pos < 64.0
    logits = jnp.where(routed, logits, -1e30)
    exponent = jnp.where(routed, jnp.exp(logits - jnp.max(logits, axis=-1, keepdims=True)), 0.0)
    gate = exponent * (1.0 / jnp.sum(exponent, axis=-1, keepdims=True))
    lane = lanes_of(gate.shape)
    columns = jnp.where(lane < 32, gate, pltpu.roll(pos, 32, 1))
    for s in range(seqs):
        top = slice(s * length, (s + 1) * length)
        store_tiles(out_ref, s, normed_moe[top])
        out_ref[s, length * TILES :] = fold(columns[top]).astype(bf16)
    if save:
        resid_ref[...] = resid
        gate_ref[...] = gate
        normed_ref[...] = normed
    else:
        loads[1].wait()

        @pl.when(second)
        def _():
            for s in range(seqs):
                store_tiles(out_ref, s, cot_ref[s])

        for copy in kept:
            copy.wait()


def vmem():
    return pl.BlockSpec(memory_space=pltpu.VMEM)


def smem():
    return pl.BlockSpec(memory_space=pltpu.SMEM)


def in_vmem(a):
    return pltpu.with_memory_space_constraint(a, pltpu.VMEM)


def hbm():
    return pl.BlockSpec(memory_space=pltpu.HBM)


def in_hbm(a):
    return pltpu.with_memory_space_constraint(a, pltpu.HBM)


def attn_forward(save, order, table, pos, x, other, w_all):
    seqs, length = x.shape[0], x.shape[1]
    rows = seqs * length
    shape = jax.ShapeDtypeStruct
    tiles = (seqs, length * TILES, LANES)
    outs = [shape((seqs, wide(length), LANES), bf16)]
    outs.append(shape((rows, D), f32) if save else pltpu.HBM(tiles, f32))
    probs = (seqs * KEY_VALUE_HEADS, 2 * length, length)
    scratch = []
    if save:
        outs += [
            shape((seqs, length, D), bf16),
            shape((rows, LANES), f32),
            shape((rows, D), bf16),
            shape((rows, D), bf16),
            shape((rows, 512), bf16),
            shape((rows, 512), bf16),
            shape(probs, f32),
            shape((rows, D), bf16),
        ]
        scratch = [pltpu.VMEM(tiles, bf16)]
        w_specs, w_args = [vmem()], [in_vmem(w_all)]
    else:
        outs.append(pltpu.HBM((16, 64, WCOLS), bf16))
        w_specs, w_args = [pl.BlockSpec(memory_space=pl.ANY)] * 18, w_all
        scratch = [pltpu.VMEM((seqs, length, D), bf16)] * 2
        scratch.append(pltpu.VMEM((rows, D), bf16))
    scratch += [
        pltpu.VMEM((length, 2 * LANES), f32),
        pltpu.VMEM((rows, LANES), f32),
        pltpu.SemaphoreType.DMA((8,)),
    ]
    if not save:
        scratch += [
            pltpu.SemaphoreType.DMA((54,)),
            pltpu.VMEM((16, 64, WCOLS), bf16),
            pltpu.VMEM(tiles, f32),
        ]
    return pl.pallas_call(
        functools.partial(attn_forward_kernel, save),
        out_shape=outs,
        in_specs=[smem()] + [hbm()] * 4 + w_specs,
        out_specs=[vmem()] * len(outs) if save else [vmem(), hbm(), hbm()],
        scratch_shapes=scratch,
        compiler_params=pltpu.CompilerParams(vmem_limit_bytes=VMEM_LIMIT),
        cost_estimate=pl.CostEstimate(
            flops=2 * rows * D * 3400, bytes_accessed=12_000_000, transcendentals=rows * 2048
        ),
        name="attn_forward",
    )(order, *map(in_hbm, [table, pos, x, other]), *w_args)


def attn_backward_kernel(
    with_grads,
    order,
    sum_ref,
    g_ref,
    x_ref,
    wide_ref,
    resid_ref,
    gate_ref,
    normed_ref,
    q_ref,
    k_ref,
    v_ref,
    probs_ref,
    mixed_ref,
    table_ref,
    *rest,
):
    w_vmem, rest = rest[0], rest[1:]
    loads = [None] * 3
    if with_grads:
        second_ref, first_ref, grad_ref, section_ref, rest = rest[0], rest[1], rest[2], rest[3], rest[4:]
        big_refs, rest = rest[:10], rest[10:]
        back_ref, gains_ref, w_scratch, sems = rest
        for part in (2, 1, 0):
            columns = pl.ds(PARTS[part][0], PARTS[part][1] - PARTS[part][0])
            loads[part] = pltpu.make_async_copy(
                w_vmem.at[:, :, columns], w_scratch.at[:, :, columns], sems.at[part]
            )
            loads[part].start()
        w_vmem = w_scratch
        loads[2].wait()
    else:
        grad_ref, back_ref = rest
    seqs, length = x_ref.shape[0], x_ref.shape[1]
    rows = seqs * length
    gain_attn, gain_moe = gains_of(w_vmem)
    gate = gate_ref[...]
    tiles = length * TILES
    sums = [sum_ref[s] for s in range(seqs)]
    if with_grads:
        lower = order[2, 0] == 0
        sums = [jnp.where(lower, a, second_ref[s]) for s, a in enumerate(sums)]
    high_low = jnp.concatenate([unfold(a[tiles:]) for a in sums], axis=0)
    grad_gate = high_low + pltpu.roll(high_low, 96, 1)
    inner = jnp.sum(gate * grad_gate, axis=-1, keepdims=True)
    grad_logits = jnp.where(lanes_of(gate.shape) < 32, gate * (grad_gate - inner), 0.0)
    grad_logits = grad_logits.astype(bf16)
    w_small = w_vmem[:, :, QKV + D :].reshape(D, LANES)
    summed = jnp.concatenate([plain(a[:tiles]) for a in sums], axis=0)
    grad_normed_moe = summed + nt(grad_logits, w_small)
    resid = resid_ref[...]
    inv_moe = rms(resid)
    if with_grads:
        g = jnp.concatenate([plain(g_ref[s]) for s in range(seqs)], axis=0)
    else:
        g = g_ref[...].reshape(rows, D)
    grad_resid = g.astype(f32) + norm_back(resid, inv_moe, gain_moe, grad_normed_moe)
    grad_branch = grad_resid.astype(bf16)
    if with_grads:
        loads[1].wait()
    w_out = w_vmem[:, :, QKV : QKV + D].reshape(D, D)
    grad_mixed = nt(grad_branch, w_out)
    cosine, sine = table_ref[:, :LANES], table_ref[:, LANES:]
    low = lanes_of((length, LANES)) < 64
    for s in range(seqs):
        top = slice(s * length, (s + 1) * length)
        key_parts, value_parts = [], []
        for j in range(KEY_VALUE_HEADS):
            here = slice(j * LANES, (j + 1) * LANES)
            pair = slice((j // 2) * LANES, (j // 2 + 1) * LANES)
            query = halves(q_ref[top, here].astype(f32)).astype(bf16)
            key = doubled(k_ref[top, pair].astype(f32), j % 2 == 1).astype(bf16)
            value = doubled(v_ref[top, pair].astype(f32), j % 2 == 1).astype(bf16)
            grad_heads = halves(grad_mixed[top, here]).astype(bf16)
            probs = probs_ref[s * KEY_VALUE_HEADS + j]
            grad_probs = nt(grad_heads, value)
            grad_value = tn(probs.astype(bf16), grad_heads)
            grad_scores = probs * (grad_probs - jnp.sum(probs * grad_probs, axis=-1, keepdims=True))
            grad_scores = grad_scores.astype(bf16)
            grad_query = join(nn(grad_scores, key)) * scale
            grad_key = tn(grad_scores, query) * scale
            back_ref[top, here] = turn(grad_query, cosine, sine, True).astype(bf16)
            key_parts.append(grad_key + pltpu.roll(grad_key, 64, 1))
            value_parts.append(grad_value + pltpu.roll(grad_value, 64, 1))
        for c in range(4):
            grad_key = jnp.where(low, key_parts[2 * c], key_parts[2 * c + 1])
            grad_value = jnp.where(low, value_parts[2 * c], value_parts[2 * c + 1])
            back_ref[top, D + c * LANES : D + (c + 1) * LANES] = turn(
                grad_key, cosine, sine, True
            ).astype(bf16)
            back_ref[top, D + 512 + c * LANES : D + 512 + (c + 1) * LANES] = grad_value.astype(bf16)
    if with_grads:
        loads[0].wait()
    w_qkv = w_vmem[:, :, :QKV].reshape(D, QKV)
    grad_rows = back_ref[...]
    grad_normed = nt(grad_rows, w_qkv)
    x = x_ref[...].reshape(rows, D).astype(f32)
    inv_attn = rms(x)
    grad_in = grad_resid + norm_back(x, inv_attn, gain_attn, grad_normed)
    if with_grads:
        grad_ref[...] = grad_in.astype(bf16).reshape(seqs, length, D)

        @pl.when(lower)
        def _():
            for s in range(seqs):
                section_ref[s] = plain(first_ref[s])

        @pl.when(jnp.logical_not(lower))
        def _():
            for s in range(seqs):
                top = slice(s * length, (s + 1) * length)
                section_ref[s] = (resid_ref[top] + plain(sum_ref[s, :tiles])).astype(bf16)

    else:
        for s in range(seqs):
            store_tiles(grad_ref, s, grad_in[s * length : (s + 1) * length])

        @pl.when(order[2, 0] == 0)
        def _():
            for s in range(seqs):
                store_tiles(grad_ref, s, g_ref[s])

    if with_grads:
        gains_ref[0:1] = jnp.sum(grad_normed * x * inv_attn, axis=0, keepdims=True)
        gains_ref[1:2] = jnp.sum(grad_normed_moe * resid * inv_moe, axis=0, keepdims=True)
        row = lax.broadcasted_iota(jnp.int32, (LANES, LANES), 0)
        lane = lanes_of((LANES, LANES))
        for k in range(8):
            columns = pl.ds(pl.multiple_of(order[0, k] * LANES, LANES), LANES)
            part_qkv = tn(normed_ref[:, columns], grad_rows)
            part_out = tn(mixed_ref[:, columns], grad_branch)
            places = [(r * TILES + order[0, k]) * TILE for r in range(length // TILE)]
            moe_rows = jnp.concatenate(
                [
                    wide_ref[s, pl.ds(pl.multiple_of(place, TILE), TILE)]
                    for s in range(seqs)
                    for place in places
                ],
                axis=0,
            )
            part_small = tn(moe_rows, grad_logits)
            for i in range(2):
                piece = gains_ref[i : i + 1, columns]
                turned = pltpu.roll(piece, 64, 1)
                part_small = part_small + jnp.where((row == i) & (lane >= 64), turned, 0.0)
                part_small = part_small + jnp.where((row == 64 + i) & (lane >= 64), piece, 0.0)
            n = min(k, 8 - k)
            place = slice(64, 128) if 0 < k < 4 else slice(0, 64)
            for part, columns in (
                (part_qkv, slice(0, QKV)),
                (part_out, slice(QKV, QKV + D)),
                (part_small, slice(QKV + D, WCOLS)),
            ):
                first_core = order[1, 0] == 0
                upper, lower = part[:64], part[64:]
                mine = jnp.where(first_core, upper, lower)
                big_refs[n][place, columns] = mine.astype(bf16)
                other = jnp.where(first_core, lower, upper)
                big_refs[5 + n][place, columns] = other.astype(bf16)


def attn_backward(with_grads, order, sums, g, saved, table, w_all, others=()):
    payload, resid, x, gate, normed, q, k, v, probs, mixed = saved
    late = hbm if with_grads else vmem
    seqs, length = x.shape[0], x.shape[1]
    rows = seqs * length
    shape = jax.ShapeDtypeStruct
    outs = [shape((seqs, length, D) if with_grads else (seqs, length * TILES, LANES), bf16)]
    scratch = [pltpu.VMEM((rows, QKV), bf16)]
    if with_grads:
        outs.append(shape((seqs, length, D), bf16))
        outs += [shape((n, WCOLS), bf16) for n in (64, 128, 128, 128, 64)] * 2
        scratch += [
            pltpu.VMEM((8, D), f32),
            pltpu.VMEM((16, 64, WCOLS), bf16),
            pltpu.SemaphoreType.DMA((3,)),
        ]
    return pl.pallas_call(
        functools.partial(attn_backward_kernel, with_grads),
        out_shape=outs,
        in_specs=[smem()] + [vmem()] * 8 + [vmem()] * 5 + [late()] + [vmem()] * len(others),
        out_specs=[vmem()] * len(outs),
        scratch_shapes=scratch,
        compiler_params=pltpu.CompilerParams(vmem_limit_bytes=VMEM_LIMIT),
        cost_estimate=pl.CostEstimate(
            flops=4 * rows * D * 3400, bytes_accessed=20_000_000, transcendentals=0
        ),
        name="attn_backward",
    )(
        order,
        *(sums, g, x, payload, resid, gate, normed, q),
        *(k, v),
        *(probs, mixed, table, (in_hbm if with_grads else in_vmem)(w_all)),
        *others,
    )


def expert_kernel(mode, parts, which, *refs):
    refs = list(refs)
    take = lambda count: [refs.pop(0) for _ in range(count)]
    x_refs = take(parts)
    g_refs = take(parts) if mode else []
    w_in, w_down = take(2)
    out_refs = take(parts)
    saved_refs = take(5) if mode == 2 else []
    x_rows = take(1)[0]
    g_rows = take(1)[0] if mode else None
    if mode == 2:
        act_rows, gate_rows, up_rows, sems = take(4)
    hot_ref, scale_ref, result_ref = take(3)

    def send(n, j):
        source = (x_rows, g_rows, act_rows, gate_rows, up_rows)[n]
        return pltpu.make_async_copy(source.at[j], saved_refs[n].at[j], sems.at[n, j])

    per = x_rows.shape[0]
    hid = w_down.shape[0] // per
    first = which[0]
    spots = [(i, s) for i in range(parts) for s in range(x_refs[i].shape[0])]
    tiles = x_refs[0].shape[1] // 17 * 16
    length = tiles // TILES
    row8 = lax.broadcasted_iota(jnp.int32, (8, LANES), 0)
    lane8 = lanes_of((8, LANES))
    pick = jnp.where((lane8 == 32 + first + row8) & (row8 < per), 1.0, 0.0).astype(bf16)
    slot = lax.broadcasted_iota(jnp.int32, (SLOTS, length), 0).astype(f32)
    lane = lanes_of((SLOTS, LANES))
    for n, (i, s) in enumerate(spots):
        columns = unfold(x_refs[i][s, tiles:].astype(f32)).astype(bf16)
        places = nt(pick, columns)
        hot = jnp.concatenate(
            [jnp.where(places[j : j + 1] == slot, 1.0, 0.0) for j in range(per)], axis=0
        ).astype(bf16)
        hot_ref[n] = hot
        taken = nn(hot, jnp.concatenate([plain(x_refs[i][s, :tiles]), columns], axis=1))
        here = slice(n * SLOTS, (n + 1) * SLOTS)
        for j in range(per):
            block = taken[j * SLOTS : (j + 1) * SLOTS]
            x_rows[j, here] = block[:, :D].astype(bf16)
            gate = jnp.sum(jnp.where(lane == first + j, block[:, D:], 0.0), axis=-1, keepdims=True)
            scale_ref[j, here] = jnp.broadcast_to(gate, (SLOTS, LANES))
        if mode:
            taken = nn(hot, plain(g_refs[i][s, :tiles]))
            for j in range(per):
                g_rows[j, here] = taken[j * SLOTS : (j + 1) * SLOTS].astype(bf16)
    total = len(spots) * SLOTS
    lane = lanes_of((total, LANES))
    if mode == 2:
        for n in range(2):
            for j in range(per):
                send(n, j).start()
    for j in range(per):
        own_rows = slice(j * hid, (j + 1) * hid)
        rows = x_rows[j]
        gate_val = nt(rows, w_in[own_rows, :D])
        up_val = nt(rows, w_in[own_rows, D:])
        sig = jax.nn.sigmoid(gate_val)
        silu = gate_val * sig
        act = silu * up_val
        gate = scale_ref[j][:, 0:1]

        def forward():
            result_ref[j, :, :D] = (nn(act.astype(bf16), w_down[own_rows]) * gate).astype(bf16)

        def backward():
            inner = nt(g_rows[j], w_down[own_rows])
            grad_gw = jnp.sum(act.astype(bf16).astype(f32) * inner, axis=-1, keepdims=True)
            inner = inner * gate
            grad_gate = (inner * up_val * sig * (1.0 + gate_val * (1.0 - sig))).astype(bf16)
            grad_up = (inner * silu).astype(bf16)
            if mode == 2:
                act_rows[j] = (act * gate).astype(bf16)
                gate_rows[j] = grad_gate
                up_rows[j] = grad_up
                for n in range(2, 5):
                    send(n, j).start()
            grad_in = nn(grad_gate, w_in[own_rows, :D]) + nn(grad_up, w_in[own_rows, D:])
            high = grad_gw.astype(bf16).astype(f32)
            extra = jnp.where(
                lane == first + j, high, jnp.where(lane == 32 + first + j, grad_gw - high, 0.0)
            )
            result_ref[j, :, :D] = grad_in.astype(bf16)
            result_ref[j, :, D:] = extra.astype(bf16)

        if mode == 0:
            forward()
        else:
            backward()
            if mode == 2:

                @pl.when(which[1] != 0)
                def _():
                    forward()

    for n, (i, s) in enumerate(spots):
        here = slice(n * SLOTS, (n + 1) * SLOTS)
        block = jnp.concatenate([result_ref[j, here] for j in range(per)], axis=0)
        block = tn(hot_ref[n], block)
        store_tiles(out_refs[i], s, block[:, :D])
        if mode:
            out_refs[i][s, tiles:] = fold(block[:, D:]).astype(bf16)
    if mode == 2:
        for n in range(5):
            for j in range(per):
                send(n, j).wait()


def expert_call(mode, which, x_parts, g_parts, w_in, w_down, per):
    parts = len(x_parts)
    seqs = sum(x.shape[0] for x in x_parts)
    whole = x_parts[0].shape[1]
    length = whole // 17 * 16 // TILES
    hid = w_down.shape[0] // per
    total = seqs * SLOTS
    out_width = D + LANES if mode else D
    out_rows = whole if mode else length * TILES
    shape = jax.ShapeDtypeStruct
    outs = [shape((x.shape[0], out_rows, LANES), bf16) for x in x_parts]
    out_specs = [vmem()] * parts
    wide, narrow = (per, total, D), (per, total, hid)
    scratch = [pltpu.VMEM(wide, bf16)] * (2 if mode else 1)
    if mode == 2:
        saved = [wide, wide, narrow, narrow, narrow]
        outs += [pltpu.HBM(a, bf16) for a in saved]
        out_specs += [hbm()] * 5
        scratch += [pltpu.VMEM(narrow, bf16)] * 3 + [pltpu.SemaphoreType.DMA((5, per))]
    scratch += [
        pltpu.VMEM((seqs, per * SLOTS, length), bf16),
        pltpu.VMEM((per, total, LANES), f32),
        pltpu.VMEM((per, total, out_width), bf16),
    ]
    units = (3, 5, 5)[mode]
    g_args = list(g_parts) if mode else []

    def body(which, *refs):
        expert_kernel(mode, parts, which, *refs)

    return pl.pallas_call(
        body,
        out_shape=outs,
        in_specs=[smem()] + [vmem()] * (parts + len(g_args) + 2),
        out_specs=out_specs,
        scratch_shapes=scratch,
        compiler_params=pltpu.CompilerParams(vmem_limit_bytes=VMEM_LIMIT),
        cost_estimate=pl.CostEstimate(
            flops=2 * units * per * total * D * hid,
            bytes_accessed=6_000_000 + 4 * seqs * length * D,
            transcendentals=per * total * hid,
        ),
        name="experts_%d" % mode,
    )(which, *x_parts, *g_args, w_in, w_down)


def weight_grad_kernel(groups, tile, j, *refs):
    refs = list(refs)
    sets = [refs[5 * n : 5 * n + 5] for n in range(groups)]
    refs = refs[5 * groups + (2 if j else 0) :]
    in_ref, down_ref, rows = refs[0], refs[1], refs[2:7]
    in_tile, down_tile, load_sems, store_sems = refs[7:]
    hid = rows[2].shape[1]
    loads = []
    for n in (3, 0, 4, 2, 1):
        offset = 0
        for g in range(groups):
            count = sets[g][n].shape[1]
            loads.append(
                pltpu.make_async_copy(
                    sets[g][n].at[j],
                    rows[n].at[pl.ds(offset, count)],
                    load_sems.at[n * groups + g],
                )
            )
            offset += count
    for load in loads:
        load.start()
    tiles = hid // tile
    stores = []

    def store(source, target, sem):
        stores.append(pltpu.make_async_copy(source, target, sem))
        stores[-1].start()

    waited = 0
    for h in range(tiles):
        columns = slice(h * tile, (h + 1) * tile)
        where = pl.ds(j * hid + h * tile, tile)
        for n, upto, target in ((3, 2, 0), (4, 3, 1), (2, 5, 2)):
            for load in loads[waited : upto * groups]:
                load.wait()
            waited = max(waited, upto * groups)
            if target < 2:
                part = pl.ds(target * D, D)
                in_tile[h, :, part] = tn(rows[n][:, columns], rows[0][...])
                store(in_tile.at[h, :, part], in_ref.at[where, part], store_sems.at[h, target])
            else:
                down_tile[h] = tn(rows[n][:, columns], rows[1][...])
                store(down_tile.at[h], down_ref.at[where], store_sems.at[h, 2])
    for copy in stores:
        copy.wait()


def weight_grads(saved, hid, per, j, earlier=()):
    tile = min(hid, 256)
    groups = len(saved)
    args = [in_hbm(a) for group in saved for a in group]
    count = sum(group[0].shape[1] for group in saved)
    wide, narrow = pltpu.VMEM((count, D), bf16), pltpu.VMEM((count, hid), bf16)
    earlier = [in_hbm(a) for a in earlier]
    return pl.pallas_call(
        functools.partial(weight_grad_kernel, groups, tile, j),
        out_shape=[pltpu.HBM((per * hid, 2 * D), f32), pltpu.HBM((per * hid, D), f32)],
        in_specs=[hbm()] * (len(args) + len(earlier)),
        out_specs=[hbm()] * 2,
        scratch_shapes=[
            wide,
            wide,
            narrow,
            narrow,
            narrow,
            pltpu.VMEM((hid // tile, tile, 2 * D), f32),
            pltpu.VMEM((hid // tile, tile, D), f32),
            pltpu.SemaphoreType.DMA((5 * groups,)),
            pltpu.SemaphoreType.DMA((hid // tile, 3)),
        ],
        input_output_aliases={len(args) + n: n for n in range(len(earlier))},
        compiler_params=pltpu.CompilerParams(vmem_limit_bytes=VMEM_LIMIT),
        cost_estimate=pl.CostEstimate(
            flops=6 * count * D * hid, bytes_accessed=14_000_000, transcendentals=0
        ),
        name="weight_grads_%d" % j,
    )(*args, *earlier)


def last_sum_kernel(plans, *refs):
    refs, (qkv_ref, out_ref, router_ref, attn_ref, moe_ref) = refs[:-5], refs[-5:]
    for n, plan in enumerate(plans):
        columns = lambda first, last: total([refs[m][low:high, first:last] for m, low, high in plan])
        rows = plan[0][2] - plan[0][1]
        place = slice(n * rows, (n + 1) * rows)
        qkv_ref[place] = columns(0, QKV)
        out_ref[place] = columns(QKV, QKV + D)
        small = columns(QKV + D, WCOLS)
        router_ref[place] = small[:, :EXPERTS]
        if n == 0:
            attn_ref[...] = small[0:1, 64:]
            moe_ref[...] = small[1:2, 64:]


def last_sum(halves):
    args, plans = [], []
    for terms in halves:
        plans.append([(len(args) + n, low, high) for n, (a, low, high) in enumerate(terms)])
        args += [a for a, low, high in terms]
    rows = sum(terms[0][2] - terms[0][1] for terms in halves)
    shape = lambda *dims: jax.ShapeDtypeStruct(dims, f32)
    return pl.pallas_call(
        functools.partial(last_sum_kernel, plans),
        out_shape=[shape(rows, QKV), shape(rows, D), shape(rows, EXPERTS), shape(1, 64), shape(1, 64)],
        in_specs=[vmem()] * len(args),
        out_specs=[vmem()] * 5,
        compiler_params=pltpu.CompilerParams(vmem_limit_bytes=VMEM_LIMIT),
        cost_estimate=pl.CostEstimate(
            flops=rows * WCOLS * 4, bytes_accessed=rows * WCOLS * 12, transcendentals=0
        ),
        name="last_sum",
    )(*args)


def add_kernel(plans, *refs):
    outs = refs[len(refs) - len(plans) :]
    for out_ref, plan in zip(outs, plans):
        out_ref[...] = total([refs[n][low:high] for n, low, high in plan]).astype(out_ref.dtype)


def add_call(sums, dtype=bf16, stated=16_000_000):
    args, plans, shapes = [], [], []
    for terms in sums:
        plan = []
        for array, low, high in terms:
            found = [n for n, a in enumerate(args) if a is array]
            plan.append((found[0] if found else len(args), low, high))
            if not found:
                args.append(array)
        plans.append(plan)
        array, low, high = terms[0]
        shapes.append(jax.ShapeDtypeStruct((high - low,) + array.shape[1:], dtype))
    return pl.pallas_call(
        functools.partial(add_kernel, plans),
        out_shape=shapes,
        in_specs=[vmem()] * len(args),
        out_specs=[vmem()] * len(shapes),
        compiler_params=pltpu.CompilerParams(vmem_limit_bytes=VMEM_LIMIT),
        cost_estimate=pl.CostEstimate(flops=0, bytes_accessed=stated, transcendentals=0),
        name="add",
    )(*args)


class Ring:
    def __init__(self):
        self.ahead, self.behind, self.core = [], [], [(i, i ^ 1) for i in range(16)]
        for p, chip in enumerate(PATH):
            for b in range(2):
                here = chip * 2 + b
                self.ahead.append((here, PATH[(p + 1) % 8] * 2 + b))
                self.behind.append((here, PATH[(p - 1) % 8] * 2 + b))
        index = lax.axis_index("fsdp")
        place = jnp.asarray(PLACE, jnp.int32)[index // 2]
        chips = jnp.asarray(PATH, jnp.int32)[(place + jnp.arange(8)) % 8]
        self.chips = chips
        self.order = jnp.stack([chips, jnp.broadcast_to(index % 2, (8,))]).astype(jnp.int32)

    def plus(self, a):
        return lax.ppermute(a, "fsdp", self.ahead)

    def minus(self, a):
        return lax.ppermute(a, "fsdp", self.behind)

    def swap(self, a):
        return lax.ppermute(a, "fsdp", self.core)

    def gather(self, own, work):
        half = own.shape[0] // 2
        group, terms, more, done = [own], [], [], None
        for r in range(5):
            if r < 3:
                coming = [self.plus(group[0]), self.minus(group[-1])]
            elif r == 3:
                coming = [self.plus(group[0][:half]), self.minus(group[1][half:])]
            if r:
                terms.append(self.meet(done, len(old)))
                more.append(done[2 * len(old) :])
            old = group
            done = work(r, group + [self.swap(a) for a in group])
            if r < 4:
                coming, done, terms = lax.optimization_barrier((coming, done, terms))
                group = coming
        terms.append(self.meet(done, 2))
        more.append(done[4:])
        return terms, more

    def meet(self, payload, count):
        return [(payload[n], self.swap(payload[count + n])) for n in range(count)]

    def gather_whole(self, own, beside):
        half = own.shape[0] // 2
        behind, ahead = [own], [own]
        for r in range(3):
            new = self.plus(behind[-1]), self.minus(ahead[-1])
            if r == 1:
                new, beside = lax.optimization_barrier((new, beside))
            else:
                new = lax.optimization_barrier(new)
            behind.append(new[0])
            ahead.append(new[1])
        far = [self.plus(behind[3][:half]), self.minus(ahead[3][half:])]
        both = lambda a: [a, self.swap(a)]
        out = [both(a) for a in ahead]
        out += [far + [self.swap(a) for a in far]]
        out += [both(a) for a in behind[:0:-1]]
        return sum(out, []), beside

    def scatter_halves(self, terms, beside=(), work=None):
        half = terms[4][0][0].shape[0]
        came = [[[], []], [[], []]]
        last = ()
        for r in range(4):
            for c in range(2):
                low, high = c * half, (c + 1) * half
                whole = lambda values: [(a, 0, half) for a in values]
                part = lambda values: [(a, low, high) for a in values]
                if r == 1 and c == 0:
                    if work:
                        beside, last = lax.optimization_barrier((beside, last))
                        beside = work(beside)
                    came[c], last, beside = lax.optimization_barrier((came[c], last, beside))
                else:
                    came[c], last = lax.optimization_barrier((came[c], last))
                if r == 0:
                    last = add_call([whole(terms[4][c])])
                else:
                    behind, ahead = terms[4 - r]
                    last = add_call(
                        [part(behind) + whole(came[c][0]), part(ahead) + whole(came[c][1])]
                    )
                if r:
                    came[c] = [[self.minus(last[0])], [self.plus(last[1])]]
                else:
                    came[c] = [[], [self.plus(last[0])]] if c else [[self.minus(last[0])], []]
        return [
            [(a, c * half, (c + 1) * half) for a in terms[0][0]] + [(a, 0, half) for a in sum(came[c], [])]
            for c in range(2)
        ], beside


def total(values):
    return functools.reduce(jnp.add, [a.astype(f32) for a in values])


def on_device(
    tokens,
    cotangent,
    routes,
    picture_start,
    w_qkv,
    w_out,
    w_router,
    gain_attn,
    gain_moe,
    w_gate_up,
    w_down,
):
    section = lax.axis_index("section")
    first_section = section == 0
    index = lax.axis_index("fsdp")
    devices = lax.axis_size("fsdp")
    seqs, length = tokens.shape[0], tokens.shape[1]
    rows = seqs * length
    w_in, w_down = w_gate_up[0], w_down[0]
    per = max(1, EXPERTS // devices)
    hid = w_down.shape[0] // per
    first_expert = index * EXPERTS // devices
    which = jnp.stack([first_expert, section]).astype(jnp.int32)
    ringed = devices == 16

    angles = np.arange(length)[:, None] * 10000.0 ** (-2.0 * (np.arange(LANES) % 32) / HEAD_SIZE)
    table = jnp.asarray(np.concatenate([np.cos(angles), np.sin(angles)], axis=1), f32)
    starts = jnp.pad(picture_start[:, 0], (0, 6))[None]

    named = jnp.any(routes[0][..., None] == jnp.arange(LANES, dtype=jnp.int32), axis=2)
    earlier = jnp.asarray(np.tril(np.ones((length, length)), -1), bf16)
    place = jnp.einsum("ts,mse->mte", earlier, named.astype(bf16), preferred_element_type=f32)
    pos = jnp.where(named, place, 255.0).reshape(rows, LANES)

    if ringed:
        ring = Ring()
        order = jnp.concatenate([ring.order, jnp.broadcast_to(section, (1, 8)).astype(jnp.int32), starts])
        gains = jnp.concatenate([gain_attn, gain_moe])
        side = jnp.concatenate([gains, jnp.zeros((62, 64), bf16)])
        whole = jnp.concatenate([w_qkv[0], w_out[0], w_router[0], jnp.zeros((64, 32), bf16), side], axis=1)
        w_all, (pos, order) = ring.gather_whole(whole, (pos, order))
    else:
        order = jnp.stack([jnp.arange(8), jnp.zeros((8,)), jnp.broadcast_to(section, (8,))])
        order = jnp.concatenate([order.astype(jnp.int32), starts])
        gather = lambda a: lax.all_gather(a[0], "fsdp", axis=0, tiled=True)
        big = jnp.concatenate([gather(w_qkv), gather(w_out)], axis=1).reshape(16, 64, QKV + D)
        gains = jnp.stack([gather(gain_attn), gather(gain_moe)]).reshape(2, 16, 64)
        side = jnp.concatenate(
            [jnp.moveaxis(gains, 0, 1), jnp.zeros((16, 62, 64), bf16)], axis=1
        )
        router = gather(w_router).reshape(16, 64, EXPERTS)
        small = jnp.concatenate([router, jnp.zeros((16, 64, 32), bf16), side], axis=2)
        w_all = jnp.concatenate([big, small], axis=2)
        far = [w_all[i, h : h + 32] for i in (8, 9) for h in (0, 32)]
        w_all = [w_all[i] for i in range(8)] + far + [w_all[i] for i in range(10, 16)]

    def gather_rows(own):
        every = lax.all_gather(own, "fsdp", axis=0, tiled=True)
        return every.reshape((-1, 8) + own.shape[1:])

    def phase(mode, own, g, x_groups=None):
        if ringed:
            seen = []

            def work(r, group):
                seen.append(group)
                x, beside = (group, g and g[r]) if x_groups is None else (x_groups[r], group)
                return expert_call(mode, which, x, beside, w_in, w_down, per)

            terms, saved = ring.gather(own, work)
            grads = ()
            if mode == 2:
                grads = weight_grads(saved, hid, per, 0)
            sums, grads = ring.scatter_halves(terms, grads)
            if mode == 2:
                grads = (saved, grads)
            sums = [total([a[low:high] for a, low, high in half]) for half in sums]
            return jnp.concatenate(sums), seen, grads

        every = gather_rows(own)
        x_all, g_all = (every, g) if x_groups is None else (x_groups, every)

        def step(grads, both):
            out = expert_call(mode, which, [both[0]], [both[1]] if mode else None, w_in, w_down, per)
            if mode == 2:
                grads = jax.tree.map(jnp.add, grads, list(weight_grads([out[1:]], hid, per, 0)))
            return grads, out[0]

        zero = [jnp.zeros((per * hid, 2 * D), f32), jnp.zeros((per * hid, D), f32)]
        grads, payload = lax.scan(
            step, zero if mode == 2 else None, (x_all, g_all if mode else x_all)
        )
        flat = payload.reshape((devices * seqs,) + payload.shape[2:])
        sums = lax.psum_scatter(flat, "fsdp", scatter_dimension=0, tiled=True).astype(f32)
        return sums, x_all, grads

    payload, resid, w_all = attn_forward(False, order, table, pos, tokens, cotangent, w_all)
    mixture, g_second, _ = phase(0, payload, None)
    first_out = (resid + mixture).astype(bf16)
    passed = lax.ppermute(first_out, "section", [(0, 1), (1, 0)])
    payload, resid, *saved = attn_forward(True, order, table, pos, tokens, passed, w_all)
    saved = [payload, resid] + saved
    sums_second, rows_all, _ = phase(1, payload, g_second)
    (grad_second,) = attn_backward(False, order, sums_second, cotangent, saved, table, w_all)

    g_third = lax.ppermute(grad_second, "section", [(0, 1), (1, 0)])
    sums_third, _, grads = phase(2, g_third, None, rows_all)
    section_grad, section_out, *big = attn_backward(
        True, order, sums_third, g_third, saved, table, w_all, (sums_second, first_out)
    )

    if ringed:
        pairs, came = [None] * 5, ()
        for n in (4, 3, 2, 1, 0):
            going, came = lax.optimization_barrier((big[5 + n], came))
            came = ring.swap(going)
            pairs[n] = (big[n], came)
        part = lambda pair, low, high: [a[low:high] for a in pair]
        terms = [[pairs[0]]]
        terms += [[part(pair, 0, 64), part(pair, 64, 128)] for pair in pairs[1:4]]
        terms += [[part(pairs[4], 0, 32), part(pairs[4], 32, 64)]]

        def other_experts(given):
            saved_rows, done = given
            for j in range(1, per):
                done = weight_grads(saved_rows, hid, per, j, done)
            return done

        halves_of, grads = ring.scatter_halves(terms, grads, other_experts)
        g_qkv, g_out, g_router, g_gain_attn, g_gain_moe = last_sum(halves_of)
        g_gain_attn, g_gain_moe = g_gain_attn[0], g_gain_moe[0]
    else:
        chips = [(big[0], big[5])] + [(big[k][64:], big[5 + k][64:]) for k in (1, 2, 3)]
        chips += [(big[4], big[9])] + [(big[k][:64], big[5 + k][:64]) for k in (3, 2, 1)]
        whole = jnp.concatenate([a for chip in chips for a in chip]).astype(f32)
        sum_up = lambda a: lax.psum_scatter(a, "fsdp", scatter_dimension=0, tiled=True)
        small = whole[:, QKV + D :]
        g_qkv, g_out = sum_up(whole[:, :QKV]), sum_up(whole[:, QKV : QKV + D])
        g_router = sum_up(small[:, :EXPERTS])
        gains = small.reshape(16, 64, LANES)
        g_gain_attn = sum_up(gains[:, 0, 64:].reshape(D))
        g_gain_moe = sum_up(gains[:, 1, 64:].reshape(D))
    grad_in, grad_down = grads
    return (
        section_out[None],
        section_grad[None],
        g_qkv[None],
        g_out[None],
        g_router[None],
        g_gain_attn[None],
        g_gain_moe[None],
        grad_in[None],
        grad_down[None],
    )


def solution(mesh):
    return jax.shard_map(
        on_device,
        mesh=mesh,
        in_specs=(
            P(None, "fsdp", None),
            P(None, "fsdp", None),
            P("section", None, "fsdp", None),
            P(None, "fsdp"),
            P("section", "fsdp", None),
            P("section", "fsdp", None),
            P("section", "fsdp", None),
            P("section", "fsdp"),
            P("section", "fsdp"),
            P("section", "fsdp", None),
            P("section", "fsdp", None),
        ),
        out_specs=(
            P("section", None, "fsdp", None),
            P("section", None, "fsdp", None),
            P("section", "fsdp", None),
            P("section", "fsdp", None),
            P("section", "fsdp", None),
            P("section", "fsdp"),
            P("section", "fsdp"),
            P("section", "fsdp", None),
            P("section", "fsdp", None),
        ),
        check_vma=False,
    )
```
